128 devices in a mesh: dp: 2 (over y_lo), seq: 8 (over x, core), tensor: 8 (over z, y_hi).
Axes of the slice: x: 4, y: 4 (y_hi: 2, y_lo: 2; y = y_hi * 2 + y_lo), z: 4, core: 2. Of those that a mesh axis runs over, the one named last changes fastest.
Arguments:
- tokens: bfloat16 [6, 2048, 2048], P('dp', 'seq'), may hold values from -6 to 6
- cotangent: bfloat16 [6, 2048, 2048], P('dp', 'seq'), may hold values from -6 to 6
- query_weight: float32 [2048, 2048], P(('dp', 'seq'), 'tensor'), may hold values from -0.125 to 0.125
- query_first: float32 [2048, 2048], P(('dp', 'seq'), 'tensor'), may hold values from -128 to 128
- query_second: float32 [2048, 2048], P(('dp', 'seq'), 'tensor'), may hold values from 2580.48 to 10321.92
- key_value_weight: float32 [2048, 8, 128], P(('dp', 'seq'), 'tensor'), may hold values from -0.125 to 0.125
- key_value_first_moment: float32 [2048, 8, 128], P(('dp', 'seq'), 'tensor'), may hold values from -224 to 224
- key_value_second_moment: float32 [2048, 8, 128], P(('dp', 'seq'), 'tensor'), may hold values from 5775.36 to 23347.2
- output_weight: float32 [2048, 2048], P('tensor', ('dp', 'seq')), may hold values from -3 to 3
- output_first: float32 [2048, 2048], P('tensor', ('dp', 'seq')), may hold values from -7 to 7
- output_second: float32 [2048, 2048], P('tensor', ('dp', 'seq')), may hold values from 5.04 to 20.4
- gate_up_weight: float32 [2, 2048, 8192], P(None, ('dp', 'seq'), 'tensor'), may hold values from -0.125 to 0.125
- gate_up_first: float32 [2, 2048, 8192], P(None, ('dp', 'seq'), 'tensor'), may hold values from -20 to 20
- gate_up_second: float32 [2, 2048, 8192], P(None, ('dp', 'seq'), 'tensor'), may hold values from 49.152 to 193.536
- down_weight: float32 [8192, 2048], P('tensor', ('dp', 'seq')), may hold values from -0.0625 to 0.0625
- down_first: float32 [8192, 2048], P('tensor', ('dp', 'seq')), may hold values from -40 to 40
- down_second: float32 [8192, 2048], P('tensor', ('dp', 'seq')), may hold values from 221.184 to 909.312
- norm_gains: float32 [2, 2048], P(None, ('dp', 'seq')), may hold values from 0.5 to 1.5
- gains_first: float32 [2, 2048], P(None, ('dp', 'seq')), may hold values from -120.558878 to 120.558878, as said below
- gains_second: float32 [2, 2048], P(None, ('dp', 'seq')), may hold values from 452.1984 to 15605.76, as said below
Outputs:
- block_out: bfloat16 [6, 2048, 2048], P('dp', ('seq', 'tensor'))
- input_grad: bfloat16 [6, 2048, 2048], P('dp', ('seq', 'tensor'))
- query_new: float32 [2048, 2048], P(('dp', 'seq'), 'tensor')
- query_first_new: float32 [2048, 2048], P(('dp', 'seq'), 'tensor')
- query_second_new: float32 [2048, 2048], P(('dp', 'seq'), 'tensor')
- pair_new: float32 [2048, 8, 128], P(('dp', 'seq'), 'tensor')
- pair_first_new: float32 [2048, 8, 128], P(('dp', 'seq'), 'tensor')
- pair_second_new: float32 [2048, 8, 128], P(('dp', 'seq'), 'tensor')
- output_new: float32 [2048, 2048], P('tensor', ('dp', 'seq'))
- output_first_new: float32 [2048, 2048], P('tensor', ('dp', 'seq'))
- output_second_new: float32 [2048, 2048], P('tensor', ('dp', 'seq'))
- gate_up_new: float32 [2, 2048, 8192], P(None, ('dp', 'seq'), 'tensor')
- gate_up_first_new: float32 [2, 2048, 8192], P(None, ('dp', 'seq'), 'tensor')
- gate_up_second_new: float32 [2, 2048, 8192], P(None, ('dp', 'seq'), 'tensor')
- down_new: float32 [8192, 2048], P('tensor', ('dp', 'seq'))
- down_first_new: float32 [8192, 2048], P('tensor', ('dp', 'seq'))
- down_second_new: float32 [8192, 2048], P('tensor', ('dp', 'seq'))
- gains_new: float32 [2, 2048], P(None, ('dp', 'seq'))
- gains_first_new: float32 [2, 2048], P(None, ('dp', 'seq'))
- gains_second_new: float32 [2, 2048], P(None, ('dp', 'seq'))
The draws below stay inside these ranges and needn't reach their ends.
Inputs may be any that keep to these rules, and one draw needn't show every extreme that they name: `gains_first`: first moments of the gains, both signs. `gains_second`: second moments of the gains, positive.
All inputs are finite; a program needn't handle non-finite values.
Results may differ from the reference program's by a relative error of at most 0.03.
Values may be sent and summed in bfloat16 or wider, within the bound.
A program may use at most 192 MiB of HBM per device.

```python
import math
import jax
import jax.numpy as jnp
from jax import lax

MODEL_WIDTH = 2048
QUERY_HEADS = 32
KEY_VALUE_HEADS = 8
HEAD_SIZE = 64
FF = 8192
SEQUENCE_LENGTH = 2048
STEP = 10
SEQUENCES = 6
TOKEN_COUNT = 12288


def gain_square_scales():
    return jnp.array([6.0 * (TOKEN_COUNT * MODEL_WIDTH // (QUERY_HEADS * HEAD_SIZE)), 0.7 * TOKEN_COUNT], dtype=jnp.float32)[:, None]


def draw_gains_first(key, part):
    key = jax.random.fold_in(key, 5)
    normal_draw = jnp.clip(jax.random.normal(key, (2, MODEL_WIDTH), jnp.float32), -4.0, 4.0)
    return 0.111 * jnp.sqrt(gain_square_scales()) * normal_draw


def draw_gains_second(key, part):
    key = jax.random.fold_in(key, 9)
    log_share = jax.random.uniform(key, (2, MODEL_WIDTH), jnp.float32)
    return 0.0526 * gain_square_scales() * jnp.exp(log_share * math.log(4.0))


def block_levels(key, dims, cuts, smallest, high):
    loudness, own = 1.0, jax.random.fold_in(key, 6)
    for axis_at, shards_of in cuts:
        steps = jnp.exp(jax.random.uniform(jax.random.fold_in(own, axis_at), (shards_of,), jnp.float32, smallest / len(cuts), high / len(cuts)))
        loudness = loudness * jnp.repeat(steps, dims[axis_at] // shards_of).reshape([-1 if axis == axis_at else 1 for axis in range(len(dims))])
    return loudness


def bell_draw(stream_key, shape, spread, reach, pieces=(), kind=jnp.bfloat16):
    entries = jax.random.normal(stream_key, shape, jnp.float32) * spread
    if len(pieces) > 0:
        entries = block_levels(stream_key, shape, pieces, -0.22, 0.18) * entries
    return jnp.clip(entries, min=-reach, max=reach).astype(kind)


def setup_inputs(seed: int = 0) -> dict:
    arg_keys = jax.random.split(jax.random.key(seed), 21)
    tokens = bell_draw(arg_keys[0], (SEQUENCES, SEQUENCE_LENGTH, MODEL_WIDTH), 1.0, 6.0, ((0, 2), (1, 8)))
    cotangent = bell_draw(arg_keys[1], (SEQUENCES, SEQUENCE_LENGTH, MODEL_WIDTH), 1.0, 6.0, ((0, 2), (1, 8)))
    query_weight = bell_draw(arg_keys[2], (MODEL_WIDTH, QUERY_HEADS * HEAD_SIZE), MODEL_WIDTH ** -0.5, 0.125, ((0, 16), (1, 8)), jnp.float32)
    query_first = bell_draw(arg_keys[3], (MODEL_WIDTH, QUERY_HEADS * HEAD_SIZE), (0.22 * (TOKEN_COUNT * MODEL_WIDTH // (QUERY_HEADS * HEAD_SIZE)) ** 0.5), 128.0, ((0, 16), (1, 8)), jnp.float32)
    query_second = jnp.clip(jnp.exp(math.log(10321.92) - 1.3862944 * jax.random.uniform(arg_keys[4], (MODEL_WIDTH, QUERY_HEADS * HEAD_SIZE), jnp.float32) ** block_levels(arg_keys[4], (MODEL_WIDTH, QUERY_HEADS * HEAD_SIZE), ((0, 16), (1, 8)), -0.2, 0.2)), 2580.48, 10321.92)
    key_value_weight = bell_draw(arg_keys[5], (MODEL_WIDTH, KEY_VALUE_HEADS, 2 * HEAD_SIZE), MODEL_WIDTH ** -0.5, 0.125, ((0, 16), (1, 8)), jnp.float32)
    key_value_first_moment = bell_draw(arg_keys[6], (MODEL_WIDTH, KEY_VALUE_HEADS, 2 * HEAD_SIZE), (0.33 * (TOKEN_COUNT * MODEL_WIDTH // (QUERY_HEADS * HEAD_SIZE)) ** 0.5), 224.0, ((0, 16), (1, 8)), jnp.float32)
    key_value_second_moment = jnp.clip(jnp.exp(math.log(23347.2) - 1.3968765 * jax.random.uniform(arg_keys[7], (MODEL_WIDTH, KEY_VALUE_HEADS, 2 * HEAD_SIZE), jnp.float32) ** block_levels(arg_keys[7], (MODEL_WIDTH, KEY_VALUE_HEADS, 2 * HEAD_SIZE), ((0, 16), (1, 8)), -0.2, 0.2)), 5775.36, 23347.2)
    output_weight = bell_draw(arg_keys[8], (QUERY_HEADS * HEAD_SIZE, MODEL_WIDTH), (max(QUERY_HEADS * HEAD_SIZE * 4 // SEQUENCE_LENGTH, 1)) ** -0.5, 3.0, ((0, 8), (1, 16)), jnp.float32)
    output_first = bell_draw(arg_keys[9], (QUERY_HEADS * HEAD_SIZE, MODEL_WIDTH), (0.44 * (TOKEN_COUNT // SEQUENCE_LENGTH) ** 0.5), 7.0, ((0, 8), (1, 16)), jnp.float32)
    output_second = jnp.clip(jnp.exp(math.log(20.4) - 1.39812881 * jax.random.uniform(arg_keys[10], (QUERY_HEADS * HEAD_SIZE, MODEL_WIDTH), jnp.float32) ** block_levels(arg_keys[10], (QUERY_HEADS * HEAD_SIZE, MODEL_WIDTH), ((0, 8), (1, 16)), -0.2, 0.2)), 5.04, 20.4)
    gate_up_weight = bell_draw(arg_keys[11], (2, MODEL_WIDTH, FF), MODEL_WIDTH ** -0.5, 0.125, ((1, 16), (2, 8)), jnp.float32)
    gate_up_first = bell_draw(arg_keys[12], (2, MODEL_WIDTH, FF), (0.061 * (TOKEN_COUNT * MODEL_WIDTH // FF) ** 0.5), 20.0, ((1, 16), (2, 8)), jnp.float32)
    gate_up_second = jnp.clip(jnp.exp(math.log(193.536) - 1.370546 * jax.random.uniform(arg_keys[13], (2, MODEL_WIDTH, FF), jnp.float32) ** block_levels(arg_keys[13], (2, MODEL_WIDTH, FF), ((1, 16), (2, 8)), -0.2, 0.2)), 49.152, 193.536)
    down_weight = bell_draw(arg_keys[14], (FF, MODEL_WIDTH), FF ** -0.5, 0.0625, ((0, 8), (1, 16)), jnp.float32)
    down_first = bell_draw(arg_keys[15], (FF, MODEL_WIDTH), (0.066 * TOKEN_COUNT ** 0.5), 40.0, ((0, 8), (1, 16)), jnp.float32)
    down_second = jnp.clip(jnp.exp(math.log(909.312) - 1.4136933 * jax.random.uniform(arg_keys[16], (FF, MODEL_WIDTH), jnp.float32) ** block_levels(arg_keys[16], (FF, MODEL_WIDTH), ((0, 8), (1, 16)), -0.2, 0.2)), 221.184, 909.312)
    norm_gains = jnp.clip(1.0 + 0.1 * jax.random.normal(arg_keys[17], (2, MODEL_WIDTH), jnp.float32), 0.5, 1.5)
    gains_first = draw_gains_first(jax.random.fold_in(arg_keys[20], 71), 0)
    gains_second = draw_gains_second(jax.random.fold_in(arg_keys[20], 71), 0)
    return {"tokens": tokens, "cotangent": cotangent, "query_weight": query_weight, "query_first": query_first, "query_second": query_second, "key_value_weight": key_value_weight, "key_value_first_moment": key_value_first_moment, "key_value_second_moment": key_value_second_moment, "output_weight": output_weight, "output_first": output_first, "output_second": output_second, "gate_up_weight": gate_up_weight, "gate_up_first": gate_up_first, "gate_up_second": gate_up_second, "down_weight": down_weight, "down_first": down_first, "down_second": down_second, "norm_gains": norm_gains, "gains_first": gains_first, "gains_second": gains_second}


@jax.custom_vjp
def low(v):
    return lax.optimization_barrier(v.astype(jnp.bfloat16)).astype(jnp.float32)

@jax.custom_vjp
def reduced_backward(v):
    return v

def low_keep(v):
    return (low(v), None)

def low_pass(kept, grad):
    return (grad,)

def back_keep(v):
    return (v, None)

def back_low(kept, grad):
    return (low(grad),)
low.defvjp(low_keep, low_pass)
reduced_backward.defvjp(back_keep, back_low)
norm_eps = 1e-05
rope_base = 500000.0
beta_first = 0.9
beta_second = 0.95
adam_eps = 1e-08
weight_decay = 0.1
rate_wide = 0.07
rate_down = 0.035
rate_output = 1.0
rate_gains = 0.7

def multiply_product(form, left, right):
    return jnp.einsum(form, left, right, precision=lax.Precision.HIGHEST)

def inverse_rms(values):
    return lax.rsqrt(lax.optimization_barrier(jnp.mean(values * values, axis=-1, keepdims=True)) + norm_eps)

def rotary(positions):
    half_size = HEAD_SIZE // 2
    freqs = rope_base ** (-2.0 * jnp.arange(half_size, dtype=jnp.float32) / HEAD_SIZE)
    angles = positions.astype(jnp.float32)[:, None] * freqs[None, :]
    return (jnp.cos(angles)[:, None, :], jnp.sin(angles)[:, None, :])

def rotate(values, cos_table, sin_table):
    half_size = values.shape[-1] // 2
    lower_half = values[..., :half_size]
    upper_half = values[..., half_size:]
    return jnp.concatenate([lower_half * cos_table - upper_half * sin_table, upper_half * cos_table + lower_half * sin_table], axis=-1)

def attend(query_block_rows, key_seq, value_seq, row_start):
    block_row_count = query_block_rows.shape[0]
    query_group = QUERY_HEADS // KEY_VALUE_HEADS
    grouped_queries = query_block_rows.reshape(block_row_count, KEY_VALUE_HEADS, query_group, HEAD_SIZE)
    scores = reduced_backward(multiply_product('qhgd,khd->hgqk', grouped_queries, key_seq) * HEAD_SIZE ** (-0.5))
    query_pos = row_start + jnp.arange(block_row_count, dtype=jnp.int32)
    key_pos = jnp.arange(SEQUENCE_LENGTH, dtype=jnp.int32)
    causal = key_pos[None, :] <= query_pos[:, None]
    scores = jnp.where(causal, scores, -1e+30)
    row_max = lax.optimization_barrier(jnp.max(scores, axis=-1, keepdims=True))
    weights = jnp.exp(scores - row_max)
    probs = weights / lax.optimization_barrier(jnp.sum(weights, axis=-1, keepdims=True))
    mixed = multiply_product('hgqk,khd->qhgd', low(probs), value_seq)
    return mixed.reshape(block_row_count, QUERY_HEADS * HEAD_SIZE)

def attention(query_rows, key, value):
    block_row_count = min(512, SEQUENCE_LENGTH)
    block_count = SEQUENCE_LENGTH // block_row_count
    sequence_total = query_rows.shape[0]

    def one_block(block_index):
        seq_index = block_index // block_count
        row_start = block_index % block_count * block_row_count
        query_seq = lax.dynamic_index_in_dim(query_rows, seq_index, 0, keepdims=False)
        query_block_rows = lax.dynamic_slice_in_dim(query_seq, row_start, block_row_count, 0)
        key_seq = lax.dynamic_index_in_dim(key, seq_index, 0, keepdims=False)
        value_seq = lax.dynamic_index_in_dim(value, seq_index, 0, keepdims=False)
        return attend(query_block_rows, key_seq, value_seq, row_start)
    blocks = lax.map(jax.checkpoint(one_block), jnp.arange(sequence_total * block_count, dtype=jnp.int32))
    return blocks.reshape(sequence_total, SEQUENCE_LENGTH, QUERY_HEADS * HEAD_SIZE)

def layer(tokens, query_projection_weight, key_value_projection_weight, output_projection_weight, gate_up_projection_weight, down_projection_weight, gains):
    sequence_total = tokens.shape[0]
    cos_table, sin_table = rotary(jnp.arange(SEQUENCE_LENGTH, dtype=jnp.int32))
    normed_one = tokens * inverse_rms(tokens)
    hidden_after_attention = low(normed_one * gains[0])
    query_rows = reduced_backward(multiply_product('wph,hv->wpv', hidden_after_attention, query_projection_weight)).reshape(sequence_total, SEQUENCE_LENGTH, QUERY_HEADS, HEAD_SIZE)
    query_rows = low(rotate(query_rows, cos_table, sin_table))
    key_value_rows = reduced_backward(multiply_product('cyp,prw->cyrw', hidden_after_attention, key_value_projection_weight))
    key = low(rotate(key_value_rows[..., :HEAD_SIZE], cos_table, sin_table))
    value = low(key_value_rows[..., HEAD_SIZE:])
    attention_output = reduced_backward(low(attention(query_rows, key, value)))
    middle_activation = tokens + reduced_backward(multiply_product('yvh,hc->yvc', attention_output, output_projection_weight))
    normed_two = middle_activation * inverse_rms(middle_activation)
    hidden_after_feedforward = low(normed_two * gains[1])
    gate_up_rows = reduced_backward(multiply_product('gyx,wxk->wgyk', hidden_after_feedforward, gate_up_projection_weight))
    hidden_state = low(jax.nn.silu(gate_up_rows[0]) * gate_up_rows[1])
    return middle_activation + reduced_backward(multiply_product('cij,jg->cig', hidden_state, down_projection_weight))

def adam(master, grad, moment_one, moment_two, rate, decay):
    new_one = beta_first * moment_one + (1.0 - beta_first) * grad
    new_two = beta_second * moment_two + (1.0 - beta_second) * grad * grad
    ahead = new_one / (1.0 - beta_first ** STEP) / (jnp.sqrt(new_two / (1.0 - beta_second ** STEP)) + adam_eps)
    return (master - rate * (ahead + decay * master), new_one, new_two)

def rounded(master):
    return master.astype(jnp.bfloat16).astype(jnp.float32)

def reference(tokens, cotangent, query_weight, query_first, query_second, key_value_weight, key_value_first_moment, key_value_second_moment, output_weight, output_first, output_second, gate_up_weight, gate_up_first, gate_up_second, down_weight, down_first, down_second, norm_gains, gains_first, gains_second):
    block_out, pullback = jax.vjp(layer, tokens.astype(jnp.float32), rounded(query_weight), rounded(key_value_weight), rounded(output_weight), rounded(gate_up_weight), rounded(down_weight), rounded(norm_gains))
    grads = pullback(cotangent.astype(jnp.float32))
    query_new, query_first_new, query_second_new = adam(query_weight, grads[1], query_first, query_second, rate_wide, weight_decay)
    pair_new, pair_first_new, pair_second_new = adam(key_value_weight, grads[2], key_value_first_moment, key_value_second_moment, rate_wide, weight_decay)
    output_new, output_first_new, output_second_new = adam(output_weight, grads[3], output_first, output_second, rate_output, weight_decay)
    gate_up_new, gate_up_first_new, gate_up_second_new = adam(gate_up_weight, grads[4], gate_up_first, gate_up_second, rate_wide, weight_decay)
    down_new, down_first_new, down_second_new = adam(down_weight, grads[5], down_first, down_second, rate_down, weight_decay)
    gains_new, gains_first_new, gains_second_new = adam(norm_gains, grads[6], gains_first, gains_second, rate_gains, 0.0)
    return (block_out.astype(jnp.bfloat16), grads[0].astype(jnp.bfloat16), query_new, query_first_new, query_second_new, pair_new, pair_first_new, pair_second_new, output_new, output_first_new, output_second_new, gate_up_new, gate_up_first_new, gate_up_second_new, down_new, down_first_new, down_second_new, gains_new, gains_first_new, gains_second_new)
```

```python
import jax
import jax.numpy as jnp
from jax import lax
from jax.experimental import pallas as pl
from jax.experimental.pallas import tpu as pltpu
from jax.sharding import PartitionSpec as P

QUERY_HEADS = 32
KEY_VALUE_HEADS = 8
HEAD_SIZE = 64
STEP = 10
GROUP = QUERY_HEADS // KEY_VALUE_HEADS


norm_eps = 1e-05
rope_base = 500000.0
beta_first = 0.9
beta_second = 0.95
adam_eps = 1e-08
weight_decay = 0.1
rate_wide = 0.07
rate_down = 0.035
rate_output = 1.0
rate_gains = 0.7

bf16 = jnp.bfloat16
f32 = jnp.float32
MESH = pl.DeviceIdType.MESH
VMEM = pl.BlockSpec(memory_space=pltpu.VMEM)
ANY = pl.BlockSpec(memory_space=pl.ANY)
MIB = 1024 * 1024


def inverse_rms(values):
    return lax.rsqrt(jnp.mean(values * values, axis=-1, keepdims=True) + norm_eps)


def rotary(positions):
    half_size = HEAD_SIZE // 2
    freqs = rope_base ** (-2.0 * jnp.arange(half_size, dtype=jnp.float32) / HEAD_SIZE)
    angles = positions.astype(jnp.float32)[:, None] * freqs[None, :]
    return (jnp.cos(angles)[:, None, :], jnp.sin(angles)[:, None, :])


def rotate(values, cos_table, sin_table):
    half_size = values.shape[-1] // 2
    lower_half = values[..., :half_size]
    upper_half = values[..., half_size:]
    return jnp.concatenate(
        [
            lower_half * cos_table - upper_half * sin_table,
            upper_half * cos_table + lower_half * sin_table,
        ],
        axis=-1,
    )


def adam(master, grad, moment_one, moment_two, rate, decay):
    new_one = beta_first * moment_one + (1.0 - beta_first) * grad
    new_two = beta_second * moment_two + (1.0 - beta_second) * grad * grad
    ahead = (
        new_one
        / (1.0 - beta_first**STEP)
        / (jnp.sqrt(new_two / (1.0 - beta_second**STEP)) + adam_eps)
    )
    return (master - rate * (ahead + decay * master), new_one, new_two)


def tensor_peers():
    me = lax.axis_index("tensor")
    z, y = me // 2, me % 2
    return [
        ((z + dz) % 4) * 2 + (y + dy) % 2
        for dz, dy in ((2, 1), (1, 1), (3, 1), (2, 0), (1, 0), (3, 0), (0, 1))
    ]


def chip_peers():
    dp, seq = lax.axis_index("dp"), lax.axis_index("seq")
    x, core = seq // 2, seq % 2
    return [
        ((dp + dd) % 2, (x + dx) % 4, core)
        for dx, dd in ((2, 1), (1, 1), (3, 1), (0, 1), (2, 0), (1, 0), (3, 0))
    ]


def row_peers():
    seq = lax.axis_index("seq")
    x, core = seq // 2, seq % 2
    return [((x + dx) % 4, core) for dx in (2, 1, 3)]


def sibling():
    seq = lax.axis_index("seq")
    return seq + 1 - 2 * (seq % 2)


def greet(devices):
    barrier = pltpu.get_barrier_semaphore()
    for device in devices:
        pl.semaphore_signal(barrier, inc=1, device_id=device, device_id_type=MESH)
    pl.semaphore_wait(barrier, len(devices))


def remote(src, dst, sends, recvs, at, device):
    return pltpu.make_async_remote_copy(src, dst, sends.at[at], recvs.at[at], device, MESH)


def params(collective_id, mib):
    return pltpu.CompilerParams(
        collective_id=collective_id, has_side_effects=True, vmem_limit_bytes=mib * MIB
    )


def gather_kernel(mine, whole, sends, recvs, near_sends, near_recvs):
    dp, seq = lax.axis_index("dp"), lax.axis_index("seq")
    me = dp * 8 + seq
    peers = chip_peers()
    near = {"seq": sibling()}
    greet([{"dp": d, "seq": 2 * x + c} for d, x, c in peers] + [near])
    out = [
        remote(mine, whole.at[me], sends, recvs, i, {"dp": d, "seq": 2 * x + c})
        for i, (d, x, c) in enumerate(peers)
    ]
    for copy in out:
        copy.start()
    first = remote(mine, whole.at[me], near_sends, near_recvs, 7, near)
    first.start()
    whole[me] = mine[...]
    passed = []
    for i, (dd, dx) in ((6, (0, 1)), (5, (0, 3)), (3, (1, 0)), (4, (0, 2)), (2, (1, 1)), (1, (1, 3)), (0, (1, 2))):
        out[i].wait_recv()
        owner = (((dp + dd) % 2) * 4 + (seq // 2 + dx) % 4) * 2 + seq % 2
        forward = remote(whole.at[owner], whole.at[owner], near_sends, near_recvs, i, near)
        forward.start()
        passed.append(forward)
    for copy in out:
        copy.wait_send()
    first.wait()
    for copy in passed:
        copy.wait()


def gather_rows(mine):
    return pl.pallas_call(
        gather_kernel,
        out_shape=jax.ShapeDtypeStruct((16,) + mine.shape, mine.dtype),
        in_specs=[VMEM],
        out_specs=VMEM,
        scratch_shapes=[
            pltpu.SemaphoreType.DMA((7,)),
            pltpu.SemaphoreType.DMA((7,)),
            pltpu.SemaphoreType.DMA((8,)),
            pltpu.SemaphoreType.DMA((8,)),
        ],
        compiler_params=params(1, 32),
        name="gather_rows",
    )(mine)


def pairs_kernel(mine, whole, sends, recvs, near_sends, near_recvs):
    seq = lax.axis_index("seq")
    peers = row_peers()
    near = {"seq": sibling()}
    greet([{"seq": 2 * x + c} for x, c in peers] + [near])
    out = [
        remote(mine, whole.at[seq], sends, recvs, i, {"seq": 2 * x + c})
        for i, (x, c) in enumerate(peers)
    ]
    for copy in out:
        copy.start()
    first = remote(mine, whole.at[seq], near_sends, near_recvs, 3, near)
    first.start()
    whole[seq] = mine[...]
    passed = []
    for i, dx in ((1, 3), (2, 1), (0, 2)):
        out[i].wait_recv()
        owner = ((seq // 2 + dx) % 4) * 2 + seq % 2
        forward = remote(whole.at[owner], whole.at[owner], near_sends, near_recvs, i, near)
        forward.start()
        passed.append(forward)
    for copy in out:
        copy.wait_send()
    first.wait()
    for copy in passed:
        copy.wait()


def gather_pairs(mine):
    return pl.pallas_call(
        pairs_kernel,
        out_shape=jax.ShapeDtypeStruct((8,) + mine.shape, mine.dtype),
        in_specs=[VMEM],
        out_specs=VMEM,
        scratch_shapes=[
            pltpu.SemaphoreType.DMA((3,)),
            pltpu.SemaphoreType.DMA((3,)),
            pltpu.SemaphoreType.DMA((4,)),
            pltpu.SemaphoreType.DMA((4,)),
        ],
        compiler_params=params(2, 32),
        name="gather_pairs",
    )(mine)


def causal_bias(bias):
    seq = lax.axis_index("seq")
    rows, keys = bias.shape
    row = lax.broadcasted_iota(jnp.int32, (rows, keys), 0) + seq * rows
    key = lax.broadcasted_iota(jnp.int32, (rows, keys), 1)
    bias[...] = jnp.where(key <= row, 0.0, -1e30).astype(f32)


def nt(left, right):
    return lax.dot_general(left, right, (((1,), (1,)), ((), ())), preferred_element_type=f32)


def attend_kernel(query, pairs, kept, mixed, bias):
    causal_bias(bias)
    rows = query.shape[2]
    keys = bias.shape[1]
    lane = lax.broadcasted_iota(jnp.int32, (rows, 2 * HEAD_SIZE), 1)

    def one_sequence(i, carry):
        pair = pairs[:, i].reshape(keys, 2 * HEAD_SIZE)
        upper = []
        for head in range(GROUP):
            scores = nt(query[i, head], pair) + bias[...]
            row_max = jnp.max(scores, axis=-1, keepdims=True)
            weights = jnp.exp(scores - row_max)
            row_sum = jnp.sum(weights, axis=-1, keepdims=True)
            mix = jnp.dot(weights.astype(bf16), pair, preferred_element_type=f32) / row_sum
            kept[i, head] = jnp.where(lane < HEAD_SIZE, row_max + jnp.log(row_sum), mix)
            upper.append(mix)
        for at in range(GROUP // 2):
            low = pltpu.roll(upper[2 * at], HEAD_SIZE, 1)
            both = jnp.where(lane < HEAD_SIZE, low, upper[2 * at + 1])
            mixed[i, :, at * 2 * HEAD_SIZE : (at + 1) * 2 * HEAD_SIZE] = both.astype(bf16)
        return carry

    lax.fori_loop(0, query.shape[0], one_sequence, 0)


def attend(query, pairs):
    count, heads, rows, width = query.shape
    keys = pairs.shape[0] * pairs.shape[2]
    return pl.pallas_call(
        attend_kernel,
        out_shape=(
            jax.ShapeDtypeStruct(query.shape, f32),
            jax.ShapeDtypeStruct((count, rows, heads * HEAD_SIZE), bf16),
        ),
        in_specs=[VMEM, VMEM],
        out_specs=(VMEM, VMEM),
        scratch_shapes=[pltpu.VMEM((rows, keys), f32)],
        compiler_params=pltpu.CompilerParams(vmem_limit_bytes=48 * MIB),
        cost_estimate=pl.CostEstimate(
            flops=4 * count * heads * rows * keys * width,
            bytes_accessed=8 * MIB,
            transcendentals=count * heads * rows * keys,
        ),
        name="attend",
    )(query, pairs)


def attend_back_kernel(query, pairs, kept, grad, parts, grad_query, grad_pairs, landed, bias, total, sends, recvs):
    tensor = lax.axis_index("tensor")
    peers = tensor_peers()
    greet([{"tensor": peer} for peer in peers])
    out = [
        remote(
            parts.at[:, pl.ds(pl.multiple_of(peer * 32, 32), 32), :],
            landed.at[i],
            sends,
            recvs,
            i,
            {"tensor": peer},
        )
        for i, peer in enumerate(peers)
    ]
    for copy in out:
        copy.start()
    causal_bias(bias)
    rows = query.shape[2]
    keys = bias.shape[1]

    def one_sequence(i, carry):
        pair = pairs[:, i].reshape(keys, 2 * HEAD_SIZE)
        for head in range(GROUP):
            query_rows = query[i, head]
            grad_rows = grad[i, head]
            kept_rows = kept[i, head]
            probs = jnp.exp(nt(query_rows, pair) + bias[...] - kept_rows[:, :1])
            inner = jnp.sum(kept_rows * grad_rows.astype(f32), axis=-1, keepdims=True)
            grad_scores = (probs * (nt(grad_rows, pair) - inner)).astype(bf16)
            grad_query[i, head] = jnp.dot(grad_scores, pair, preferred_element_type=f32)
            term = jnp.dot(query_rows.T, grad_scores, preferred_element_type=f32) + jnp.dot(
                grad_rows.T, probs.astype(bf16), preferred_element_type=f32
            )
            if head == 0:
                total[...] = term
            else:
                total[...] += term
        for block in range(grad_pairs.shape[0]):
            grad_pairs[block, i] = total[:, block * rows : (block + 1) * rows].T.astype(bf16)
        return carry

    lax.fori_loop(0, query.shape[0], one_sequence, 0)
    for copy in out:
        copy.wait()


def attend_back(query, pairs, kept, grad, parts):
    count, heads, rows, width = query.shape
    keys = pairs.shape[0] * pairs.shape[2]
    return pl.pallas_call(
        attend_back_kernel,
        out_shape=(
            jax.ShapeDtypeStruct(query.shape, f32),
            jax.ShapeDtypeStruct(pairs.shape, bf16),
            jax.ShapeDtypeStruct((7, count, 32, parts.shape[2]), bf16),
        ),
        in_specs=[VMEM, VMEM, VMEM, VMEM, ANY],
        out_specs=(VMEM, VMEM, ANY),
        scratch_shapes=[
            pltpu.VMEM((rows, keys), f32),
            pltpu.VMEM((width, keys), f32),
            pltpu.SemaphoreType.DMA((7,)),
            pltpu.SemaphoreType.DMA((7,)),
        ],
        compiler_params=params(3, 56),
        cost_estimate=pl.CostEstimate(
            flops=10 * count * heads * rows * keys * width,
            bytes_accessed=10 * MIB,
            transcendentals=count * heads * rows * keys,
        ),
        name="attend_back",
    )(query, pairs, kept, grad, parts)


def block_of(peer):
    return pl.ds(pl.multiple_of(peer * 32, 32), 32)


def scatter_start(part, landed, sends, recvs):
    out = [
        remote(part.at[:, block_of(peer), :], landed.at[i], sends, recvs, i, {"tensor": peer})
        for i, peer in enumerate(tensor_peers())
    ]
    for copy in out:
        copy.start()
    return out


def owned_sum(part, landed, i, row):
    tensor = lax.axis_index("tensor")
    total = part[i, pl.ds(pl.multiple_of(tensor * 32 + row, 16), 16), :].astype(f32)
    for j in range(7):
        total = total + landed[j, i, pl.ds(row, 16), :].astype(f32)
    return total


def spread(rows, sends, recvs):
    tensor = lax.axis_index("tensor")
    mine = rows.at[:, block_of(tensor), :]
    out = [
        remote(mine, mine, sends, recvs, i, {"tensor": peer}) for i, peer in enumerate(tensor_peers())
    ]
    for copy in out:
        copy.start()
    for copy in out:
        copy.wait()


def own_chunks(body):
    def step(k, carry):
        body(k // 2, pl.multiple_of((k % 2) * 16, 16))
        return carry

    lax.fori_loop(0, 6, step, 0)


def middle_kernel(part, tokens, gain, mid, whole, landed, sends, recvs, sends_two, recvs_two):
    tensor = lax.axis_index("tensor")
    greet([{"tensor": peer} for peer in tensor_peers()])
    out = scatter_start(part, landed, sends, recvs)
    for copy in out:
        copy.wait()

    def chunk(i, row):
        rows = owned_sum(part, landed, i, row) + tokens[i, pl.ds(row, 16), :].astype(f32)
        mid[i, pl.ds(row, 16), :] = rows
        normed = rows * inverse_rms(rows)
        at = pl.ds(pl.multiple_of(tensor * 32 + row, 16), 16)
        whole[i, at, :] = (normed * gain[...]).astype(bf16)

    own_chunks(chunk)
    spread(whole, sends_two, recvs_two)


def tensor_semaphores():
    return [pltpu.SemaphoreType.DMA((7,))] * 4


def middle(part, tokens, gain):
    count, rows, width = part.shape
    return pl.pallas_call(
        middle_kernel,
        out_shape=(
            jax.ShapeDtypeStruct((count, 32, width), f32),
            jax.ShapeDtypeStruct(part.shape, bf16),
        ),
        in_specs=[VMEM] * 3,
        out_specs=(VMEM, VMEM),
        scratch_shapes=[pltpu.VMEM((7, count, 32, width), bf16)] + tensor_semaphores(),
        compiler_params=params(4, 48),
        cost_estimate=pl.CostEstimate(flops=MIB, bytes_accessed=200 * MIB, transcendentals=0),
        name="middle",
    )(part, tokens, gain)


def middle_back_kernel(
    part, mid, cotangent, gain, grad_mid, grad_gain, whole, landed, sends, recvs, sends_two, recvs_two
):
    tensor = lax.axis_index("tensor")
    greet([{"tensor": peer} for peer in tensor_peers()])
    out = scatter_start(part, landed, sends, recvs)
    for copy in out:
        copy.wait()
    grad_gain[...] = jnp.zeros_like(grad_gain)

    def chunk(i, row):
        grad = owned_sum(part, landed, i, row)
        rows = mid[i, pl.ds(row, 16), :]
        inverse = inverse_rms(rows)
        normed = rows * inverse
        product = grad * normed
        grad_gain[...] += product[:8] + product[8:]
        inner = jnp.mean(product * gain[...], axis=-1, keepdims=True)
        result = cotangent[i, pl.ds(row, 16), :].astype(f32) + inverse * (
            grad * gain[...] - normed * inner
        )
        grad_mid[i, pl.ds(row, 16), :] = result
        at = pl.ds(pl.multiple_of(tensor * 32 + row, 16), 16)
        whole[i, at, :] = result.astype(bf16)

    own_chunks(chunk)
    spread(whole, sends_two, recvs_two)


def middle_back(part, mid, cotangent, gain):
    count, rows, width = part.shape
    return pl.pallas_call(
        middle_back_kernel,
        out_shape=(
            jax.ShapeDtypeStruct((count, 32, width), f32),
            jax.ShapeDtypeStruct((8, width), f32),
            jax.ShapeDtypeStruct(part.shape, bf16),
        ),
        in_specs=[VMEM] * 4,
        out_specs=(VMEM, VMEM, VMEM),
        scratch_shapes=[pltpu.VMEM((7, count, 32, width), bf16)] + tensor_semaphores(),
        compiler_params=params(5, 48),
        cost_estimate=pl.CostEstimate(flops=MIB, bytes_accessed=200 * MIB, transcendentals=0),
        name="middle_back",
    )(part, mid, cotangent, gain)


def pairs_back_kernel(parts, total, near, ready, landed, near_sends, near_recvs, sends, recvs):
    seq = lax.axis_index("seq")
    x, core = seq // 2, seq % 2
    peers = row_peers()
    beside = {"seq": sibling()}
    greet([{"seq": 2 * px + c} for px, c in peers] + [beside])
    across = [
        remote(parts.at[2 * px + 1 - core], near.at[px], near_sends, near_recvs, px, beside)
        for px in range(4)
    ]
    for copy in across:
        copy.start()
    for copy in across:
        copy.wait()
    out = []
    for i, (px, c) in enumerate(peers):
        ready[i] = (parts[2 * px + core].astype(f32) + near[px].astype(f32)).astype(bf16)
        copy = remote(ready.at[i], landed.at[i], sends, recvs, i, {"seq": 2 * px + c})
        copy.start()
        out.append(copy)
    mine = parts[seq].astype(f32) + near[x].astype(f32)
    for copy in out:
        copy.wait()
    for i in range(3):
        mine = mine + landed[i].astype(f32)
    total[...] = mine


def scatter_pairs(parts):
    shape = parts.shape[1:]
    return pl.pallas_call(
        pairs_back_kernel,
        out_shape=jax.ShapeDtypeStruct(shape, f32),
        in_specs=[VMEM],
        out_specs=VMEM,
        scratch_shapes=[
            pltpu.VMEM((4,) + shape, bf16),
            pltpu.VMEM((3,) + shape, bf16),
            pltpu.VMEM((3,) + shape, bf16),
            pltpu.SemaphoreType.DMA((4,)),
            pltpu.SemaphoreType.DMA((4,)),
            pltpu.SemaphoreType.DMA((3,)),
            pltpu.SemaphoreType.DMA((3,)),
        ],
        compiler_params=params(6, 32),
        name="scatter_pairs",
    )(parts)


def ending_kernel(
    part, tokens, grad_mid, gain, weights, gain_two,
    input_grad, share, gain_sum,
    landed, near, ready, shares, gains, gains_in, gains_near,
    sends, recvs, near_sends, near_recvs, far_sends, far_recvs,
    gain_sends, gain_recvs, last_sends, last_recvs,
):
    dp, seq, tensor = lax.axis_index("dp"), lax.axis_index("seq"), lax.axis_index("tensor")
    x, core = seq // 2, seq % 2
    chips = chip_peers()
    beside = {"seq": sibling()}
    owners = [((dp + k // 8) % 2, (seq + k % 8) % 8) for k in range(1, 16)]
    greet(
        [{"tensor": peer} for peer in tensor_peers()]
        + [{"dp": d, "seq": s} for d, s in owners]
    )
    across = remote(weights.at[:, 1 - core], near, near_sends, near_recvs, 0, beside)
    across.start()
    out = scatter_start(part, landed, sends, recvs)
    across.wait()
    far = []
    for i, (d, px, c) in enumerate(chips):
        at = d * 4 + px
        ready[i] = (weights[at, core].astype(f32) + near[at].astype(f32)).astype(bf16)
        copy = remote(ready.at[i], shares.at[i], far_sends, far_recvs, i, {"dp": d, "seq": 2 * px + c})
        copy.start()
        far.append(copy)
    for copy in out:
        copy.wait()
    gains[0] = jnp.zeros_like(gains[0])
    gains[1] = gain_two[...]

    def chunk(i, row):
        grad = owned_sum(part, landed, i, row)
        rows = tokens[i, pl.ds(row, 16), :].astype(f32)
        inverse = inverse_rms(rows)
        normed = rows * inverse
        product = grad * normed
        gains[0] += product[:8] + product[8:]
        inner = jnp.mean(product * gain[...], axis=-1, keepdims=True)
        result = grad_mid[i, pl.ds(row, 16), :] + inverse * (grad * gain[...] - normed * inner)
        input_grad[i, pl.ds(row, 16), :] = result.astype(bf16)

    own_chunks(chunk)
    spread_gains = []
    for k, (d, s) in enumerate(owners):
        at = pl.ds(pl.multiple_of((d * 8 + s) * 128, 128), 128)
        copy = remote(gains.at[:, :, at], gains_in.at[k], gain_sends, gain_recvs, k, {"dp": d, "seq": s})
        copy.start()
        spread_gains.append(copy)
    for copy in far:
        copy.wait()
    mine = dp * 4 + x
    total = weights[mine, core].astype(f32) + near[mine].astype(f32)
    for i in range(7):
        total = total + shares[i].astype(f32)
    share[...] = total
    own = gains[:, :, pl.ds(pl.multiple_of((dp * 8 + seq) * 128, 128), 128)]
    for k, copy in enumerate(spread_gains):
        copy.wait()
        own = own + gains_in[k]
    gains_near[7] = own
    last = [
        remote(gains_near.at[7], gains_near.at[i], last_sends, last_recvs, i, {"tensor": peer})
        for i, peer in enumerate(tensor_peers())
    ]
    for copy in last:
        copy.start()
    for copy in last:
        copy.wait()
    z, y = tensor // 2, tensor % 2
    shifts = ((2, 1), (1, 1), (3, 1), (2, 0), (1, 0), (3, 0), (0, 1))
    total = jnp.zeros_like(own)
    for t in range(8):
        slot = jnp.int32(7)
        for i, (dz, dy) in enumerate(shifts):
            source = ((z + 4 - dz) % 4) * 2 + (y + dy) % 2
            slot = jnp.where(source == t, i, slot)
        total = total + gains_near[slot]
    gain_sum[...] = jnp.sum(total, axis=1)


def ending(part, tokens, grad_mid, gain, weights, gain_two):
    count, rows, width = part.shape
    columns = weights.shape[-1]
    weights = weights.reshape(8, 2, 128, columns)
    dma = pltpu.SemaphoreType.DMA
    return pl.pallas_call(
        ending_kernel,
        out_shape=(
            jax.ShapeDtypeStruct((count, 32, width), bf16),
            jax.ShapeDtypeStruct((128, columns), f32),
            jax.ShapeDtypeStruct((2, 128), f32),
        ),
        in_specs=[VMEM] * 6,
        out_specs=(VMEM, VMEM, VMEM),
        scratch_shapes=[
            pltpu.VMEM((7, count, 32, width), bf16),
            pltpu.VMEM((8, 128, columns), bf16),
            pltpu.VMEM((7, 128, columns), bf16),
            pltpu.VMEM((7, 128, columns), bf16),
            pltpu.VMEM((2, 8, width), f32),
            pltpu.VMEM((15, 2, 8, 128), f32),
            pltpu.VMEM((8, 2, 8, 128), f32),
            dma((7,)), dma((7,)), dma((1,)), dma((1,)), dma((7,)), dma((7,)),
            dma((15,)), dma((15,)), dma((7,)), dma((7,)),
        ],
        compiler_params=params(7, 48),
        name="ending",
    )(part, tokens, grad_mid, gain, weights, gain_two)


def shards(
    tokens,
    cotangent,
    query_weight,
    query_first,
    query_second,
    key_value_weight,
    key_value_first_moment,
    key_value_second_moment,
    output_weight,
    output_first,
    output_second,
    gate_up_weight,
    gate_up_first,
    gate_up_second,
    down_weight,
    down_first,
    down_second,
    norm_gains,
    gains_first,
    gains_second,
):
    count, local_len, width = tokens.shape
    token_count = count * local_len
    tensor = lax.axis_index("tensor")
    owners = ("dp", "seq")

    def own_rows(values):
        return lax.dynamic_slice_in_dim(values, tensor * 32, 32, 1)

    gate_up_low = jnp.concatenate([gate_up_weight[0], gate_up_weight[1]], axis=1).astype(bf16)
    gate_up_all = lax.all_gather(gate_up_low, owners, axis=0, tiled=True)
    down_all = lax.all_gather(down_weight.T.astype(bf16), owners, axis=0, tiled=True)

    packed = jnp.concatenate(
        [
            query_weight,
            key_value_weight.reshape(128, 2 * HEAD_SIZE),
            output_weight.T,
            jnp.pad(norm_gains.T, ((0, 0), (0, 126))),
        ],
        axis=1,
    ).astype(bf16)
    packed_all = gather_rows(packed).reshape(width, packed.shape[1])
    projection = packed_all[:, :384]
    output_all = packed_all[:, 384:640]
    gains_used = packed_all[:, 640:642].T.astype(f32)

    positions = lax.axis_index("seq") * local_len + jnp.arange(local_len, dtype=jnp.int32)
    cos_table, sin_table = rotary(positions)
    scale = HEAD_SIZE ** (-0.5)
    token_rows = tokens.astype(f32)
    inv_one = inverse_rms(token_rows)
    h_first = (token_rows * inv_one * gains_used[0]).astype(bf16).reshape(token_count, width)
    raw = jnp.dot(h_first, projection, preferred_element_type=f32)
    raw = raw.reshape(count, local_len, GROUP + 2, HEAD_SIZE)
    rotated = rotate(raw[:, :, : GROUP + 1], cos_table, sin_table).astype(bf16)
    query = (rotated[:, :, :GROUP] * bf16(scale)).transpose(0, 2, 1, 3)
    query = jnp.pad(query, ((0, 0), (0, 0), (0, 0), (0, HEAD_SIZE)))
    pair = jnp.concatenate([rotated[:, :, GROUP], raw[:, :, GROUP + 1].astype(bf16)], axis=-1)
    pairs = gather_pairs(pair)
    kept, mixed = attend(query, pairs)
    mixed = mixed.reshape(token_count, GROUP * HEAD_SIZE)
    attn_term = nt(mixed, output_all).astype(bf16).reshape(count, local_len, width)
    mid, h_second = middle(attn_term, own_rows(tokens), gains_used[1:])
    h_second = h_second.reshape(token_count, width)
    cotangent_rows = cotangent.reshape(token_count, width)

    units = gate_up_weight.shape[2]
    gate_up = jnp.dot(h_second, gate_up_all, preferred_element_type=f32)
    gate_in, up_in = gate_up[:, :units], gate_up[:, units:]
    sigmoid_gate = jax.nn.sigmoid(gate_in)
    silu_gate = gate_in * sigmoid_gate
    hidden_state = (silu_gate * up_in).astype(bf16)
    grad_hidden = jnp.dot(cotangent_rows, down_all, preferred_element_type=f32)
    grad_gate = grad_hidden * up_in * sigmoid_gate * (1.0 + gate_in * (1.0 - sigmoid_gate))
    grad_up = grad_hidden * silu_gate
    grad_units = jnp.concatenate([grad_gate.astype(bf16), grad_up.astype(bf16)], axis=1)
    second_term = nt(grad_units, gate_up_all).astype(bf16).reshape(count, local_len, width)
    mlp_term = nt(hidden_state, down_all).astype(bf16).reshape(count, local_len, width)

    def tn(left, right):
        return lax.dot_general(left, right, (((0,), (0,)), ((), ())), preferred_element_type=f32)

    grad_gate_up = tn(h_second, grad_units).astype(bf16)
    grad_down = tn(cotangent_rows, hidden_state).astype(bf16)
    share_gate_up = lax.psum_scatter(grad_gate_up, owners, scatter_dimension=0, tiled=True)
    share_down = lax.psum_scatter(grad_down, owners, scatter_dimension=0, tiled=True)

    grad_mid, gain_two, branch_low = middle_back(
        second_term, mid, own_rows(cotangent), gains_used[1:]
    )
    branch_low = branch_low.reshape(token_count, width)
    grad_attended = jnp.dot(branch_low, output_all, preferred_element_type=f32).astype(bf16)
    grad_out = tn(branch_low, mixed).astype(bf16)
    share_output = lax.psum_scatter(grad_out, owners, scatter_dimension=0, tiled=True)
    grad_groups = grad_attended.reshape(count, local_len, GROUP, HEAD_SIZE).transpose(0, 2, 1, 3)
    grad_groups = jnp.pad(grad_groups, ((0, 0), (0, 0), (0, 0), (HEAD_SIZE, 0)))
    grad_query, grad_pairs, landed = attend_back(query, pairs, kept, grad_groups, mlp_term)
    block_out = mid + own_rows(mlp_term).astype(f32) + jnp.sum(landed.astype(f32), axis=0)

    grad_pair = scatter_pairs(grad_pairs)
    grad_raw = jnp.concatenate(
        [
            grad_query[..., :HEAD_SIZE].transpose(0, 2, 1, 3) * scale,
            grad_pair[:, :, None, :HEAD_SIZE],
        ],
        axis=2,
    )
    grad_raw = rotate(grad_raw, cos_table, -sin_table)
    grad_raw = jnp.concatenate([grad_raw, grad_pair[:, :, None, HEAD_SIZE:]], axis=2)
    grad_raw = grad_raw.astype(bf16).reshape(token_count, 384)
    first_term = nt(grad_raw, projection).astype(bf16).reshape(count, local_len, width)
    grad_projection = tn(h_first, grad_raw).astype(bf16)
    input_grad, share_projection, share_gains = ending(
        first_term, own_rows(tokens), grad_mid, gains_used[:1], grad_projection, gain_two
    )

    query_new, query_first_new, query_second_new = adam(
        query_weight, share_projection[:, :256], query_first, query_second, rate_wide, weight_decay
    )
    pair_new, pair_first_new, pair_second_new = adam(
        key_value_weight,
        share_projection[:, None, 256:],
        key_value_first_moment,
        key_value_second_moment,
        rate_wide,
        weight_decay,
    )
    output_new, output_first_new, output_second_new = adam(
        output_weight,
        share_output.T.astype(f32),
        output_first,
        output_second,
        rate_output,
        weight_decay,
    )
    share_gate_up = share_gate_up.astype(f32)
    gate_up_new, gate_up_first_new, gate_up_second_new = adam(
        gate_up_weight,
        jnp.stack([share_gate_up[:, :units], share_gate_up[:, units:]]),
        gate_up_first,
        gate_up_second,
        rate_wide,
        weight_decay,
    )
    down_new, down_first_new, down_second_new = adam(
        down_weight, share_down.T.astype(f32), down_first, down_second, rate_down, weight_decay
    )
    gains_new, gains_first_new, gains_second_new = adam(
        norm_gains, share_gains, gains_first, gains_second, rate_gains, 0.0
    )
    return (
        block_out.astype(bf16),
        input_grad,
        query_new,
        query_first_new,
        query_second_new,
        pair_new,
        pair_first_new,
        pair_second_new,
        output_new,
        output_first_new,
        output_second_new,
        gate_up_new,
        gate_up_first_new,
        gate_up_second_new,
        down_new,
        down_first_new,
        down_second_new,
        gains_new,
        gains_first_new,
        gains_second_new,
    )


def solution(mesh):
    return jax.shard_map(
        shards,
        mesh=mesh,
        in_specs=(
            P("dp", "seq", None),
            P("dp", "seq", None),
            P(("dp", "seq"), "tensor"),
            P(("dp", "seq"), "tensor"),
            P(("dp", "seq"), "tensor"),
            P(("dp", "seq"), "tensor", None),
            P(("dp", "seq"), "tensor", None),
            P(("dp", "seq"), "tensor", None),
            P("tensor", ("dp", "seq")),
            P("tensor", ("dp", "seq")),
            P("tensor", ("dp", "seq")),
            P(None, ("dp", "seq"), "tensor"),
            P(None, ("dp", "seq"), "tensor"),
            P(None, ("dp", "seq"), "tensor"),
            P("tensor", ("dp", "seq")),
            P("tensor", ("dp", "seq")),
            P("tensor", ("dp", "seq")),
            P(None, ("dp", "seq")),
            P(None, ("dp", "seq")),
            P(None, ("dp", "seq")),
        ),
        out_specs=(
            P("dp", ("seq", "tensor"), None),
            P("dp", ("seq", "tensor"), None),
            P(("dp", "seq"), "tensor"),
            P(("dp", "seq"), "tensor"),
            P(("dp", "seq"), "tensor"),
            P(("dp", "seq"), "tensor", None),
            P(("dp", "seq"), "tensor", None),
            P(("dp", "seq"), "tensor", None),
            P("tensor", ("dp", "seq")),
            P("tensor", ("dp", "seq")),
            P("tensor", ("dp", "seq")),
            P(None, ("dp", "seq"), "tensor"),
            P(None, ("dp", "seq"), "tensor"),
            P(None, ("dp", "seq"), "tensor"),
            P("tensor", ("dp", "seq")),
            P("tensor", ("dp", "seq")),
            P("tensor", ("dp", "seq")),
            P(None, ("dp", "seq")),
            P(None, ("dp", "seq")),
            P(None, ("dp", "seq")),
        ),
        check_vma=False,
    )
```

```python
import jax
import jax.numpy as jnp
from jax import lax
from jax.experimental import pallas as pl
from jax.experimental.pallas import tpu as pltpu
from jax.sharding import PartitionSpec as P

QUERY_HEADS = 32
KEY_VALUE_HEADS = 8
HEAD_SIZE = 64
STEP = 10
GROUP = QUERY_HEADS // KEY_VALUE_HEADS


norm_eps = 1e-05
rope_base = 500000.0
beta_first = 0.9
beta_second = 0.95
adam_eps = 1e-08
weight_decay = 0.1
rate_wide = 0.07
rate_down = 0.035
rate_output = 1.0
rate_gains = 0.7

bf16 = jnp.bfloat16
f32 = jnp.float32
MESH = pl.DeviceIdType.MESH
VMEM = pl.BlockSpec(memory_space=pltpu.VMEM)
ANY = pl.BlockSpec(memory_space=pl.ANY)
MIB = 1024 * 1024


def inverse_rms(values):
    return lax.rsqrt(jnp.mean(values * values, axis=-1, keepdims=True) + norm_eps)


def rotary(positions):
    half_size = HEAD_SIZE // 2
    freqs = rope_base ** (-2.0 * jnp.arange(half_size, dtype=jnp.float32) / HEAD_SIZE)
    angles = positions.astype(jnp.float32)[:, None] * freqs[None, :]
    return (jnp.cos(angles)[:, None, :], jnp.sin(angles)[:, None, :])


def rotate(values, cos_table, sin_table):
    half_size = values.shape[-1] // 2
    lower_half = values[..., :half_size]
    upper_half = values[..., half_size:]
    return jnp.concatenate(
        [
            lower_half * cos_table - upper_half * sin_table,
            upper_half * cos_table + lower_half * sin_table,
        ],
        axis=-1,
    )


def adam(master, grad, moment_one, moment_two, rate, decay):
    new_one = beta_first * moment_one + (1.0 - beta_first) * grad
    new_two = beta_second * moment_two + (1.0 - beta_second) * grad * grad
    ahead = (
        new_one
        / (1.0 - beta_first**STEP)
        / (jnp.sqrt(new_two / (1.0 - beta_second**STEP)) + adam_eps)
    )
    return (master - rate * (ahead + decay * master), new_one, new_two)


def tensor_peers():
    me = lax.axis_index("tensor")
    z, y = me // 2, me % 2
    return [
        ((z + dz) % 4) * 2 + (y + dy) % 2
        for dz, dy in ((2, 1), (1, 1), (3, 1), (2, 0), (1, 0), (3, 0), (0, 1))
    ]


def chip_peers():
    dp, seq = lax.axis_index("dp"), lax.axis_index("seq")
    x, core = seq // 2, seq % 2
    return [
        ((dp + dd) % 2, (x + dx) % 4, core)
        for dx, dd in ((2, 1), (1, 1), (3, 1), (0, 1), (2, 0), (1, 0), (3, 0))
    ]


def row_peers():
    seq = lax.axis_index("seq")
    x, core = seq // 2, seq % 2
    return [((x + dx) % 4, core) for dx in (2, 1, 3)]


def sibling():
    seq = lax.axis_index("seq")
    return seq + 1 - 2 * (seq % 2)


def greet(devices):
    barrier = pltpu.get_barrier_semaphore()
    for device in devices:
        pl.semaphore_signal(barrier, inc=1, device_id=device, device_id_type=MESH)
    pl.semaphore_wait(barrier, len(devices))


def remote(src, dst, sends, recvs, at, device):
    return pltpu.make_async_remote_copy(src, dst, sends.at[at], recvs.at[at], device, MESH)


def params(collective_id, mib):
    return pltpu.CompilerParams(
        collective_id=collective_id, has_side_effects=True, vmem_limit_bytes=mib * MIB
    )


def gather_kernel(mine, whole, sends, recvs, near_sends, near_recvs):
    dp, seq = lax.axis_index("dp"), lax.axis_index("seq")
    me = dp * 8 + seq
    peers = chip_peers()
    near = {"seq": sibling()}
    greet([{"dp": d, "seq": 2 * x + c} for d, x, c in peers] + [near])
    out = [
        remote(mine, whole.at[me], sends, recvs, i, {"dp": d, "seq": 2 * x + c})
        for i, (d, x, c) in enumerate(peers)
    ]
    for copy in out:
        copy.start()
    first = remote(mine, whole.at[me], near_sends, near_recvs, 7, near)
    first.start()
    whole[me] = mine[...]
    passed = []
    for i, (dd, dx) in ((6, (0, 1)), (5, (0, 3)), (3, (1, 0)), (4, (0, 2)), (2, (1, 1)), (1, (1, 3)), (0, (1, 2))):
        out[i].wait_recv()
        owner = (((dp + dd) % 2) * 4 + (seq // 2 + dx) % 4) * 2 + seq % 2
        forward = remote(whole.at[owner], whole.at[owner], near_sends, near_recvs, i, near)
        forward.start()
        passed.append(forward)
    for copy in out:
        copy.wait_send()
    first.wait()
    for copy in passed:
        copy.wait()


def gather_rows(mine):
    return pl.pallas_call(
        gather_kernel,
        out_shape=jax.ShapeDtypeStruct((16,) + mine.shape, mine.dtype),
        in_specs=[VMEM],
        out_specs=VMEM,
        scratch_shapes=[
            pltpu.SemaphoreType.DMA((7,)),
            pltpu.SemaphoreType.DMA((7,)),
            pltpu.SemaphoreType.DMA((8,)),
            pltpu.SemaphoreType.DMA((8,)),
        ],
        compiler_params=params(1, 32),
        name="gather_rows",
    )(mine)


def pairs_kernel(mine, whole, sends, recvs, near_sends, near_recvs):
    seq = lax.axis_index("seq")
    peers = row_peers()
    near = {"seq": sibling()}
    greet([{"seq": 2 * x + c} for x, c in peers] + [near])
    out = [
        remote(mine, whole.at[seq], sends, recvs, i, {"seq": 2 * x + c})
        for i, (x, c) in enumerate(peers)
    ]
    for copy in out:
        copy.start()
    first = remote(mine, whole.at[seq], near_sends, near_recvs, 3, near)
    first.start()
    whole[seq] = mine[...]
    passed = []
    for i, dx in ((1, 3), (2, 1), (0, 2)):
        out[i].wait_recv()
        owner = ((seq // 2 + dx) % 4) * 2 + seq % 2
        forward = remote(whole.at[owner], whole.at[owner], near_sends, near_recvs, i, near)
        forward.start()
        passed.append(forward)
    for copy in out:
        copy.wait_send()
    first.wait()
    for copy in passed:
        copy.wait()


def gather_pairs(mine):
    return pl.pallas_call(
        pairs_kernel,
        out_shape=jax.ShapeDtypeStruct((8,) + mine.shape, mine.dtype),
        in_specs=[VMEM],
        out_specs=VMEM,
        scratch_shapes=[
            pltpu.SemaphoreType.DMA((3,)),
            pltpu.SemaphoreType.DMA((3,)),
            pltpu.SemaphoreType.DMA((4,)),
            pltpu.SemaphoreType.DMA((4,)),
        ],
        compiler_params=params(2, 32),
        name="gather_pairs",
    )(mine)


def causal_bias(bias):
    seq = lax.axis_index("seq")
    rows, keys = bias.shape
    row = lax.broadcasted_iota(jnp.int32, (rows, keys), 0) + seq * rows
    key = lax.broadcasted_iota(jnp.int32, (rows, keys), 1)
    bias[...] = jnp.where(key <= row, 0.0, -1e30).astype(f32)


def nt(left, right):
    return lax.dot_general(left, right, (((1,), (1,)), ((), ())), preferred_element_type=f32)


def attend_kernel(query, pairs, kept, mixed, bias):
    causal_bias(bias)
    rows = query.shape[2]
    keys = bias.shape[1]
    lane = lax.broadcasted_iota(jnp.int32, (rows, 2 * HEAD_SIZE), 1)

    def one_sequence(i, carry):
        pair = pairs[:, i].reshape(keys, 2 * HEAD_SIZE)
        upper = []
        for head in range(GROUP):
            scores = nt(query[i, head], pair) + bias[...]
            row_max = jnp.max(scores, axis=-1, keepdims=True)
            weights = jnp.exp(scores - row_max)
            row_sum = jnp.sum(weights, axis=-1, keepdims=True)
            mix = jnp.dot(weights.astype(bf16), pair, preferred_element_type=f32) / row_sum
            kept[i, head] = jnp.where(lane < HEAD_SIZE, row_max + jnp.log(row_sum), mix)
            upper.append(mix)
        for at in range(GROUP // 2):
            low = pltpu.roll(upper[2 * at], HEAD_SIZE, 1)
            both = jnp.where(lane < HEAD_SIZE, low, upper[2 * at + 1])
            mixed[i, :, at * 2 * HEAD_SIZE : (at + 1) * 2 * HEAD_SIZE] = both.astype(bf16)
        return carry

    lax.fori_loop(0, query.shape[0], one_sequence, 0)


def attend(query, pairs):
    count, heads, rows, width = query.shape
    keys = pairs.shape[0] * pairs.shape[2]
    return pl.pallas_call(
        attend_kernel,
        out_shape=(
            jax.ShapeDtypeStruct(query.shape, f32),
            jax.ShapeDtypeStruct((count, rows, heads * HEAD_SIZE), bf16),
        ),
        in_specs=[VMEM, VMEM],
        out_specs=(VMEM, VMEM),
        scratch_shapes=[pltpu.VMEM((rows, keys), f32)],
        compiler_params=pltpu.CompilerParams(vmem_limit_bytes=48 * MIB),
        cost_estimate=pl.CostEstimate(
            flops=4 * count * heads * rows * keys * width,
            bytes_accessed=8 * MIB,
            transcendentals=count * heads * rows * keys,
        ),
        name="attend",
    )(query, pairs)


def block_of(peer):
    return pl.ds(pl.multiple_of(peer * 32, 32), 32)


def scatter_start(part, landed, sends, recvs):
    out = [
        remote(part.at[:, block_of(peer), :], landed.at[i], sends, recvs, i, {"tensor": peer})
        for i, peer in enumerate(tensor_peers())
    ]
    for copy in out:
        copy.start()
    return out


def owned_sum(part, landed, i, row):
    tensor = lax.axis_index("tensor")
    total = part[i, pl.ds(pl.multiple_of(tensor * 32 + row, 16), 16), :].astype(f32)
    for j in range(7):
        total = total + landed[j, i, pl.ds(row, 16), :].astype(f32)
    return total


def own_chunks(body):
    def step(k, carry):
        body(k // 2, pl.multiple_of((k % 2) * 16, 16))
        return carry

    lax.fori_loop(0, 6, step, 0)


def middle_kernel(part, tokens, gain, mid, normed_rows, landed, sends, recvs):
    greet([{"tensor": peer} for peer in tensor_peers()])
    out = scatter_start(part, landed, sends, recvs)
    for copy in out:
        copy.wait()

    def chunk(i, row):
        at = pl.ds(row, 16)
        rows = owned_sum(part, landed, i, row) + tokens[i, at, :].astype(f32)
        mid[i, at, :] = rows
        normed_rows[i, at, :] = (rows * inverse_rms(rows) * gain[...]).astype(bf16)

    own_chunks(chunk)


def middle(part, tokens, gain):
    count, rows, width = part.shape
    return pl.pallas_call(
        middle_kernel,
        out_shape=(
            jax.ShapeDtypeStruct((count, 32, width), f32),
            jax.ShapeDtypeStruct((count, 32, width), bf16),
        ),
        in_specs=[VMEM] * 3,
        out_specs=(VMEM, VMEM),
        scratch_shapes=[
            pltpu.VMEM((7, count, 32, width), bf16),
            pltpu.SemaphoreType.DMA((7,)),
            pltpu.SemaphoreType.DMA((7,)),
        ],
        compiler_params=params(4, 48),
        cost_estimate=pl.CostEstimate(flops=MIB, bytes_accessed=100 * MIB, transcendentals=0),
        name="middle",
    )(part, tokens, gain)


class Spread:
    def __init__(self, buffer, sends, recvs):
        tensor = lax.axis_index("tensor")
        self.buffer, self.sends, self.recvs = buffer, sends, recvs
        self.z, self.y = tensor // 2, tensor % 2
        self.started = {}

    def at(self, dz, dy):
        return ((self.z + dz) % 4) * 2 + (self.y + dy) % 2

    def send(self, k, block, to, half=None):
        ref = self.buffer.at[block]
        if half is not None:
            rows = self.buffer.shape[1] // 2
            ref = self.buffer.at[block, pl.ds(half * rows, rows)]
        copy = remote(ref, ref, self.sends, self.recvs, k, {"tensor": to})
        copy.start()
        self.started[k] = copy

    def start(self):
        mine = self.at(0, 0)
        self.send(0, mine, self.at(0, 1))
        self.send(1, mine, self.at(1, 0))
        self.send(2, mine, self.at(3, 0))

    def pass_partner(self):
        self.started[0].wait_recv()
        self.send(3, self.at(0, 1), self.at(1, 0))
        self.send(4, self.at(0, 1), self.at(3, 0))

    def pass_on(self, dy):
        k = 1 + 2 * dy
        self.started[k].wait_recv()
        self.send(5 + 2 * dy, self.at(3, dy), self.at(1, 0), 0)
        self.started[k + 1].wait_recv()
        self.send(6 + 2 * dy, self.at(1, dy), self.at(3, 0), 1)

    def finish(self):
        for k in range(5, 9):
            self.started[k].wait_recv()

    def drain(self):
        for copy in self.started.values():
            copy.wait_send()


def spread_peers():
    tensor = lax.axis_index("tensor")
    z, y = tensor // 2, tensor % 2
    return [((z + dz) % 4) * 2 + (y + dy) % 2 for dz, dy in ((0, 1), (1, 0), (3, 0))]


def tn(left, right):
    return lax.dot_general(left, right, (((0,), (0,)), ((), ())), preferred_element_type=f32)


def columns(tile, size):
    return pl.ds(pl.multiple_of(tile * size, size), size)


def feed_forward_kernel(
    own, cotangent, weights, mid, gain,
    branch, grad_mid, grad_gain, mlp_out, grads_out,
    gate_up, down, cot, normed, grad_hidden, grad_units, hidden, second, landed, mlp, grads,
    sends, recvs, back_sends, back_recvs, local, cot_sems, out_sems, mlp_sem,
):
    tensor = lax.axis_index("tensor")
    units = down.shape[3]
    width = 16 * 128
    dp = lax.axis_index("dp")
    load_down = [
        pltpu.make_async_copy(
            weights.at[:, k, :, pl.ds(2 * units, units)], down.at[(dp + k) % 2], local.at[k]
        )
        for k in range(2)
    ]
    load_gate_up = [
        pltpu.make_async_copy(
            weights.at[:, k, :, pl.ds(0, 2 * units)], gate_up.at[(dp + k) % 2], local.at[2 + k]
        )
        for k in range(2)
    ]
    for copy in load_down:
        copy.start()
    load_cot = [
        pltpu.make_async_copy(cotangent.at[:, t], cot.at[t], cot_sems.at[t]) for t in range(8)
    ]
    for copy in load_cot:
        copy.start()
    for copy in load_gate_up:
        copy.start()
    greet([{"tensor": peer} for peer in tensor_peers()])
    for i in range(3):
        normed[tensor, 32 * i : 32 * i + 32, :] = own[i]
    spread = Spread(normed, sends, recvs)
    spread.start()
    for copy in load_cot + load_down:
        copy.wait()

    def hidden_step(tile, carry):
        at = columns(tile, 256)
        product = jnp.dot(
            cot[...].reshape(8 * 96, width),
            down[:, :, :, at].reshape(width, 256),
            preferred_element_type=f32,
        )
        grad_hidden[:, :, at] = product.reshape(8, 96, 256)
        return carry

    lax.fori_loop(0, units // 256, hidden_step, 0)
    for copy in load_gate_up:
        copy.wait()

    back = {}

    def block(dz):
        first = ((spread.z + dz) % 4) * 2
        both = pl.ds(first, 2)

        def units_step(tile, carry):
            at = columns(tile, 256)
            up_at = pl.ds(pl.multiple_of(units + tile * 256, 256), 256)
            rows = normed[both].reshape(192, width)
            gate_columns = gate_up[:, :, :, at].reshape(width, 256)
            up_columns = gate_up[:, :, :, up_at].reshape(width, 256)
            gate_in = jnp.dot(rows, gate_columns, preferred_element_type=f32)
            up_in = jnp.dot(rows, up_columns, preferred_element_type=f32)
            grad = grad_hidden[both, :, at].reshape(192, 256)
            sigmoid = jax.nn.sigmoid(gate_in)
            silu = gate_in * sigmoid
            hidden[both, :, at] = (silu * up_in).astype(bf16).reshape(2, 96, 256)
            grad_gate = grad * up_in * sigmoid * (1.0 + gate_in * (1.0 - sigmoid))
            grad_units[both, :, at] = grad_gate.astype(bf16).reshape(2, 96, 256)
            grad_units[both, :, up_at] = (grad * silu).astype(bf16).reshape(2, 96, 256)
            return carry

        lax.fori_loop(0, units // 256, units_step, 0)

        def second_step(tile, carry):
            at = columns(tile, 512)
            rows = grad_units[both].reshape(192, 2 * units)
            weight_rows = gate_up[tile // 2, pl.ds((tile % 2) * 4, 4)].reshape(512, 2 * units)
            second[both, :, at] = nt(rows, weight_rows).astype(bf16).reshape(2, 96, 512)
            return carry

        lax.fori_loop(0, width // 512, second_step, 0)
        for dy in (1, 0):
            if (dz, dy) != (0, 0):
                to = spread.at(dz, dy)
                k = 2 * dz + dy - 1
                copy = remote(
                    second.at[to], landed.at[k], back_sends, back_recvs, k, {"tensor": to}
                )
                copy.start()
                back[k] = copy

    spread.pass_partner()
    spread.pass_on(0)
    block(0)
    spread.pass_on(1)
    block(1)
    block(3)
    spread.finish()
    block(2)

    def mlp_step(tile, carry):
        at = columns(tile, 256)
        rows = hidden[...].reshape(8 * 96, units)
        weight_rows = down[tile // 4, pl.ds((tile % 4) * 2, 2)].reshape(256, units)
        mlp[:, :, at] = nt(rows, weight_rows).astype(bf16).reshape(8, 96, 256)
        return carry

    lax.fori_loop(0, width // 256, mlp_step, 0)
    store_mlp = pltpu.make_async_copy(mlp, mlp_out, mlp_sem)
    store_mlp.start()

    def store(tile, slot):
        place = grads_out.at[pl.ds((tile % 4) * 2, 2), (tile // 4 + dp) % 2]
        return pltpu.make_async_copy(grads.at[slot], place, out_sems.at[slot])

    def grads_pair(pair, carry):
        for slot in range(2):
            tile = 2 * pair + slot
            at = columns(tile, 256)

            @pl.when(pair > 0)
            def _():
                store(tile - 2, slot).wait()

            wide = tn(
                normed[:, :, at].reshape(8 * 96, 256), grad_units[...].reshape(8 * 96, 2 * units)
            )
            grads[slot, :, :, : 2 * units] = wide.astype(bf16).reshape(2, 128, 2 * units)
            narrow = tn(cot[:, :, :, at].reshape(8 * 96, 256), hidden[...].reshape(8 * 96, units))
            grads[slot, :, :, 2 * units :] = narrow.astype(bf16).reshape(2, 128, units)
            store(tile, slot).start()
        return carry

    tiles = width // 256
    lax.fori_loop(0, tiles // 2, grads_pair, 0)
    for slot in range(2):
        store(tiles - 2 + slot, slot).wait()
    store_mlp.wait()
    spread.drain()
    for copy in back.values():
        copy.wait()
    grad_gain[...] = jnp.zeros_like(grad_gain)

    def chunk(k, carry):
        at = pl.ds(pl.multiple_of(k * 16, 16), 16)
        grad = second[tensor, at, :].astype(f32)
        for j in range(7):
            grad = grad + landed[j, at, :].astype(f32)
        rows = mid[at, :]
        inverse = inverse_rms(rows)
        normed_rows = rows * inverse
        product = grad * normed_rows
        grad_gain[...] += product[:8] + product[8:]
        inner = jnp.mean(product * gain[...], axis=-1, keepdims=True)
        own_cot = cot[tensor, k // 2, pl.ds(pl.multiple_of((k % 2) * 16, 16), 16), :].astype(f32)
        result = own_cot + inverse * (grad * gain[...] - normed_rows * inner)
        grad_mid[at, :] = result
        branch[at, :] = result.astype(bf16)
        return carry

    lax.fori_loop(0, 6, chunk, 0)


def feed_forward(own, cotangent, weights, mid, gain):
    rows, width = mid.shape
    units = weights.shape[3] // 3
    dma = pltpu.SemaphoreType.DMA
    return pl.pallas_call(
        feed_forward_kernel,
        out_shape=(
            jax.ShapeDtypeStruct((rows, width), bf16),
            jax.ShapeDtypeStruct((rows, width), f32),
            jax.ShapeDtypeStruct((8, width), f32),
            jax.ShapeDtypeStruct((8, rows, width), bf16),
            jax.ShapeDtypeStruct(weights.shape, bf16),
        ),
        in_specs=[VMEM, ANY, ANY, VMEM, VMEM],
        out_specs=(VMEM, VMEM, VMEM, ANY, ANY),
        scratch_shapes=[
            pltpu.VMEM((2, 8, 128, 2 * units), bf16),
            pltpu.VMEM((2, 8, 128, units), bf16),
            pltpu.VMEM((8, 3, 32, width), bf16),
            pltpu.VMEM((8, rows, width), bf16),
            pltpu.VMEM((8, rows, units), f32),
            pltpu.VMEM((8, rows, 2 * units), bf16),
            pltpu.VMEM((8, rows, units), bf16),
            pltpu.VMEM((8, rows, width), bf16),
            pltpu.VMEM((7, rows, width), bf16),
            pltpu.VMEM((8, rows, width), bf16),
            pltpu.VMEM((2, 2, 128, 3 * units), bf16),
            dma((9,)), dma((9,)), dma((7,)), dma((7,)), dma((4,)), dma((8,)), dma((2,)), dma,
        ],
        compiler_params=params(5, 60),
        cost_estimate=pl.CostEstimate(
            flops=18 * 8 * rows * width * units, bytes_accessed=120 * MIB, transcendentals=0
        ),
        name="feed_forward",
    )(own, cotangent, weights, mid, gain)


def turn(values, cos_table, sin_table):
    lane = lax.broadcasted_iota(jnp.int32, values.shape, 1)
    half = HEAD_SIZE // 2
    other = jnp.where(
        lane % HEAD_SIZE < half,
        pltpu.roll(values, values.shape[1] - half, 1),
        pltpu.roll(values, half, 1),
    )
    return values * cos_table + other * sin_table


def backward_kernel(
    branch, query, pairs, kept, mixed, packed, h_first, mlp_part, mid, tokens, grad_mid, gain,
    gain_two, cos_table, sin_table,
    input_grad, block_out, share, gain_sum,
    whole, part, landed, mlp_landed, mlp_own, attended, raw, grad_pairs, near_pairs, ready_pairs,
    landed_pairs, bias, total, weights, near, ready, shares, gains, gains_in, gains_near,
    out_sends, out_recvs, mlp_sends, mlp_recvs, back_sends, back_recvs, pair_near_sends,
    pair_near_recvs, pair_sends, pair_recvs, near_sends, near_recvs, far_sends, far_recvs,
    gain_sends, gain_recvs, last_sends, last_recvs, local,
):
    dp, seq, tensor = lax.axis_index("dp"), lax.axis_index("seq"), lax.axis_index("tensor")
    x, core = seq // 2, seq % 2
    peers = tensor_peers()
    rows_beside = row_peers()
    chips = chip_peers()
    beside = {"seq": sibling()}
    owners = [((dp + k // 8) % 2, (seq + k % 8) % 8) for k in range(1, 16)]
    count, width = whole.shape[0], whole.shape[2]
    rows, keys = bias.shape
    greet(
        [{"tensor": peer} for peer in peers] + [{"dp": d, "seq": s} for d, s in owners]
    )
    mine = pl.ds(pl.multiple_of(tensor * 32, 32), 32)
    spread = [
        remote(
            branch.at[pl.ds(32 * i, 32)], whole.at[i, mine], out_sends, out_recvs, 7 * i + k,
            {"tensor": peer},
        )
        for i in range(count)
        for k, peer in enumerate(peers)
    ]
    for copy in spread:
        copy.start()
    mlp = [
        remote(mlp_part.at[peer], mlp_landed.at[k], mlp_sends, mlp_recvs, k, {"tensor": peer})
        for k, peer in enumerate(peers)
    ]
    for copy in mlp:
        copy.start()
    load_own = pltpu.make_async_copy(mlp_part.at[tensor], mlp_own, local)
    load_own.start()
    for i in range(count):
        whole[i, mine, :] = branch[32 * i : 32 * i + 32, :]
    causal_bias(bias)
    lane = lax.broadcasted_iota(jnp.int32, (rows, 2 * HEAD_SIZE), 1)
    scale = HEAD_SIZE ** (-0.5)

    def sequence(i):
        for copy in spread[7 * i : 7 * i + 7]:
            copy.wait_recv()
        attended[...] = (
            jnp.dot(whole[i], packed[:, 384:640], preferred_element_type=f32)
            .astype(bf16)
            .astype(f32)
        )
        total[...] = jnp.zeros_like(total)

        def head_pair(at, carry):
            columns_at = columns(at, 2 * HEAD_SIZE)
            grads_here = attended[:, columns_at]
            grad_query = []
            for odd in range(2):
                pair = pairs[:, i].reshape(keys, 2 * HEAD_SIZE)
                placed = grads_here if odd else pltpu.roll(grads_here, HEAD_SIZE, 1)
                placed = jnp.where(lane >= HEAD_SIZE, placed, 0.0)
                grad_rows = placed.astype(bf16)
                query_rows = query[i, 2 * at + odd]
                kept_rows = kept[i, 2 * at + odd]
                probs = jnp.exp(nt(query_rows, pair) + bias[...] - kept_rows[:, :1])
                inner = jnp.sum(kept_rows * placed, axis=-1, keepdims=True)
                grad_scores = (probs * (nt(grad_rows, pair) - inner)).astype(bf16)
                grad_query.append(jnp.dot(grad_scores, pair, preferred_element_type=f32))
                total[...] += jnp.dot(
                    query_rows.T, grad_scores, preferred_element_type=f32
                ) + jnp.dot(grad_rows.T, probs.astype(bf16), preferred_element_type=f32)
            both = jnp.where(lane < HEAD_SIZE, grad_query[0], pltpu.roll(grad_query[1], HEAD_SIZE, 1))
            both = turn(both * scale, cos_table[...], sin_table[...])
            raw[i, :, columns_at] = both.astype(bf16)
            return carry

        lax.fori_loop(0, GROUP // 2, head_pair, 0)
        for block in range(8):
            grad_pairs[block // 2, block % 2, i] = (
                total[:, block * rows : (block + 1) * rows].T.astype(bf16)
            )

    def cross(i):
        copy = remote(
            grad_pairs.at[:, 1 - core, i], near_pairs.at[i], pair_near_sends, pair_near_recvs, i,
            beside,
        )
        copy.start()
        return copy

    def onward(i, crossing):
        crossing.wait()
        out = []
        for k, (px, c) in enumerate(rows_beside):
            both = grad_pairs[px, core, i].astype(f32) + near_pairs[i, px].astype(f32)
            ready_pairs[i, k] = both.astype(bf16)
            copy = remote(
                ready_pairs.at[i, k], landed_pairs.at[i, k], pair_sends, pair_recvs, 3 * i + k,
                {"seq": 2 * px + c},
            )
            copy.start()
            out.append(copy)
        return out

    def settle(i, moving):
        mine_pairs = grad_pairs[x, core, i].astype(f32) + near_pairs[i, x].astype(f32)
        for k, copy in enumerate(moving):
            copy.wait()
            mine_pairs = mine_pairs + landed_pairs[i, k].astype(f32)
        turned = turn(mine_pairs, cos_table[...], sin_table[...])
        raw[i, :, 256:] = jnp.where(lane < HEAD_SIZE, turned, mine_pairs).astype(bf16)

        def term(tile, carry):
            at = columns(tile, 512)
            part[i, :, at] = nt(raw[i], packed[at, :384]).astype(bf16)
            return carry

        lax.fori_loop(0, width // 512, term, 0)
        out = [
            remote(
                part.at[i, block_of(peer)], landed.at[k, i], back_sends, back_recvs, 7 * i + k,
                {"tensor": peer},
            )
            for k, peer in enumerate(peers)
        ]
        for copy in out:
            copy.start()
        return out

    def outer(tile, carry):
        at = columns(tile, 256)
        product = tn(
            whole[:, :, at].reshape(count * rows, 256), mixed[...].reshape(count * rows, 256)
        )
        weights[tile, :, :, 384:] = product.astype(bf16).reshape(2, 128, 256)
        return carry

    def inner_weights(tile, carry):
        at = columns(tile, 256)
        product = tn(
            h_first[:, :, at].reshape(count * rows, 256), raw[...].reshape(count * rows, 384)
        )
        weights[tile, :, :, :384] = product.astype(bf16).reshape(2, 128, 384)
        return carry

    sequence(0)
    crossing = cross(0)
    sequence(1)
    moving = onward(0, crossing)
    crossing = cross(1)
    sequence(2)
    back = settle(0, moving)
    moving = onward(1, crossing)
    crossing = cross(2)
    lax.fori_loop(0, width // 256, outer, 0)
    back += settle(1, moving)
    moving = onward(2, crossing)
    gains[0] = jnp.zeros_like(gains[0])
    gains[1] = gain_two[...]
    back += settle(2, moving)
    lax.fori_loop(0, width // 256, inner_weights, 0)
    across = remote(weights.at[:, 1 - core], near, near_sends, near_recvs, 0, beside)
    across.start()
    load_own.wait()
    for copy in mlp:
        copy.wait()

    def finish_rows(i, row):
        at = pl.ds(pl.multiple_of(i * 32 + row, 16), 16)
        result = mid[at, :] + mlp_own[at, :].astype(f32)
        for k in range(7):
            result = result + mlp_landed[k, at, :].astype(f32)
        block_out[i, pl.ds(row, 16), :] = result.astype(bf16)

    own_chunks(finish_rows)
    across.wait()
    far = []
    for i, (d, px, c) in enumerate(chips):
        at = d * 4 + px
        ready[i] = (weights[at, core].astype(f32) + near[at].astype(f32)).astype(bf16)
        copy = remote(ready.at[i], shares.at[i], far_sends, far_recvs, i, {"dp": d, "seq": 2 * px + c})
        copy.start()
        far.append(copy)
    for copy in spread:
        copy.wait_send()
    for copy in back:
        copy.wait()

    def chunk(i, row):
        grad = owned_sum(part, landed, i, row)
        token_rows = tokens[i, pl.ds(row, 16), :].astype(f32)
        inverse = inverse_rms(token_rows)
        normed = token_rows * inverse
        product = grad * normed
        gains[0] += product[:8] + product[8:]
        inner = jnp.mean(product * gain[...], axis=-1, keepdims=True)
        at = pl.ds(pl.multiple_of(i * 32 + row, 16), 16)
        result = grad_mid[at, :] + inverse * (grad * gain[...] - normed * inner)
        input_grad[i, pl.ds(row, 16), :] = result.astype(bf16)

    own_chunks(chunk)
    spread_gains = []
    for k, (d, s) in enumerate(owners):
        at = pl.ds(pl.multiple_of((d * 8 + s) * 128, 128), 128)
        copy = remote(gains.at[:, :, at], gains_in.at[k], gain_sends, gain_recvs, k, {"dp": d, "seq": s})
        copy.start()
        spread_gains.append(copy)
    for copy in far:
        copy.wait()
    here = dp * 4 + x
    sums = weights[here, core].astype(f32) + near[here].astype(f32)
    for i in range(7):
        sums = sums + shares[i].astype(f32)
    share[...] = sums
    own = gains[:, :, pl.ds(pl.multiple_of((dp * 8 + seq) * 128, 128), 128)]
    for k, copy in enumerate(spread_gains):
        copy.wait()
        own = own + gains_in[k]
    gains_near[7] = own
    last = [
        remote(gains_near.at[7], gains_near.at[i], last_sends, last_recvs, i, {"tensor": peer})
        for i, peer in enumerate(peers)
    ]
    for copy in last:
        copy.start()
    for copy in last:
        copy.wait()
    z, y = tensor // 2, tensor % 2
    shifts = ((2, 1), (1, 1), (3, 1), (2, 0), (1, 0), (3, 0), (0, 1))
    sums = jnp.zeros_like(own)
    for t in range(8):
        slot = jnp.int32(7)
        for i, (dz, dy) in enumerate(shifts):
            source = ((z + 4 - dz) % 4) * 2 + (y + dy) % 2
            slot = jnp.where(source == t, i, slot)
        sums = sums + gains_near[slot]
    gain_sum[...] = jnp.sum(sums, axis=1)


def backward(
    branch, query, pairs, kept, mixed, packed, h_first, mlp_part, mid, tokens, grad_mid, gain,
    gain_two, cos_table, sin_table,
):
    count, rows, width = h_first.shape
    keys = pairs.shape[0] * rows
    pair_rows = (rows, 2 * HEAD_SIZE)
    dma = pltpu.SemaphoreType.DMA
    vmem = pltpu.VMEM
    return pl.pallas_call(
        backward_kernel,
        out_shape=(
            jax.ShapeDtypeStruct((count, 32, width), bf16),
            jax.ShapeDtypeStruct((count, 32, width), bf16),
            jax.ShapeDtypeStruct((128, 640), f32),
            jax.ShapeDtypeStruct((2, 128), f32),
        ),
        in_specs=[VMEM] * 7 + [ANY] + [VMEM] * 7,
        out_specs=(VMEM,) * 4,
        scratch_shapes=[
            vmem((count, rows, width), bf16),
            vmem((count, rows, width), bf16),
            vmem((7, count, 32, width), bf16),
            vmem((7, count * 32, width), bf16),
            vmem((count * 32, width), bf16),
            vmem((rows, GROUP * HEAD_SIZE), f32),
            vmem((count, rows, 384), bf16),
            vmem((4, 2, count) + pair_rows, bf16),
            vmem((count, 4) + pair_rows, bf16),
            vmem((count, 3) + pair_rows, bf16),
            vmem((count, 3) + pair_rows, bf16),
            vmem((rows, keys), f32),
            vmem((2 * HEAD_SIZE, keys), f32),
            vmem((8, 2, 128, 640), bf16),
            vmem((8, 128, 640), bf16),
            vmem((7, 128, 640), bf16),
            vmem((7, 128, 640), bf16),
            vmem((2, 8, width), f32),
            vmem((15, 2, 8, 128), f32),
            vmem((8, 2, 8, 128), f32),
            dma((21,)), dma((21,)), dma((7,)), dma((7,)), dma((21,)), dma((21,)),
            dma((3,)), dma((3,)), dma((9,)), dma((9,)), dma((1,)), dma((1,)), dma((7,)), dma((7,)),
            dma((15,)), dma((15,)), dma((7,)), dma((7,)), dma,
        ],
        compiler_params=params(7, 62),
        cost_estimate=pl.CostEstimate(flops=40000 * MIB, bytes_accessed=200 * MIB, transcendentals=0),
        name="backward",
    )(
        branch, query, pairs, kept, mixed, packed, h_first, mlp_part, mid, tokens, grad_mid, gain,
        gain_two, cos_table, sin_table,
    )


def shards(
    tokens,
    cotangent,
    query_weight,
    query_first,
    query_second,
    key_value_weight,
    key_value_first_moment,
    key_value_second_moment,
    output_weight,
    output_first,
    output_second,
    gate_up_weight,
    gate_up_first,
    gate_up_second,
    down_weight,
    down_first,
    down_second,
    norm_gains,
    gains_first,
    gains_second,
):
    count, local_len, width = tokens.shape
    token_count = count * local_len
    tensor = lax.axis_index("tensor")

    def own_rows(values):
        return lax.dynamic_slice_in_dim(values, tensor * 32, 32, 1)

    packed = jnp.concatenate(
        [
            query_weight,
            key_value_weight.reshape(128, 2 * HEAD_SIZE),
            output_weight.T,
            jnp.pad(norm_gains.T, ((0, 0), (0, 126))),
        ],
        axis=1,
    ).astype(bf16)
    packed_all = gather_rows(packed)
    units = down_weight.shape[0]
    ff_low = jnp.concatenate(
        [gate_up_weight[0], gate_up_weight[1], down_weight.T], axis=1
    ).astype(bf16)
    swap = [(0, 1), (1, 0)]
    ff_pair = jnp.stack([ff_low, lax.ppermute(ff_low, "dp", swap)])
    ff_all = lax.all_gather(ff_pair, "seq", axis=0, tiled=False)
    packed_all = packed_all.reshape(width, packed.shape[1])
    projection = packed_all[:, :384]
    output_all = packed_all[:, 384:640]
    gains_used = packed_all[:, 640:642].T.astype(f32)

    positions = lax.axis_index("seq") * local_len + jnp.arange(local_len, dtype=jnp.int32)
    cos_table, sin_table = rotary(positions)
    scale = HEAD_SIZE ** (-0.5)
    token_rows = tokens.astype(f32)
    inv_one = inverse_rms(token_rows)
    h_first = (token_rows * inv_one * gains_used[0]).astype(bf16).reshape(token_count, width)
    raw = jnp.dot(h_first, projection, preferred_element_type=f32)
    raw = raw.reshape(count, local_len, GROUP + 2, HEAD_SIZE)
    rotated = rotate(raw[:, :, : GROUP + 1], cos_table, sin_table).astype(bf16)
    query = (rotated[:, :, :GROUP] * bf16(scale)).transpose(0, 2, 1, 3)
    query = jnp.pad(query, ((0, 0), (0, 0), (0, 0), (0, HEAD_SIZE)))
    pair = jnp.concatenate([rotated[:, :, GROUP], raw[:, :, GROUP + 1].astype(bf16)], axis=-1)
    pairs = gather_pairs(pair)
    kept, mixed = attend(query, pairs)
    attn_term = nt(mixed.reshape(token_count, GROUP * HEAD_SIZE), output_all).astype(bf16).reshape(count, local_len, width)
    mid, h_second = middle(attn_term, own_rows(tokens), gains_used[1:])
    mid = mid.reshape(96, width)
    branch_own, grad_mid, gain_two, mlp_term, grads = feed_forward(
        h_second,
        cotangent.reshape(count, 8, 32, width),
        ff_all,
        mid,
        gains_used[1:],
    )
    shares_ff = lax.psum_scatter(grads, "seq", scatter_dimension=0, tiled=False)
    shares_far = lax.ppermute(shares_ff[1], "dp", swap)
    cos_wide = jnp.tile(cos_table[:, 0], (1, 4))
    sin_wide = jnp.tile(jnp.concatenate([sin_table[:, 0], -sin_table[:, 0]], axis=1), (1, 2))
    input_grad, block_out, share_projection, share_gains = backward(
        branch_own,
        query,
        pairs,
        kept,
        mixed,
        packed_all,
        h_first.reshape(count, local_len, width),
        mlp_term,
        mid,
        own_rows(tokens),
        grad_mid,
        gains_used[:1],
        gain_two,
        cos_wide,
        sin_wide,
    )

    query_new, query_first_new, query_second_new = adam(
        query_weight, share_projection[:, :256], query_first, query_second, rate_wide, weight_decay
    )
    pair_new, pair_first_new, pair_second_new = adam(
        key_value_weight,
        share_projection[:, None, 256:384],
        key_value_first_moment,
        key_value_second_moment,
        rate_wide,
        weight_decay,
    )
    output_new, output_first_new, output_second_new = adam(
        output_weight,
        share_projection[:, 384:].T,
        output_first,
        output_second,
        rate_output,
        weight_decay,
    )
    shares_ff = shares_ff[0].astype(f32) + shares_far.astype(f32)
    gate_up_new, gate_up_first_new, gate_up_second_new = adam(
        gate_up_weight,
        jnp.stack([shares_ff[:, :units], shares_ff[:, units : 2 * units]]),
        gate_up_first,
        gate_up_second,
        rate_wide,
        weight_decay,
    )
    down_new, down_first_new, down_second_new = adam(
        down_weight, shares_ff[:, 2 * units :].T, down_first, down_second, rate_down, weight_decay
    )
    gains_new, gains_first_new, gains_second_new = adam(
        norm_gains, share_gains, gains_first, gains_second, rate_gains, 0.0
    )
    return (
        block_out,
        input_grad,
        query_new,
        query_first_new,
        query_second_new,
        pair_new,
        pair_first_new,
        pair_second_new,
        output_new,
        output_first_new,
        output_second_new,
        gate_up_new,
        gate_up_first_new,
        gate_up_second_new,
        down_new,
        down_first_new,
        down_second_new,
        gains_new,
        gains_first_new,
        gains_second_new,
    )


def solution(mesh):
    return jax.shard_map(
        shards,
        mesh=mesh,
        in_specs=(
            P("dp", "seq", None),
            P("dp", "seq", None),
            P(("dp", "seq"), "tensor"),
            P(("dp", "seq"), "tensor"),
            P(("dp", "seq"), "tensor"),
            P(("dp", "seq"), "tensor", None),
            P(("dp", "seq"), "tensor", None),
            P(("dp", "seq"), "tensor", None),
            P("tensor", ("dp", "seq")),
            P("tensor", ("dp", "seq")),
            P("tensor", ("dp", "seq")),
            P(None, ("dp", "seq"), "tensor"),
            P(None, ("dp", "seq"), "tensor"),
            P(None, ("dp", "seq"), "tensor"),
            P("tensor", ("dp", "seq")),
            P("tensor", ("dp", "seq")),
            P("tensor", ("dp", "seq")),
            P(None, ("dp", "seq")),
            P(None, ("dp", "seq")),
            P(None, ("dp", "seq")),
        ),
        out_specs=(
            P("dp", ("seq", "tensor"), None),
            P("dp", ("seq", "tensor"), None),
            P(("dp", "seq"), "tensor"),
            P(("dp", "seq"), "tensor"),
            P(("dp", "seq"), "tensor"),
            P(("dp", "seq"), "tensor", None),
            P(("dp", "seq"), "tensor", None),
            P(("dp", "seq"), "tensor", None),
            P("tensor", ("dp", "seq")),
            P("tensor", ("dp", "seq")),
            P("tensor", ("dp", "seq")),
            P(None, ("dp", "seq"), "tensor"),
            P(None, ("dp", "seq"), "tensor"),
            P(None, ("dp", "seq"), "tensor"),
            P("tensor", ("dp", "seq")),
            P("tensor", ("dp", "seq")),
            P("tensor", ("dp", "seq")),
            P(None, ("dp", "seq")),
            P(None, ("dp", "seq")),
            P(None, ("dp", "seq")),
        ),
        check_vma=False,
    )
```

```python
import jax
import jax.numpy as jnp
from jax import lax
from jax.experimental import pallas as pl
from jax.experimental.pallas import tpu as pltpu
from jax.sharding import PartitionSpec as P

QUERY_HEADS = 32
KEY_VALUE_HEADS = 8
HEAD_SIZE = 64
STEP = 10
GROUP = QUERY_HEADS // KEY_VALUE_HEADS


norm_eps = 1e-05
rope_base = 500000.0
beta_first = 0.9
beta_second = 0.95
adam_eps = 1e-08
weight_decay = 0.1
rate_wide = 0.07
rate_down = 0.035
rate_output = 1.0
rate_gains = 0.7

bf16 = jnp.bfloat16
f32 = jnp.float32
MESH = pl.DeviceIdType.MESH
VMEM = pl.BlockSpec(memory_space=pltpu.VMEM)
ANY = pl.BlockSpec(memory_space=pl.ANY)
MIB = 1024 * 1024


def inverse_rms(values):
    return lax.rsqrt(jnp.mean(values * values, axis=-1, keepdims=True) + norm_eps)


def rotary(positions):
    half_size = HEAD_SIZE // 2
    freqs = rope_base ** (-2.0 * jnp.arange(half_size, dtype=jnp.float32) / HEAD_SIZE)
    angles = positions.astype(jnp.float32)[:, None] * freqs[None, :]
    return (jnp.cos(angles), jnp.sin(angles))


def adam(master, grad, moment_one, moment_two, rate, decay):
    new_one = beta_first * moment_one + (1.0 - beta_first) * grad
    new_two = beta_second * moment_two + (1.0 - beta_second) * grad * grad
    ahead = (
        new_one
        / (1.0 - beta_first**STEP)
        / (jnp.sqrt(new_two / (1.0 - beta_second**STEP)) + adam_eps)
    )
    return (master - rate * (ahead + decay * master), new_one, new_two)


def tensor_peers():
    me = lax.axis_index("tensor")
    z, y = me // 2, me % 2
    return [
        ((z + dz) % 4) * 2 + (y + dy) % 2
        for dz, dy in ((2, 1), (1, 1), (3, 1), (2, 0), (1, 0), (3, 0), (0, 1))
    ]


def chip_peers():
    dp, seq = lax.axis_index("dp"), lax.axis_index("seq")
    x, core = seq // 2, seq % 2
    return [
        ((dp + dd) % 2, (x + dx) % 4, core)
        for dx, dd in ((2, 1), (1, 1), (3, 1), (0, 1), (2, 0), (1, 0), (3, 0))
    ]


def row_peers():
    seq = lax.axis_index("seq")
    x, core = seq // 2, seq % 2
    return [((x + dx) % 4, core) for dx in (2, 1, 3)]


def sibling():
    seq = lax.axis_index("seq")
    return seq + 1 - 2 * (seq % 2)


def greet(devices):
    barrier = pltpu.get_barrier_semaphore()
    for device in devices:
        pl.semaphore_signal(barrier, inc=1, device_id=device, device_id_type=MESH)
    pl.semaphore_wait(barrier, len(devices))


def remote(src, dst, sends, recvs, at, device):
    return pltpu.make_async_remote_copy(src, dst, sends.at[at], recvs.at[at], device, MESH)


def params(collective_id, mib):
    return pltpu.CompilerParams(
        collective_id=collective_id, has_side_effects=True, vmem_limit_bytes=mib * MIB
    )


def causal_bias(bias):
    seq = lax.axis_index("seq")
    rows, keys = bias.shape
    row = lax.broadcasted_iota(jnp.int32, (rows, keys), 0) + seq * rows
    key = lax.broadcasted_iota(jnp.int32, (rows, keys), 1)
    bias[...] = jnp.where(key <= row, 0.0, -1e30).astype(f32)


def nt(left, right):
    return lax.dot_general(left, right, (((1,), (1,)), ((), ())), preferred_element_type=f32)


def tn(left, right):
    return lax.dot_general(left, right, (((0,), (0,)), ((), ())), preferred_element_type=f32)


def columns(tile, size):
    return pl.ds(pl.multiple_of(tile * size, size), size)


def turn(values, cos_table, sin_table):
    lane = lax.broadcasted_iota(jnp.int32, values.shape, 1)
    half = HEAD_SIZE // 2
    other = jnp.where(
        lane % HEAD_SIZE < half,
        pltpu.roll(values, values.shape[1] - half, 1),
        pltpu.roll(values, half, 1),
    )
    return values * cos_table + other * sin_table


def block_of(peer):
    return pl.ds(pl.multiple_of(peer * 32, 32), 32)


def scatter_start(part, landed, sends, recvs):
    out = [
        remote(part.at[:, block_of(peer), :], landed.at[i], sends, recvs, i, {"tensor": peer})
        for i, peer in enumerate(tensor_peers())
    ]
    for copy in out:
        copy.start()
    return out


def owned_sum(part, landed, i, row):
    tensor = lax.axis_index("tensor")
    total = part[i, pl.ds(pl.multiple_of(tensor * 32 + row, 16), 16), :].astype(f32)
    for j in range(7):
        total = total + landed[j, i, pl.ds(row, 16), :].astype(f32)
    return total


def own_chunks(body):
    def step(k, carry):
        body(k // 2, pl.multiple_of((k % 2) * 16, 16))
        return carry

    lax.fori_loop(0, 6, step, 0)


class Weights:
    def __init__(self, mine, whole, sends, recvs, near_sends, near_recvs):
        self.dp, self.seq = lax.axis_index("dp"), lax.axis_index("seq")
        self.mine, self.whole = mine, whole
        self.sends, self.recvs = sends, recvs
        self.near_sends, self.near_recvs = near_sends, near_recvs
        self.started, self.passed = {}, []

    def owner(self, dx, dd):
        x, core = self.seq // 2, self.seq % 2
        return (self.dp + dd) % 2, ((x + dx) % 4) * 2 + core

    def device(self, dx, dd):
        dp, seq = self.owner(dx, dd)
        return {"dp": dp, "seq": seq}

    def view(self, dx, dd, half=None):
        ref = self.whole.at[self.owner(dx, dd)]
        return ref if half is None else ref.at[pl.ds(64 * half, 64)]

    def send(self, k, block, to, half=None):
        place = self.view(*block, half)
        source = place
        if block == (0, 0):
            source = self.mine if half is None else self.mine.at[pl.ds(64 * half, 64)]
        copy = remote(source, place, self.sends, self.recvs, k, self.device(*to))
        copy.start()
        self.started[k] = copy

    def beside(self, k, block, half=None):
        place = self.view(*block, half)
        source = self.mine if block == (0, 0) else place
        copy = remote(source, place, self.near_sends, self.near_recvs, k, {"seq": sibling()})
        copy.start()
        self.passed.append(copy)

    def start(self):
        self.send(0, (0, 0), (0, 1))
        self.send(1, (0, 0), (1, 0), 0)
        self.send(2, (0, 0), (3, 0), 0)
        self.beside(0, (0, 0))

    def rest(self):
        self.send(3, (0, 0), (1, 0), 1)
        self.send(4, (0, 0), (3, 0), 1)

    def partner(self):
        self.started[0].wait_recv()
        self.send(5, (0, 1), (1, 0))
        self.send(6, (0, 1), (3, 0))
        self.beside(1, (0, 1))

    def own_ring(self):
        self.started[1].wait_recv()
        self.send(7, (3, 0), (1, 0), 0)
        self.started[4].wait_recv()
        self.send(8, (1, 0), (3, 0), 1)
        self.started[3].wait_recv()
        self.beside(2, (3, 0))
        self.started[2].wait_recv()
        self.beside(3, (1, 0))

    def partner_ring(self):
        self.started[5].wait_recv()
        self.send(9, (3, 1), (1, 0), 0)
        self.beside(4, (3, 1))
        self.started[6].wait_recv()
        self.send(10, (1, 1), (3, 0), 1)
        self.beside(5, (1, 1))

    def finish(self):
        for k, half, dd in ((7, 0, 0), (8, 1, 0), (9, 0, 1), (10, 1, 1)):
            self.started[k].wait_recv()
            self.beside(k - 1, (2, dd), half)
        for copy in self.started.values():
            copy.wait_send()
        for copy in self.passed:
            copy.wait()


def forward_kernel(
    tokens, mine, gains_mine, ff_mine, cos_table, sin_table,
    query, pairs, kept, mixed, packed, h_first, mid, h_second, ff_all, gains,
    part, landed, bias,
    sends, recvs, near_sends, near_recvs, gain_sends, gain_recvs, pair_sends, pair_recvs,
    pair_near_sends, pair_near_recvs, out_sends, out_recvs, ff_sends, ff_recvs, ff_near_sends,
    ff_near_recvs, local,
):
    dp, seq, tensor = lax.axis_index("dp"), lax.axis_index("seq"), lax.axis_index("tensor")
    me = dp * 8 + seq
    count, rows, width = tokens.shape
    keys = bias.shape[1]
    near = {"seq": sibling()}
    owners = [((dp + k // 8) % 2, (seq + k % 8) % 8) for k in range(1, 16)]
    greet(
        [{"tensor": peer} for peer in tensor_peers()] + [{"dp": d, "seq": s} for d, s in owners]
    )
    gain_at = pl.ds(pl.multiple_of(me * 128, 128), 128)
    gain_copies = [
        remote(gains_mine, gains.at[:, gain_at], gain_sends, gain_recvs, k, {"dp": d, "seq": s})
        for k, (d, s) in enumerate(owners)
    ]
    for copy in gain_copies:
        copy.start()
    out = [
        remote(mine, packed.at[me], sends, recvs, i, {"dp": d, "seq": 2 * x + c})
        for i, (d, x, c) in enumerate(chip_peers())
    ]
    for copy in out:
        copy.start()
    first = remote(mine, packed.at[me], near_sends, near_recvs, 7, near)
    first.start()
    ff = Weights(ff_mine, ff_all, ff_sends, ff_recvs, ff_near_sends, ff_near_recvs)
    ff.start()
    store_ff = pltpu.make_async_copy(ff_mine, ff_all.at[dp, seq], local)
    store_ff.start()
    packed[me] = mine[...]
    gains[:, gain_at] = gains_mine[...]
    causal_bias(bias)
    for copy in gain_copies:
        copy.wait()

    def normalize(k, carry):
        i = k // 16
        at = pl.ds(pl.multiple_of((k % 16) * 16, 16), 16)
        token_rows = tokens[i, at, :].astype(f32)
        h_first[i, at, :] = (token_rows * inverse_rms(token_rows) * gains[0:1, :]).astype(bf16)
        return carry

    lax.fori_loop(0, count * 16, normalize, 0)
    passed = []
    for i, (dd, dx) in (
        (6, (0, 1)), (5, (0, 3)), (3, (1, 0)), (4, (0, 2)), (2, (1, 1)), (1, (1, 3)), (0, (1, 2)),
    ):
        out[i].wait_recv()
        owner = (((dp + dd) % 2) * 4 + (seq // 2 + dx) % 4) * 2 + seq % 2
        forward = remote(packed.at[owner], packed.at[owner], near_sends, near_recvs, i, near)
        forward.start()
        passed.append(forward)
    first.wait()
    for copy in passed:
        copy.wait()
    scale = HEAD_SIZE ** (-0.5)
    lane = lax.broadcasted_iota(jnp.int32, (rows, 2 * HEAD_SIZE), 1)

    def project(i, carry):
        raw = jnp.dot(
            h_first[i], packed[:, :, :384].reshape(width, 384), preferred_element_type=f32
        )
        for at in range(GROUP // 2):
            both = raw[:, at * 2 * HEAD_SIZE : (at + 1) * 2 * HEAD_SIZE]
            both = turn(both, cos_table[...], -sin_table[...]) * scale
            query[i, 2 * at] = jnp.where(lane < HEAD_SIZE, both, 0.0).astype(bf16)
            moved = pltpu.roll(both, HEAD_SIZE, 1)
            query[i, 2 * at + 1] = jnp.where(lane < HEAD_SIZE, moved, 0.0).astype(bf16)
        pair = raw[:, GROUP * HEAD_SIZE :]
        turned = turn(pair, cos_table[...], -sin_table[...])
        pairs[seq, i] = jnp.where(lane < HEAD_SIZE, turned, pair).astype(bf16)
        return carry

    lax.fori_loop(0, count, project, 0)
    pair_out = [
        remote(pairs.at[seq], pairs.at[seq], pair_sends, pair_recvs, i, {"seq": 2 * x + c})
        for i, (x, c) in enumerate(row_peers())
    ]
    for copy in pair_out:
        copy.start()
    pair_first = remote(pairs.at[seq], pairs.at[seq], pair_near_sends, pair_near_recvs, 3, near)
    pair_first.start()
    ff.rest()
    pair_passed = []
    for i, dx in ((1, 3), (2, 1), (0, 2)):
        pair_out[i].wait_recv()
        owner = ((seq // 2 + dx) % 4) * 2 + seq % 2
        forward = remote(
            pairs.at[owner], pairs.at[owner], pair_near_sends, pair_near_recvs, i, near
        )
        forward.start()
        pair_passed.append(forward)
    pair_first.wait()
    for copy in pair_passed:
        copy.wait()
    ff.partner()

    def attend(i):
        upper = []
        pair = pairs[:, i].reshape(keys, 2 * HEAD_SIZE)
        for head in range(GROUP):
            scores = nt(query[i, head], pair) + bias[...]
            row_max = jnp.max(scores, axis=-1, keepdims=True)
            exps = jnp.exp(scores - row_max)
            row_sum = jnp.sum(exps, axis=-1, keepdims=True)
            mix = jnp.dot(exps.astype(bf16), pair, preferred_element_type=f32) / row_sum
            kept[i, head] = jnp.where(lane < HEAD_SIZE, row_max + jnp.log(row_sum), mix)
            upper.append(mix)
        for at in range(GROUP // 2):
            low = pltpu.roll(upper[2 * at], HEAD_SIZE, 1)
            both = jnp.where(lane < HEAD_SIZE, low, upper[2 * at + 1])
            mixed[i, :, at * 2 * HEAD_SIZE : (at + 1) * 2 * HEAD_SIZE] = both.astype(bf16)

    def attend_step(i, carry):
        attend(i)

        def term(tile, inner_carry):
            weight_rows = packed[pl.ds(tile * 4, 4), :, 384:640].reshape(512, 256)
            part[i, :, columns(tile, 512)] = nt(mixed[i], weight_rows).astype(bf16)
            return inner_carry

        lax.fori_loop(0, width // 512, term, 0)
        return carry

    back = []
    for i in range(count):
        lax.fori_loop(i, i + 1, attend_step, 0)
        for k, peer in enumerate(tensor_peers()):
            copy = remote(
                part.at[i, block_of(peer)], landed.at[k, i], out_sends, out_recvs, 7 * i + k,
                {"tensor": peer},
            )
            copy.start()
            back.append(copy)
    ff.own_ring()
    ff.partner_ring()
    for copy in back:
        copy.wait()

    def chunk(i, row):
        at = pl.ds(pl.multiple_of(tensor * 32 + row, 16), 16)
        result = owned_sum(part, landed, i, row) + tokens[i, at, :].astype(f32)
        at = pl.ds(pl.multiple_of(i * 32 + row, 16), 16)
        mid[at, :] = result
        h_second[at, :] = (result * inverse_rms(result) * gains[1:2, :]).astype(bf16)

    own_chunks(chunk)
    for copy in out + pair_out:
        copy.wait_send()
    store_ff.wait()
    ff.finish()


def forward(tokens, mine, gains_mine, ff_mine, cos_table, sin_table):
    count, rows, width = tokens.shape
    dma = pltpu.SemaphoreType.DMA
    lanes = 2 * HEAD_SIZE
    return pl.pallas_call(
        forward_kernel,
        out_shape=(
            jax.ShapeDtypeStruct((count, GROUP, rows, lanes), bf16),
            jax.ShapeDtypeStruct((8, count, rows, lanes), bf16),
            jax.ShapeDtypeStruct((count, GROUP, rows, lanes), f32),
            jax.ShapeDtypeStruct((count, rows, GROUP * HEAD_SIZE), bf16),
            jax.ShapeDtypeStruct((16,) + mine.shape, bf16),
            jax.ShapeDtypeStruct((count, rows, width), bf16),
            jax.ShapeDtypeStruct((count * 32, width), f32),
            jax.ShapeDtypeStruct((count * 32, width), bf16),
            jax.ShapeDtypeStruct((2, 8) + ff_mine.shape, bf16),
            jax.ShapeDtypeStruct((8, width), f32),
        ),
        in_specs=[VMEM] * 6,
        out_specs=(VMEM,) * 8 + (ANY, VMEM),
        scratch_shapes=[
            pltpu.VMEM((count, rows, width), bf16),
            pltpu.VMEM((7, count, 32, width), bf16),
            pltpu.VMEM((rows, 8 * rows), f32),
            dma((7,)), dma((7,)), dma((8,)), dma((8,)), dma((15,)), dma((15,)), dma((3,)), dma((3,)),
            dma((4,)), dma((4,)), dma((21,)), dma((21,)), dma((11,)), dma((11,)), dma((10,)),
            dma((10,)), dma,
        ],
        compiler_params=params(1, 60),
        cost_estimate=pl.CostEstimate(flops=40000 * MIB, bytes_accessed=200 * MIB, transcendentals=0),
        name="forward",
    )(tokens, mine, gains_mine, ff_mine, cos_table, sin_table)


class Spread:
    def __init__(self, buffer, sends, recvs):
        tensor = lax.axis_index("tensor")
        self.buffer, self.sends, self.recvs = buffer, sends, recvs
        self.z, self.y = tensor // 2, tensor % 2
        self.started = {}

    def at(self, dz, dy):
        return ((self.z + dz) % 4) * 2 + (self.y + dy) % 2

    def send(self, k, block, to, half=None):
        ref = self.buffer.at[block]
        if half is not None:
            rows = self.buffer.shape[1] // 2
            ref = self.buffer.at[block, pl.ds(half * rows, rows)]
        copy = remote(ref, ref, self.sends, self.recvs, k, {"tensor": to})
        copy.start()
        self.started[k] = copy

    def start(self):
        mine = self.at(0, 0)
        self.send(0, mine, self.at(0, 1))
        self.send(1, mine, self.at(1, 0))
        self.send(2, mine, self.at(3, 0))

    def pass_partner(self):
        self.started[0].wait_recv()
        self.send(3, self.at(0, 1), self.at(1, 0))
        self.send(4, self.at(0, 1), self.at(3, 0))

    def pass_on(self, dy):
        k = 1 + 2 * dy
        self.started[k].wait_recv()
        self.send(5 + 2 * dy, self.at(3, dy), self.at(1, 0), 0)
        self.started[k + 1].wait_recv()
        self.send(6 + 2 * dy, self.at(1, dy), self.at(3, 0), 1)

    def finish(self):
        for k in range(5, 9):
            self.started[k].wait_recv()

    def drain(self):
        for copy in self.started.values():
            copy.wait_send()


def spread_peers():
    tensor = lax.axis_index("tensor")
    z, y = tensor // 2, tensor % 2
    return [((z + dz) % 4) * 2 + (y + dy) % 2 for dz, dy in ((0, 1), (1, 0), (3, 0))]


def feed_forward_kernel(
    own, cotangent, weights, mid, gain,
    branch, grad_mid, grad_gain, mlp_out, grads_out,
    gate_up, down, cot, normed, grad_hidden, grad_units, hidden, second, landed, mlp, grads,
    sends, recvs, back_sends, back_recvs, local, cot_sems, out_sems, mlp_sem,
):
    tensor = lax.axis_index("tensor")
    units = down.shape[3]
    width = 16 * 128
    dp = lax.axis_index("dp")
    load_down = pltpu.make_async_copy(
        weights.at[:, :, :, pl.ds(2 * units, units)], down, local.at[0]
    )
    load_gate_up = pltpu.make_async_copy(
        weights.at[:, :, :, pl.ds(0, 2 * units)], gate_up, local.at[1]
    )
    load_down.start()
    load_cot = [
        pltpu.make_async_copy(cotangent.at[:, t], cot.at[t], cot_sems.at[t]) for t in range(8)
    ]
    for copy in load_cot:
        copy.start()
    load_gate_up.start()
    greet([{"tensor": peer} for peer in tensor_peers()])
    normed[tensor] = own[...]
    spread = Spread(normed, sends, recvs)
    spread.start()
    for copy in load_cot:
        copy.wait()
    load_down.wait()

    def hidden_step(tile, carry):
        at = columns(tile, 256)
        product = jnp.dot(
            cot[...].reshape(8 * 96, width),
            down[:, :, :, at].reshape(width, 256),
            preferred_element_type=f32,
        )
        grad_hidden[:, :, at] = product.reshape(8, 96, 256)
        return carry

    lax.fori_loop(0, units // 256, hidden_step, 0)
    load_gate_up.wait()

    back = {}

    def block(dz):
        first = ((spread.z + dz) % 4) * 2
        both = pl.ds(first, 2)

        def units_step(tile, carry):
            at = columns(tile, 256)
            up_at = pl.ds(pl.multiple_of(units + tile * 256, 256), 256)
            rows = normed[both].reshape(192, width)
            gate_columns = gate_up[:, :, :, at].reshape(width, 256)
            up_columns = gate_up[:, :, :, up_at].reshape(width, 256)
            gate_in = jnp.dot(rows, gate_columns, preferred_element_type=f32)
            up_in = jnp.dot(rows, up_columns, preferred_element_type=f32)
            grad = grad_hidden[both, :, at].reshape(192, 256)
            sigmoid = jax.nn.sigmoid(gate_in)
            silu = gate_in * sigmoid
            hidden[both, :, at] = (silu * up_in).astype(bf16).reshape(2, 96, 256)
            grad_gate = grad * up_in * sigmoid * (1.0 + gate_in * (1.0 - sigmoid))
            grad_units[both, :, at] = grad_gate.astype(bf16).reshape(2, 96, 256)
            grad_units[both, :, up_at] = (grad * silu).astype(bf16).reshape(2, 96, 256)
            return carry

        lax.fori_loop(0, units // 256, units_step, 0)

        def second_step(tile, carry):
            at = columns(tile, 512)
            rows = grad_units[both].reshape(192, 2 * units)
            weight_rows = gate_up[tile // 2, pl.ds((tile % 2) * 4, 4)].reshape(512, 2 * units)
            second[both, :, at] = nt(rows, weight_rows).astype(bf16).reshape(2, 96, 512)
            return carry

        lax.fori_loop(0, width // 512, second_step, 0)
        for dy in (1, 0):
            if (dz, dy) != (0, 0):
                to = spread.at(dz, dy)
                k = 2 * dz + dy - 1
                copy = remote(
                    second.at[to], landed.at[k], back_sends, back_recvs, k, {"tensor": to}
                )
                copy.start()
                back[k] = copy

    spread.pass_partner()
    spread.pass_on(0)
    block(0)
    spread.pass_on(1)
    block(1)
    block(3)
    spread.finish()
    block(2)

    def mlp_step(tile, carry):
        at = columns(tile, 256)
        rows = hidden[...].reshape(8 * 96, units)
        weight_rows = down[tile // 4, pl.ds((tile % 4) * 2, 2)].reshape(256, units)
        mlp[:, :, at] = nt(rows, weight_rows).astype(bf16).reshape(8, 96, 256)
        return carry

    lax.fori_loop(0, width // 256, mlp_step, 0)
    store_mlp = pltpu.make_async_copy(mlp, mlp_out, mlp_sem)
    store_mlp.start()

    def store(tile, slot):
        place = grads_out.at[pl.ds((tile % 4) * 2, 2), (tile // 4 + dp) % 2]
        return pltpu.make_async_copy(grads.at[slot], place, out_sems.at[slot])

    def grads_pair(pair, carry):
        for slot in range(2):
            tile = 2 * pair + slot
            at = columns(tile, 256)

            @pl.when(pair > 0)
            def _():
                store(tile - 2, slot).wait()

            wide = tn(
                normed[:, :, at].reshape(8 * 96, 256), grad_units[...].reshape(8 * 96, 2 * units)
            )
            grads[slot, :, :, : 2 * units] = wide.astype(bf16).reshape(2, 128, 2 * units)
            narrow = tn(cot[:, :, :, at].reshape(8 * 96, 256), hidden[...].reshape(8 * 96, units))
            grads[slot, :, :, 2 * units :] = narrow.astype(bf16).reshape(2, 128, units)
            store(tile, slot).start()
        return carry

    tiles = width // 256
    lax.fori_loop(0, tiles // 2, grads_pair, 0)
    for slot in range(2):
        store(tiles - 2 + slot, slot).wait()
    store_mlp.wait()
    spread.drain()
    for copy in back.values():
        copy.wait()
    grad_gain[...] = jnp.zeros_like(grad_gain)

    def chunk(k, carry):
        at = pl.ds(pl.multiple_of(k * 16, 16), 16)
        grad = second[tensor, at, :].astype(f32)
        for j in range(7):
            grad = grad + landed[j, at, :].astype(f32)
        rows = mid[at, :]
        inverse = inverse_rms(rows)
        normed_rows = rows * inverse
        product = grad * normed_rows
        grad_gain[...] += product[:8] + product[8:]
        inner = jnp.mean(product * gain[...], axis=-1, keepdims=True)
        own_cot = cot[tensor, k // 2, pl.ds(pl.multiple_of((k % 2) * 16, 16), 16), :].astype(f32)
        result = own_cot + inverse * (grad * gain[...] - normed_rows * inner)
        grad_mid[at, :] = result
        branch[at, :] = result.astype(bf16)
        return carry

    lax.fori_loop(0, 6, chunk, 0)


def feed_forward(own, cotangent, weights, mid, gain):
    rows, width = mid.shape
    units = weights.shape[3] // 3
    dma = pltpu.SemaphoreType.DMA
    return pl.pallas_call(
        feed_forward_kernel,
        out_shape=(
            jax.ShapeDtypeStruct((rows, width), bf16),
            jax.ShapeDtypeStruct((rows, width), f32),
            jax.ShapeDtypeStruct((8, width), f32),
            jax.ShapeDtypeStruct((8, rows, width), bf16),
            jax.ShapeDtypeStruct((8, 2) + weights.shape[2:], bf16),
        ),
        in_specs=[VMEM, ANY, ANY, VMEM, VMEM],
        out_specs=(VMEM, VMEM, VMEM, ANY, ANY),
        scratch_shapes=[
            pltpu.VMEM((2, 8, 128, 2 * units), bf16),
            pltpu.VMEM((2, 8, 128, units), bf16),
            pltpu.VMEM((8, 3, 32, width), bf16),
            pltpu.VMEM((8, rows, width), bf16),
            pltpu.VMEM((8, rows, units), f32),
            pltpu.VMEM((8, rows, 2 * units), bf16),
            pltpu.VMEM((8, rows, units), bf16),
            pltpu.VMEM((8, rows, width), bf16),
            pltpu.VMEM((7, rows, width), bf16),
            pltpu.VMEM((8, rows, width), bf16),
            pltpu.VMEM((2, 2, 128, 3 * units), bf16),
            dma((9,)), dma((9,)), dma((7,)), dma((7,)), dma((2,)), dma((8,)), dma((2,)), dma,
        ],
        compiler_params=params(5, 60),
        cost_estimate=pl.CostEstimate(
            flops=18 * 8 * rows * width * units, bytes_accessed=120 * MIB, transcendentals=0
        ),
        name="feed_forward",
    )(own, cotangent, weights, mid, gain)


def backward_kernel(
    branch, query_hbm, pairs_hbm, kept_hbm, mixed_hbm, packed_hbm, first_hbm, mlp_part, mid_hbm,
    cos_table, sin_table,
    part, ready, block_out,
    query, pairs, kept, mixed, packed, h_first, mid,
    whole, attended, raw, grad_pairs, near_pairs, ready_pairs, landed_pairs, bias, total, weights,
    near, mlp_own, mlp_landed, mlp_partner, mlp_last,
    out_sends, out_recvs, pair_near_sends, pair_near_recvs, pair_sends, pair_recvs, near_sends,
    near_recvs, mlp_sends, mlp_recvs, last_sends, last_recvs, local,
):
    dp, seq, tensor = lax.axis_index("dp"), lax.axis_index("seq"), lax.axis_index("tensor")
    x, core = seq // 2, seq % 2
    peers = tensor_peers()
    rows_beside = row_peers()
    beside = {"seq": sibling()}
    z, y = tensor // 2, tensor % 2
    count, width = whole.shape[0], whole.shape[2]
    rows, keys = bias.shape
    loads = [
        pltpu.make_async_copy(source, place, local.at[k])
        for k, (source, place) in enumerate(
            (
                (packed_hbm, packed),
                (pairs_hbm, pairs),
                (query_hbm, query),
                (kept_hbm, kept),
                (mixed_hbm, mixed),
                (first_hbm, h_first),
                (mid_hbm, mid),
                (mlp_part.at[pl.ds(2 * z, 2)], mlp_own),
            )
        )
    ]
    for copy in loads:
        copy.start()
    greet(
        [{"tensor": peer} for peer in peers]
        + [{"seq": 2 * px + c} for px, c in rows_beside]
        + [beside]
    )
    mine = pl.ds(pl.multiple_of(tensor * 32, 32), 32)
    spread = [
        remote(
            branch.at[pl.ds(32 * i, 32)], whole.at[i, mine], out_sends, out_recvs, 7 * i + k,
            {"tensor": peer},
        )
        for i in range(count)
        for k, peer in enumerate(peers)
    ]
    for copy in spread:
        copy.start()
    mlp = []
    for k, dz in enumerate((2, 1, 3)):
        other = (z + dz) % 4
        copy = remote(
            mlp_part.at[pl.ds(2 * other, 2)], mlp_landed.at[k], mlp_sends, mlp_recvs, k,
            {"tensor": 2 * other + y},
        )
        copy.start()
        mlp.append(copy)
    for i in range(count):
        whole[i, mine, :] = branch[32 * i : 32 * i + 32, :]
    causal_bias(bias)
    for copy in loads:
        copy.wait()
    lane = lax.broadcasted_iota(jnp.int32, (rows, 2 * HEAD_SIZE), 1)
    scale = HEAD_SIZE ** (-0.5)

    def sequence(i):
        for copy in spread[7 * i : 7 * i + 7]:
            copy.wait_recv()
        attended[...] = (
            jnp.dot(
                whole[i], packed[:, :, 384:640].reshape(width, 256), preferred_element_type=f32
            )
            .astype(bf16)
            .astype(f32)
        )
        total[...] = jnp.zeros_like(total)

        def head_pair(at, carry):
            columns_at = columns(at, 2 * HEAD_SIZE)
            grads_here = attended[:, columns_at]
            grad_query = []
            for odd in range(2):
                pair = pairs[:, i].reshape(keys, 2 * HEAD_SIZE)
                placed = grads_here if odd else pltpu.roll(grads_here, HEAD_SIZE, 1)
                placed = jnp.where(lane >= HEAD_SIZE, placed, 0.0)
                grad_rows = placed.astype(bf16)
                query_rows = query[i, 2 * at + odd]
                kept_rows = kept[i, 2 * at + odd]
                probs = jnp.exp(nt(query_rows, pair) + bias[...] - kept_rows[:, :1])
                inner = jnp.sum(kept_rows * placed, axis=-1, keepdims=True)
                grad_scores = (probs * (nt(grad_rows, pair) - inner)).astype(bf16)
                grad_query.append(jnp.dot(grad_scores, pair, preferred_element_type=f32))
                total[...] += jnp.dot(
                    query_rows.T, grad_scores, preferred_element_type=f32
                ) + jnp.dot(grad_rows.T, probs.astype(bf16), preferred_element_type=f32)
            both = jnp.where(lane < HEAD_SIZE, grad_query[0], pltpu.roll(grad_query[1], HEAD_SIZE, 1))
            both = turn(both * scale, cos_table[...], sin_table[...])
            raw[i, :, columns_at] = both.astype(bf16)
            return carry

        lax.fori_loop(0, GROUP // 2, head_pair, 0)
        for block in range(8):
            grad_pairs[block // 2, block % 2, i] = (
                total[:, block * rows : (block + 1) * rows].T.astype(bf16)
            )

    def cross(i):
        copy = remote(
            grad_pairs.at[:, 1 - core, i], near_pairs.at[i], pair_near_sends, pair_near_recvs, i,
            beside,
        )
        copy.start()
        return copy

    def onward(i, crossing):
        crossing.wait()
        out = []
        for k, (px, c) in enumerate(rows_beside):
            both = grad_pairs[px, core, i].astype(f32) + near_pairs[i, px].astype(f32)
            ready_pairs[i, k] = both.astype(bf16)
            copy = remote(
                ready_pairs.at[i, k], landed_pairs.at[i, k], pair_sends, pair_recvs, 3 * i + k,
                {"seq": 2 * px + c},
            )
            copy.start()
            out.append(copy)
        return out

    def settle(i, moving):
        mine_pairs = grad_pairs[x, core, i].astype(f32) + near_pairs[i, x].astype(f32)
        for k, copy in enumerate(moving):
            copy.wait()
            mine_pairs = mine_pairs + landed_pairs[i, k].astype(f32)
        turned = turn(mine_pairs, cos_table[...], sin_table[...])
        raw[i, :, 256:] = jnp.where(lane < HEAD_SIZE, turned, mine_pairs).astype(bf16)

        def term(tile, carry):
            at = columns(tile, 512)
            weight_rows = packed[pl.ds(tile * 4, 4), :, :384].reshape(512, 384)
            part[i, :, at] = nt(raw[i], weight_rows).astype(bf16)
            return carry

        lax.fori_loop(0, width // 512, term, 0)

    def outer(tile, carry):
        at = columns(tile, 256)
        product = tn(
            whole[:, :, at].reshape(count * rows, 256), mixed[...].reshape(count * rows, 256)
        )
        weights[tile, :, :, 256:512] = product.astype(bf16).reshape(2, 128, 256)
        return carry

    def query_weights(tile, carry):
        at = columns(tile, 256)
        product = tn(
            h_first[:, :, at].reshape(count * rows, 256), raw[:, :, :256].reshape(count * rows, 256)
        )
        weights[tile, :, :, :256] = product.astype(bf16).reshape(2, 128, 256)
        return carry

    def pair_weights(tile, carry):
        at = columns(tile, 512)
        product = tn(
            h_first[:, :, at].reshape(count * rows, 512), raw[:, :, 256:].reshape(count * rows, 128)
        )
        weights[pl.ds(2 * tile, 2), :, :, 512:] = product.astype(bf16).reshape(2, 2, 128, 128)
        return carry

    sequence(0)
    crossing = cross(0)
    sequence(1)
    moving = onward(0, crossing)
    crossing = cross(1)
    settle(0, moving)
    sequence(2)
    crossing_last = cross(2)
    moving = onward(1, crossing)
    lax.fori_loop(0, width // 256, outer, 0)
    moving_last = onward(2, crossing_last)
    settle(1, moving)
    lax.fori_loop(0, width // 256, query_weights, 0)
    settle(2, moving_last)
    lax.fori_loop(0, width // 512, pair_weights, 0)
    across = remote(weights.at[:, 1 - core], near, near_sends, near_recvs, 0, beside)
    across.start()
    for copy in spread:
        copy.wait_send()
    for copy in mlp:
        copy.wait()

    def partner_rows(k, carry):
        at = pl.ds(pl.multiple_of(k * 16, 16), 16)
        result = mlp_own[1 - y, at, :].astype(f32)
        for j in range(3):
            result = result + mlp_landed[j, 1 - y, at, :].astype(f32)
        mlp_partner[at, :] = result.astype(bf16)
        return carry

    lax.fori_loop(0, 6, partner_rows, 0)
    last = remote(mlp_partner, mlp_last, last_sends, last_recvs, 0, {"tensor": 2 * z + 1 - y})
    last.start()
    across.wait()
    for at in range(8):
        ready[at] = (weights[at, core].astype(f32) + near[at].astype(f32)).astype(bf16)
    last.wait()

    def finish_rows(i, row):
        at = pl.ds(pl.multiple_of(i * 32 + row, 16), 16)
        result = mid[at, :] + mlp_own[y, at, :].astype(f32) + mlp_last[at, :].astype(f32)
        for j in range(3):
            result = result + mlp_landed[j, y, at, :].astype(f32)
        block_out[i, pl.ds(row, 16), :] = result.astype(bf16)

    own_chunks(finish_rows)


def backward(
    branch, query, pairs, kept, mixed, packed, h_first, mlp_part, mid, cos_table, sin_table
):
    count, rows, width = h_first.shape
    keys = pairs.shape[0] * rows
    pair_rows = (rows, 2 * HEAD_SIZE)
    own = mid.shape[0]
    dma = pltpu.SemaphoreType.DMA
    vmem = pltpu.VMEM
    return pl.pallas_call(
        backward_kernel,
        out_shape=(
            jax.ShapeDtypeStruct((count, rows, width), bf16),
            jax.ShapeDtypeStruct((8, 128, 640), bf16),
            jax.ShapeDtypeStruct((count, 32, width), bf16),
        ),
        in_specs=[VMEM] + [ANY] * 8 + [VMEM] * 2,
        out_specs=(VMEM,) * 3,
        scratch_shapes=[
            vmem(query.shape, bf16),
            vmem(pairs.shape, bf16),
            vmem(kept.shape, f32),
            vmem(mixed.shape, bf16),
            vmem(packed.shape, bf16),
            vmem(h_first.shape, bf16),
            vmem(mid.shape, f32),
            vmem((count, rows, width), bf16),
            vmem((rows, GROUP * HEAD_SIZE), f32),
            vmem((count, rows, 384), bf16),
            vmem((4, 2, count) + pair_rows, bf16),
            vmem((count, 4) + pair_rows, bf16),
            vmem((count, 3) + pair_rows, bf16),
            vmem((count, 3) + pair_rows, bf16),
            vmem((rows, keys), f32),
            vmem((2 * HEAD_SIZE, keys), f32),
            vmem((8, 2, 128, 640), bf16),
            vmem((8, 128, 640), bf16),
            vmem((2, own, width), bf16),
            vmem((3, 2, own, width), bf16),
            vmem((own, width), bf16),
            vmem((own, width), bf16),
            dma((21,)), dma((21,)), dma((3,)), dma((3,)), dma((9,)), dma((9,)), dma((1,)), dma((1,)),
            dma((3,)), dma((3,)), dma((1,)), dma((1,)), dma((8,)),
        ],
        compiler_params=params(7, 62),
        cost_estimate=pl.CostEstimate(flops=40000 * MIB, bytes_accessed=200 * MIB, transcendentals=0),
        name="backward",
    )(
        branch, query, pairs, kept, mixed, packed, h_first, mlp_part, mid, cos_table, sin_table
    )


def ending_kernel(
    part, weights, ff, tokens, grad_mid, gain, gain_two,
    input_grad, share_query, share_pair, share_output, gain_sum, share_gate_up, share_down,
    landed, ours, partner, landed_last, shares, ff_in, grads, gains, gains_in, gains_near,
    sends, recvs, last_sends, last_recvs, far_sends, far_recvs, ff_sends, ff_recvs,
    gain_sends, gain_recvs, gain_last_sends, gain_last_recvs,
):
    dp, seq, tensor = lax.axis_index("dp"), lax.axis_index("seq"), lax.axis_index("tensor")
    z, y = tensor // 2, tensor % 2
    peers = tensor_peers()
    chips = chip_peers()
    owners = [((dp + k // 8) % 2, (seq + k % 8) % 8) for k in range(1, 16)]
    count = part.shape[0]
    units = share_down.shape[0]
    greet(
        [{"tensor": peer} for peer in peers] + [{"dp": d, "seq": s} for d, s in owners]
    )

    def pair_of(at):
        return pl.ds(pl.multiple_of(at * 64, 64), 64)

    out = []
    for i in range(count):
        for k, dz in enumerate((2, 1, 3)):
            other = (z + dz) % 4
            copy = remote(
                part.at[i, pair_of(other)], landed.at[i, k], sends, recvs, 3 * i + k,
                {"tensor": 2 * other + y},
            )
            copy.start()
            out.append(copy)
    swap = remote(ff.at[1], ff_in, ff_sends, ff_recvs, 0, {"dp": 1 - dp})
    swap.start()
    far = [
        remote(
            weights.at[d * 4 + px], shares.at[i], far_sends, far_recvs, i,
            {"dp": d, "seq": 2 * px + c},
        )
        for i, (d, px, c) in enumerate(chips)
    ]
    for copy in far:
        copy.start()
    grads[...] = jnp.zeros_like(grads)

    def collect(i):
        for copy in out[3 * i : 3 * i + 3]:
            copy.wait()

        def step(k, carry):
            row = pl.multiple_of(k * 16, 16)
            for own in (False, True):
                side = y if own else 1 - y
                at = pl.ds(pl.multiple_of(z * 64 + side * 32 + row, 16), 16)
                result = part[i, at, :].astype(f32)
                at = pl.ds(pl.multiple_of(side * 32 + row, 16), 16)
                for j in range(3):
                    result = result + landed[i, j, at, :].astype(f32)
                if own:
                    ours[i, pl.ds(row, 16), :] = result
                else:
                    partner[i, pl.ds(row, 16), :] = result.astype(bf16)
            return carry

        lax.fori_loop(0, 2, step, 0)
        copy = remote(
            partner.at[i], landed_last.at[i], last_sends, last_recvs, i, {"tensor": 2 * z + 1 - y}
        )
        copy.start()
        return copy

    def conclude(i, copy):
        copy.wait()

        def step(k, carry):
            row = pl.ds(pl.multiple_of(k * 16, 16), 16)
            grad = ours[i, row, :] + landed_last[i, row, :].astype(f32)
            token_rows = tokens[i, row, :].astype(f32)
            inverse = inverse_rms(token_rows)
            normed = token_rows * inverse
            product = grad * normed
            grads[...] += product[:8] + product[8:]
            inner = jnp.mean(product * gain[...], axis=-1, keepdims=True)
            at = pl.ds(pl.multiple_of(i * 32 + k * 16, 16), 16)
            result = grad_mid[at, :] + inverse * (grad * gain[...] - normed * inner)
            input_grad[i, row, :] = result.astype(bf16)
            return carry

        lax.fori_loop(0, 2, step, 0)

    swap.wait()
    for tile in range(8):
        at = slice(128 * tile, 128 * tile + 128)
        share_gate_up[0, :, at] = ff[0, :, at].astype(f32) + ff_in[:, at].astype(f32)
        up_at = slice(units + 128 * tile, units + 128 * tile + 128)
        share_gate_up[1, :, at] = ff[0, :, up_at].astype(f32) + ff_in[:, up_at].astype(f32)
        down_at = slice(2 * units + 128 * tile, 2 * units + 128 * tile + 128)
        both = ff[0, :, down_at].astype(f32) + ff_in[:, down_at].astype(f32)
        share_down[at, :] = both.T
    first = collect(0)
    second = collect(1)
    for copy in far:
        copy.wait()
    here = dp * 4 + seq // 2
    sums = weights[here].astype(f32)
    for i in range(7):
        sums = sums + shares[i].astype(f32)
    share_query[...] = sums[:, :256]
    share_pair[...] = sums[:, 512:]
    share_output[...] = sums[:, 256:512].T
    conclude(0, first)
    third = collect(2)
    conclude(1, second)
    conclude(2, third)
    gains[...] = jnp.zeros_like(gains)
    gains[0:1, :] = jnp.sum(grads[...], axis=0, keepdims=True)
    gains[1:2, :] = jnp.sum(gain_two[...], axis=0, keepdims=True)
    spread_gains = []
    for k, (d, s) in enumerate(owners):
        at = pl.ds(pl.multiple_of((d * 8 + s) * 128, 128), 128)
        copy = remote(gains.at[:, at], gains_in.at[k], gain_sends, gain_recvs, k, {"dp": d, "seq": s})
        copy.start()
        spread_gains.append(copy)
    own = gains[:, pl.ds(pl.multiple_of((dp * 8 + seq) * 128, 128), 128)]
    for k, copy in enumerate(spread_gains):
        copy.wait()
        own = own + gains_in[k]
    gains_near[7] = own
    last = [
        remote(gains_near.at[7], gains_near.at[i], gain_last_sends, gain_last_recvs, i, {"tensor": peer})
        for i, peer in enumerate(peers)
    ]
    for copy in last:
        copy.start()
    for copy in last:
        copy.wait()
    shifts = ((2, 1), (1, 1), (3, 1), (2, 0), (1, 0), (3, 0), (0, 1))
    sums = jnp.zeros_like(own)
    for t in range(8):
        slot = jnp.int32(7)
        for i, (dz, dy) in enumerate(shifts):
            source = ((z + 4 - dz) % 4) * 2 + (y + dy) % 2
            slot = jnp.where(source == t, i, slot)
        sums = sums + gains_near[slot]
    gain_sum[...] = sums[0:2, :]


def ending(part, weights, ff, tokens, grad_mid, gain, gain_two):
    count, rows, width = part.shape
    units = ff.shape[2] // 3
    dma = pltpu.SemaphoreType.DMA
    vmem = pltpu.VMEM
    return pl.pallas_call(
        ending_kernel,
        out_shape=(
            jax.ShapeDtypeStruct((count, 32, width), bf16),
            jax.ShapeDtypeStruct((128, 256), f32),
            jax.ShapeDtypeStruct((128, 128), f32),
            jax.ShapeDtypeStruct((256, 128), f32),
            jax.ShapeDtypeStruct((2, 128), f32),
            jax.ShapeDtypeStruct((2, 128, units), f32),
            jax.ShapeDtypeStruct((units, 128), f32),
        ),
        in_specs=[VMEM] * 7,
        out_specs=(VMEM,) * 7,
        scratch_shapes=[
            vmem((count, 3, 64, width), bf16),
            vmem((count, 32, width), f32),
            vmem((count, 32, width), bf16),
            vmem((count, 32, width), bf16),
            vmem((7, 128, 640), bf16),
            vmem((128, 3 * units), bf16),
            vmem((8, width), f32),
            vmem((8, width), f32),
            vmem((15, 8, 128), f32),
            vmem((8, 8, 128), f32),
            dma((9,)), dma((9,)), dma((3,)), dma((3,)), dma((7,)), dma((7,)), dma((1,)), dma((1,)),
            dma((15,)), dma((15,)), dma((7,)), dma((7,)),
        ],
        compiler_params=params(2, 48),
        cost_estimate=pl.CostEstimate(flops=MIB, bytes_accessed=150 * MIB, transcendentals=0),
        name="ending",
    )(part, weights, ff, tokens, grad_mid, gain, gain_two)


def shards(
    tokens,
    cotangent,
    query_weight,
    query_first,
    query_second,
    key_value_weight,
    key_value_first_moment,
    key_value_second_moment,
    output_weight,
    output_first,
    output_second,
    gate_up_weight,
    gate_up_first,
    gate_up_second,
    down_weight,
    down_first,
    down_second,
    norm_gains,
    gains_first,
    gains_second,
):
    count, local_len, width = tokens.shape
    tensor = lax.axis_index("tensor")

    def own_rows(values):
        return lax.dynamic_slice_in_dim(values, tensor * 32, 32, 1)

    packed = jnp.concatenate(
        [
            query_weight,
            key_value_weight.reshape(128, 2 * HEAD_SIZE),
            output_weight.T,
        ],
        axis=1,
    ).astype(bf16)
    ff_low = jnp.concatenate(
        [gate_up_weight[0], gate_up_weight[1], down_weight.T], axis=1
    ).astype(bf16)
    gains_low = jnp.pad(norm_gains.astype(bf16).astype(f32), ((0, 6), (0, 0)))
    positions = lax.axis_index("seq") * local_len + jnp.arange(local_len, dtype=jnp.int32)
    cos_table, sin_table = rotary(positions)
    cos_wide = jnp.tile(cos_table, (1, 4))
    sin_wide = jnp.tile(jnp.concatenate([sin_table, -sin_table], axis=1), (1, 2))
    query, pairs, kept, mixed, packed_all, h_first, mid, h_second, ff_all, gains_used = forward(
        tokens, packed, gains_low, ff_low, cos_wide, sin_wide
    )
    branch_own, grad_mid, gain_two, mlp_term, grads = feed_forward(
        h_second,
        cotangent.reshape(count, 8, 32, width),
        ff_all,
        mid,
        gains_used[1:2],
    )
    shares_ff = lax.psum_scatter(grads, "seq", scatter_dimension=0, tiled=False)
    part, grads_projection, block_out = backward(
        branch_own,
        query,
        pairs,
        kept,
        mixed,
        packed_all,
        h_first,
        mlp_term,
        mid,
        cos_wide,
        sin_wide,
    )
    (
        input_grad,
        share_query,
        share_pair,
        share_output,
        share_gains,
        share_gate_up,
        share_down,
    ) = ending(
        part,
        grads_projection,
        shares_ff,
        own_rows(tokens),
        grad_mid,
        gains_used[:1],
        gain_two,
    )

    query_new, query_first_new, query_second_new = adam(
        query_weight, share_query, query_first, query_second, rate_wide, weight_decay
    )
    pair_new, pair_first_new, pair_second_new = adam(
        key_value_weight,
        share_pair[:, None, :],
        key_value_first_moment,
        key_value_second_moment,
        rate_wide,
        weight_decay,
    )
    output_new, output_first_new, output_second_new = adam(
        output_weight,
        share_output,
        output_first,
        output_second,
        rate_output,
        weight_decay,
    )
    gate_up_new, gate_up_first_new, gate_up_second_new = adam(
        gate_up_weight,
        share_gate_up,
        gate_up_first,
        gate_up_second,
        rate_wide,
        weight_decay,
    )
    down_new, down_first_new, down_second_new = adam(
        down_weight, share_down, down_first, down_second, rate_down, weight_decay
    )
    gains_new, gains_first_new, gains_second_new = adam(
        norm_gains, share_gains, gains_first, gains_second, rate_gains, 0.0
    )
    return (
        block_out,
        input_grad,
        query_new,
        query_first_new,
        query_second_new,
        pair_new,
        pair_first_new,
        pair_second_new,
        output_new,
        output_first_new,
        output_second_new,
        gate_up_new,
        gate_up_first_new,
        gate_up_second_new,
        down_new,
        down_first_new,
        down_second_new,
        gains_new,
        gains_first_new,
        gains_second_new,
    )


def solution(mesh):
    return jax.shard_map(
        shards,
        mesh=mesh,
        in_specs=(
            P("dp", "seq", None),
            P("dp", "seq", None),
            P(("dp", "seq"), "tensor"),
            P(("dp", "seq"), "tensor"),
            P(("dp", "seq"), "tensor"),
            P(("dp", "seq"), "tensor", None),
            P(("dp", "seq"), "tensor", None),
            P(("dp", "seq"), "tensor", None),
            P("tensor", ("dp", "seq")),
            P("tensor", ("dp", "seq")),
            P("tensor", ("dp", "seq")),
            P(None, ("dp", "seq"), "tensor"),
            P(None, ("dp", "seq"), "tensor"),
            P(None, ("dp", "seq"), "tensor"),
            P("tensor", ("dp", "seq")),
            P("tensor", ("dp", "seq")),
            P("tensor", ("dp", "seq")),
            P(None, ("dp", "seq")),
            P(None, ("dp", "seq")),
            P(None, ("dp", "seq")),
        ),
        out_specs=(
            P("dp", ("seq", "tensor"), None),
            P("dp", ("seq", "tensor"), None),
            P(("dp", "seq"), "tensor"),
            P(("dp", "seq"), "tensor"),
            P(("dp", "seq"), "tensor"),
            P(("dp", "seq"), "tensor", None),
            P(("dp", "seq"), "tensor", None),
            P(("dp", "seq"), "tensor", None),
            P("tensor", ("dp", "seq")),
            P("tensor", ("dp", "seq")),
            P("tensor", ("dp", "seq")),
            P(None, ("dp", "seq"), "tensor"),
            P(None, ("dp", "seq"), "tensor"),
            P(None, ("dp", "seq"), "tensor"),
            P("tensor", ("dp", "seq")),
            P("tensor", ("dp", "seq")),
            P("tensor", ("dp", "seq")),
            P(None, ("dp", "seq")),
            P(None, ("dp", "seq")),
            P(None, ("dp", "seq")),
        ),
        check_vma=False,
    )
```

```python
import jax
import jax.numpy as jnp
from jax import lax
from jax.experimental import pallas as pl
from jax.experimental.pallas import tpu as pltpu
from jax.sharding import PartitionSpec as P

QUERY_HEADS = 32
KEY_VALUE_HEADS = 8
HEAD_SIZE = 64
STEP = 10
GROUP = QUERY_HEADS // KEY_VALUE_HEADS


norm_eps = 1e-05
rope_base = 500000.0
beta_first = 0.9
beta_second = 0.95
adam_eps = 1e-08
weight_decay = 0.1
rate_wide = 0.07
rate_down = 0.035
rate_output = 1.0
rate_gains = 0.7

bf16 = jnp.bfloat16
f32 = jnp.float32
MESH = pl.DeviceIdType.MESH
VMEM = pl.BlockSpec(memory_space=pltpu.VMEM)
ANY = pl.BlockSpec(memory_space=pl.ANY)
MIB = 1024 * 1024


def inverse_rms(values):
    return lax.rsqrt(jnp.mean(values * values, axis=-1, keepdims=True) + norm_eps)


def rotary(positions):
    half_size = HEAD_SIZE // 2
    freqs = rope_base ** (-2.0 * jnp.arange(half_size, dtype=jnp.float32) / HEAD_SIZE)
    angles = positions.astype(jnp.float32)[:, None] * freqs[None, :]
    return (jnp.cos(angles), jnp.sin(angles))


def adam(master, grad, moment_one, moment_two, rate, decay):
    new_one = beta_first * moment_one + (1.0 - beta_first) * grad
    new_two = beta_second * moment_two + (1.0 - beta_second) * grad * grad
    ahead = (
        new_one
        / (1.0 - beta_first**STEP)
        / (jnp.sqrt(new_two / (1.0 - beta_second**STEP)) + adam_eps)
    )
    return (master - rate * (ahead + decay * master), new_one, new_two)


def tensor_peers():
    me = lax.axis_index("tensor")
    z, y = me // 2, me % 2
    return [
        ((z + dz) % 4) * 2 + (y + dy) % 2
        for dz, dy in ((2, 1), (1, 1), (3, 1), (2, 0), (1, 0), (3, 0), (0, 1))
    ]


def chip_peers():
    dp, seq = lax.axis_index("dp"), lax.axis_index("seq")
    x, core = seq // 2, seq % 2
    return [
        ((dp + dd) % 2, (x + dx) % 4, core)
        for dx, dd in ((2, 1), (1, 1), (3, 1), (0, 1), (2, 0), (1, 0), (3, 0))
    ]


def row_peers():
    seq = lax.axis_index("seq")
    x, core = seq // 2, seq % 2
    return [((x + dx) % 4, core) for dx in (2, 1, 3)]


def sibling():
    seq = lax.axis_index("seq")
    return seq + 1 - 2 * (seq % 2)


def greet(devices):
    barrier = pltpu.get_barrier_semaphore()
    for device in devices:
        pl.semaphore_signal(barrier, inc=1, device_id=device, device_id_type=MESH)
    pl.semaphore_wait(barrier, len(devices))


def remote(src, dst, sends, recvs, at, device):
    return pltpu.make_async_remote_copy(src, dst, sends.at[at], recvs.at[at], device, MESH)


def params(collective_id, mib):
    return pltpu.CompilerParams(
        collective_id=collective_id, has_side_effects=True, vmem_limit_bytes=mib * MIB
    )


def causal_bias(bias):
    seq = lax.axis_index("seq")
    rows, keys = bias.shape
    row = lax.broadcasted_iota(jnp.int32, (rows, keys), 0) + seq * rows
    key = lax.broadcasted_iota(jnp.int32, (rows, keys), 1)
    bias[...] = jnp.where(key <= row, 0.0, -1e30).astype(f32)


def nt(left, right):
    return lax.dot_general(left, right, (((1,), (1,)), ((), ())), preferred_element_type=f32)


def tn(left, right):
    return lax.dot_general(left, right, (((0,), (0,)), ((), ())), preferred_element_type=f32)


def columns(tile, size):
    return pl.ds(pl.multiple_of(tile * size, size), size)


def turn(values, cos_table, sin_table):
    lane = lax.broadcasted_iota(jnp.int32, values.shape, 1)
    half = HEAD_SIZE // 2
    other = jnp.where(
        lane % HEAD_SIZE < half,
        pltpu.roll(values, values.shape[1] - half, 1),
        pltpu.roll(values, half, 1),
    )
    return values * cos_table + other * sin_table


def block_of(peer):
    return pl.ds(pl.multiple_of(peer * 32, 32), 32)


def own_chunks(body):
    def step(k, carry):
        body(k // 2, pl.multiple_of((k % 2) * 16, 16))
        return carry

    lax.fori_loop(0, 6, step, 0)


FIRST = 896
SHIFTS = (2, 1, 3)


def fold_scratch(lead, rows, width):
    rest = width - FIRST
    return [
        pltpu.VMEM(lead + shape, bf16)
        for shape in (
            (3, 2, rows, FIRST),
            (4, rows, rest),
            (3, rows, rest),
            (3, rows, rest),
            (rows, FIRST),
            (rows, FIRST),
        )
    ]


class Fold:
    def __init__(self, source, local, refs, sends, recvs, base):
        tensor = lax.axis_index("tensor")
        self.z, self.y = tensor // 2, tensor % 2
        self.source, self.local = source, local
        self.over_z, self.from_partner, self.ready, self.second, self.mine, self.last = refs
        self.rows, self.width = self.from_partner.shape[1], FIRST + self.from_partner.shape[2]
        self.sends, self.recvs, self.base = sends, recvs, base
        self.copies = {}

    def send(self, k, source, place, z, y):
        copy = remote(
            source, place, self.sends, self.recvs, self.base + k, {"tensor": 2 * (z % 4) + y}
        )
        copy.start()
        self.copies[k] = copy

    def begin(self, dz):
        to = (self.z + dz) % 4
        first, rest = pl.ds(0, FIRST), pl.ds(FIRST, self.width - FIRST)
        if dz:
            k = SHIFTS.index(dz)
            self.send(k, self.source.at[to, :, :, first], self.over_z.at[k], to, self.y)
        self.send(
            3 + dz, self.source.at[to, 1 - self.y, :, rest], self.from_partner.at[dz], self.z,
            1 - self.y,
        )

    def chunks(self, body):
        def step(k, carry):
            body(pl.ds(pl.multiple_of(k * 16, 16), 16))
            return carry

        lax.fori_loop(0, self.rows // 16, step, 0)

    def pass_z(self, dz):
        self.copies[3 + dz].wait_recv()
        if dz == 0:
            return
        k = SHIFTS.index(dz)

        def body(at):
            both = self.local(dz, 0, at)[:, FIRST:] + self.from_partner[dz, at, :].astype(f32)
            self.ready[k, at, :] = both.astype(bf16)

        self.chunks(body)
        self.send(8 + k, self.ready.at[k], self.second.at[k], self.z + dz, self.y)

    def pass_partner(self):
        for k in range(3):
            self.copies[k].wait_recv()

        def body(at):
            result = self.local(0, 1, at)[:, :FIRST]
            for k in range(3):
                result = result + self.over_z[k, 1 - self.y, at, :].astype(f32)
            self.mine[at, :] = result.astype(bf16)

        self.chunks(body)
        self.send(7, self.mine, self.last, self.z, 1 - self.y)

    def finish(self):
        for k in (7, 8, 9, 10):
            self.copies[k].wait_recv()
        for copy in self.copies.values():
            copy.wait_send()

    def total(self, at):
        own = self.local(0, 0, at)
        low = own[:, :FIRST] + self.last[at, :].astype(f32)
        high = own[:, FIRST:] + self.from_partner[0, at, :].astype(f32)
        for k in range(3):
            low = low + self.over_z[k, self.y, at, :].astype(f32)
            high = high + self.second[k, at, :].astype(f32)
        return jnp.concatenate([low, high], axis=1)


class Weights:
    def __init__(self, mine, whole, sends, recvs, near_sends, near_recvs):
        self.dp, self.seq = lax.axis_index("dp"), lax.axis_index("seq")
        self.mine, self.whole = mine, whole
        self.sends, self.recvs = sends, recvs
        self.near_sends, self.near_recvs = near_sends, near_recvs
        self.started, self.passed = {}, []

    def owner(self, dx, dd):
        x, core = self.seq // 2, self.seq % 2
        return (self.dp + dd) % 2, ((x + dx) % 4) * 2 + core

    def device(self, dx, dd):
        dp, seq = self.owner(dx, dd)
        return {"dp": dp, "seq": seq}

    def view(self, dx, dd, half=None):
        ref = self.whole.at[self.owner(dx, dd)]
        return ref if half is None else ref.at[pl.ds(64 * half, 64)]

    def send(self, k, block, to, half=None):
        place = self.view(*block, half)
        source = place
        if block == (0, 0):
            source = self.mine if half is None else self.mine.at[pl.ds(64 * half, 64)]
        copy = remote(source, place, self.sends, self.recvs, k, self.device(*to))
        copy.start()
        self.started[k] = copy

    def beside(self, k, block, half=None):
        place = self.view(*block, half)
        source = self.mine if block == (0, 0) else place
        copy = remote(source, place, self.near_sends, self.near_recvs, k, {"seq": sibling()})
        copy.start()
        self.passed.append(copy)

    def start(self):
        self.send(0, (0, 0), (0, 1))
        self.send(1, (0, 0), (1, 0), 0)
        self.send(2, (0, 0), (3, 0), 0)
        self.beside(0, (0, 0))

    def rest(self):
        self.send(3, (0, 0), (1, 0), 1)
        self.send(4, (0, 0), (3, 0), 1)

    def partner(self):
        self.started[0].wait_recv()
        self.send(5, (0, 1), (1, 0))
        self.send(6, (0, 1), (3, 0))
        self.beside(1, (0, 1))

    def own_ring(self):
        self.started[1].wait_recv()
        self.send(7, (3, 0), (1, 0), 0)
        self.started[4].wait_recv()
        self.send(8, (1, 0), (3, 0), 1)
        self.started[3].wait_recv()
        self.beside(2, (3, 0))
        self.started[2].wait_recv()
        self.beside(3, (1, 0))

    def partner_ring(self):
        self.started[5].wait_recv()
        self.send(9, (3, 1), (1, 0), 0)
        self.beside(4, (3, 1))
        self.started[6].wait_recv()
        self.send(10, (1, 1), (3, 0), 1)
        self.beside(5, (1, 1))

    def finish(self):
        for k, half, dd in ((7, 0, 0), (8, 1, 0), (9, 0, 1), (10, 1, 1)):
            self.started[k].wait_recv()
            self.beside(k - 1, (2, dd), half)
        for copy in self.started.values():
            copy.wait_send()
        for copy in self.passed:
            copy.wait()


def forward_kernel(
    tokens, mine, gains_mine, ff_mine, cos_table, sin_table,
    query_out, pairs_out, kept_out, mixed_out, packed_out, first_out, mid, rows_in, ff_all, gains,
    query, pairs, kept, mixed, packed, h_first, part, over_z, from_partner, ready, second, own_first, last_first, bias,
    sends, recvs, near_sends, near_recvs, late_sends, late_recvs, late_near_sends,
    late_near_recvs, gain_sends, gain_recvs, pair_sends, pair_recvs,
    pair_near_sends, pair_near_recvs, out_sends, out_recvs, ff_sends, ff_recvs, ff_near_sends,
    ff_near_recvs, row_sends, row_recvs, local, stores,
):
    dp, seq, tensor = lax.axis_index("dp"), lax.axis_index("seq"), lax.axis_index("tensor")
    me = dp * 8 + seq
    stored = []

    def store(source, place):
        copy = pltpu.make_async_copy(source, place, stores.at[len(stored)])
        copy.start()
        stored.append(copy)

    count, rows, width = tokens.shape
    keys = bias.shape[1]
    near = {"seq": sibling()}
    owners = [((dp + k // 8) % 2, (seq + k % 8) % 8) for k in range(1, 16)]
    greet(
        [{"tensor": peer} for peer in tensor_peers()] + [{"dp": d, "seq": s} for d, s in owners]
    )
    gain_at = pl.ds(pl.multiple_of(me * 128, 128), 128)
    gain_copies = [
        remote(gains_mine, gains.at[:, gain_at], gain_sends, gain_recvs, k, {"dp": d, "seq": s})
        for k, (d, s) in enumerate(owners)
    ]
    for copy in gain_copies:
        copy.start()
    early, late = pl.ds(0, 384), pl.ds(384, 256)
    out, out_late = [
        [
            remote(
                mine.at[:, at], packed.at[me, :, at], ss, rs, i, {"dp": d, "seq": 2 * x + c}
            )
            for i, (d, x, c) in enumerate(chip_peers())
        ]
        for at, ss, rs in ((early, sends, recvs), (late, late_sends, late_recvs))
    ]
    first, first_late = [
        remote(mine.at[:, at], packed.at[me, :, at], ss, rs, 7, near)
        for at, ss, rs in (
            (early, near_sends, near_recvs),
            (late, late_near_sends, late_near_recvs),
        )
    ]
    for copy in out + [first] + out_late + [first_late]:
        copy.start()
    ff = Weights(ff_mine, ff_all, ff_sends, ff_recvs, ff_near_sends, ff_near_recvs)
    ff.start()
    store_ff = pltpu.make_async_copy(ff_mine, ff_all.at[dp, seq], local)
    store_ff.start()
    packed[me] = mine[...]
    gains[:, gain_at] = gains_mine[...]
    causal_bias(bias)
    for copy in gain_copies:
        copy.wait()

    def normalize(k, carry):
        i = k // 16
        at = pl.ds(pl.multiple_of((k % 16) * 16, 16), 16)
        token_rows = tokens[i, at, :].astype(f32)
        h_first[i, at, :] = (token_rows * inverse_rms(token_rows) * gains[0:1, :]).astype(bf16)
        return carry

    lax.fori_loop(0, count * 16, normalize, 0)
    store(h_first, first_out)

    def pass_weights(out, first, at, ss, rs):
        passed = [first]
        for i, (dd, dx) in (
            (6, (0, 1)), (5, (0, 3)), (3, (1, 0)), (4, (0, 2)), (2, (1, 1)), (1, (1, 3)), (0, (1, 2)),
        ):
            out[i].wait_recv()
            owner = (((dp + dd) % 2) * 4 + (seq // 2 + dx) % 4) * 2 + seq % 2
            block = packed.at[owner, :, at]
            copy = remote(block, block, ss, rs, i, near)
            copy.start()
            passed.append(copy)
        return passed

    for copy in pass_weights(out, first, early, near_sends, near_recvs):
        copy.wait()
    scale = HEAD_SIZE ** (-0.5)
    lane = lax.broadcasted_iota(jnp.int32, (rows, 2 * HEAD_SIZE), 1)

    def project(i, carry):
        raw = jnp.dot(
            h_first[i], packed[:, :, :384].reshape(width, 384), preferred_element_type=f32
        )
        for at in range(GROUP // 2):
            both = raw[:, at * 2 * HEAD_SIZE : (at + 1) * 2 * HEAD_SIZE]
            both = turn(both, cos_table[...], -sin_table[...]) * scale
            query[i, 2 * at] = jnp.where(lane < HEAD_SIZE, both, 0.0).astype(bf16)
            moved = pltpu.roll(both, HEAD_SIZE, 1)
            query[i, 2 * at + 1] = jnp.where(lane < HEAD_SIZE, moved, 0.0).astype(bf16)
        pair = raw[:, GROUP * HEAD_SIZE :]
        turned = turn(pair, cos_table[...], -sin_table[...])
        pairs[seq, i] = jnp.where(lane < HEAD_SIZE, turned, pair).astype(bf16)
        return carry

    lax.fori_loop(0, count, project, 0)
    pair_out = [
        remote(pairs.at[seq], pairs.at[seq], pair_sends, pair_recvs, i, {"seq": 2 * x + c})
        for i, (x, c) in enumerate(row_peers())
    ]
    for copy in pair_out:
        copy.start()
    pair_first = remote(pairs.at[seq], pairs.at[seq], pair_near_sends, pair_near_recvs, 3, near)
    pair_first.start()
    ff.rest()
    pair_passed = []
    for i, dx in ((1, 3), (2, 1), (0, 2)):
        pair_out[i].wait_recv()
        owner = ((seq // 2 + dx) % 4) * 2 + seq % 2
        forward = remote(
            pairs.at[owner], pairs.at[owner], pair_near_sends, pair_near_recvs, i, near
        )
        forward.start()
        pair_passed.append(forward)
    pair_first.wait()
    for copy in pair_passed:
        copy.wait()
    store(query, query_out)
    store(pairs, pairs_out)
    passed_late = pass_weights(out_late, first_late, late, late_near_sends, late_near_recvs)
    ff.partner()

    def attend(i):
        upper = []
        pair = pairs[:, i].reshape(keys, 2 * HEAD_SIZE)
        for head in range(GROUP):
            scores = nt(query[i, head], pair) + bias[...]
            row_max = jnp.max(scores, axis=-1, keepdims=True)
            exps = jnp.exp(scores - row_max)
            row_sum = jnp.sum(exps, axis=-1, keepdims=True)
            mix = jnp.dot(exps.astype(bf16), pair, preferred_element_type=f32) / row_sum
            kept[i, head] = jnp.where(lane < HEAD_SIZE, row_max + jnp.log(row_sum), mix)
            upper.append(mix)
        for at in range(GROUP // 2):
            low = pltpu.roll(upper[2 * at], HEAD_SIZE, 1)
            both = jnp.where(lane < HEAD_SIZE, low, upper[2 * at + 1])
            mixed[i, :, at * 2 * HEAD_SIZE : (at + 1) * 2 * HEAD_SIZE] = both.astype(bf16)

    def attend_step(i, carry):
        attend(i)
        return carry

    def output_step(i, carry):
        def term(tile, inner_carry):
            weight_rows = packed[pl.ds(tile * 4, 4), :, 384:640].reshape(512, 256)
            product = nt(mixed[i], weight_rows).astype(bf16)
            part[i, :, :, :, columns(tile, 512)] = product.reshape(4, 2, 32, 512)
            return inner_carry

        lax.fori_loop(0, width // 512, term, 0)
        return carry

    def term_of(i):
        def local(dz, dy, at):
            return part[i, (tensor // 2 + dz) % 4, (tensor + dy) % 2, at, :].astype(f32)

        return local

    folds = []
    for i in range(count):
        lax.fori_loop(i, i + 1, attend_step, 0)
        if i == 0:
            for copy in passed_late:
                copy.wait()
            store(packed, packed_out)
        lax.fori_loop(i, i + 1, output_step, 0)
        fold = Fold(
            part.at[i],
            term_of(i),
            [ref.at[i] for ref in (over_z, from_partner, ready, second, own_first, last_first)],
            out_sends,
            out_recvs,
            11 * i,
        )
        for dz in (2, 1, 3, 0):
            fold.begin(dz)
        folds.append(fold)
        if i:
            for dz in (2, 1, 3, 0):
                folds[i - 1].pass_z(dz)
    store(kept, kept_out)
    store(mixed, mixed_out)
    folds[0].pass_partner()
    for dz in (2, 1, 3, 0):
        folds[2].pass_z(dz)
    folds[1].pass_partner()
    ff.own_ring()
    folds[2].pass_partner()
    ff.partner_ring()
    for i, fold in enumerate(folds):
        fold.finish()

        def chunk(k, carry, i=i, fold=fold):
            row = pl.multiple_of(k * 16, 16)
            at = pl.ds(pl.multiple_of(tensor * 32 + row, 16), 16)
            result = fold.total(pl.ds(row, 16)) + tokens[i, at, :].astype(f32)
            at = pl.ds(pl.multiple_of(i * 32 + row, 16), 16)
            mid[at, :] = result
            rows_in[0, at, :] = (result * inverse_rms(result) * gains[1:2, :]).astype(bf16)
            return carry

        lax.fori_loop(0, 2, chunk, 0)
    z, y = tensor // 2, tensor % 2
    row_copies = [
        remote(
            rows_in.at[0], rows_in.at[k + 1], row_sends, row_recvs, k,
            {"tensor": 2 * ((z + dz) % 4) + (y + dy) % 2},
        )
        for k, (dz, dy) in enumerate(((0, 1), (1, 0), (3, 0)))
    ]
    for copy in row_copies:
        copy.start()
    for copy in out + out_late + pair_out:
        copy.wait_send()
    store_ff.wait()
    ff.finish()
    for copy in row_copies + stored:
        copy.wait()


def forward(tokens, mine, gains_mine, ff_mine, cos_table, sin_table):
    count, rows, width = tokens.shape
    dma = pltpu.SemaphoreType.DMA
    lanes = 2 * HEAD_SIZE
    return pl.pallas_call(
        forward_kernel,
        out_shape=(
            jax.ShapeDtypeStruct((count, GROUP, rows, lanes), bf16),
            jax.ShapeDtypeStruct((8, count, rows, lanes), bf16),
            jax.ShapeDtypeStruct((count, GROUP, rows, lanes), f32),
            jax.ShapeDtypeStruct((count, rows, GROUP * HEAD_SIZE), bf16),
            jax.ShapeDtypeStruct((16,) + mine.shape, bf16),
            jax.ShapeDtypeStruct((count, rows, width), bf16),
            jax.ShapeDtypeStruct((count * 32, width), f32),
            jax.ShapeDtypeStruct((4, count * 32, width), bf16),
            jax.ShapeDtypeStruct((2, 8) + ff_mine.shape, bf16),
            jax.ShapeDtypeStruct((8, width), f32),
        ),
        in_specs=[VMEM] * 6,
        out_specs=(ANY,) * 6 + (VMEM, VMEM, ANY, VMEM),
        scratch_shapes=[
            pltpu.VMEM((count, GROUP, rows, lanes), bf16),
            pltpu.VMEM((8, count, rows, lanes), bf16),
            pltpu.VMEM((count, GROUP, rows, lanes), f32),
            pltpu.VMEM((count, rows, GROUP * HEAD_SIZE), bf16),
            pltpu.VMEM((16,) + mine.shape, bf16),
            pltpu.VMEM((count, rows, width), bf16),
            pltpu.VMEM((count, 4, 2, 32, width), bf16),
            *fold_scratch((count,), 32, width),
            pltpu.VMEM((rows, 8 * rows), f32),
            dma((7,)), dma((7,)), dma((8,)), dma((8,)), dma((7,)), dma((7,)), dma((8,)), dma((8,)),
            dma((15,)), dma((15,)), dma((3,)), dma((3,)),
            dma((4,)), dma((4,)), dma((33,)), dma((33,)), dma((11,)), dma((11,)), dma((10,)),
            dma((10,)), dma((3,)), dma((3,)), dma, dma((6,)),
        ],
        compiler_params=params(1, 60),
        cost_estimate=pl.CostEstimate(flops=40000 * MIB, bytes_accessed=200 * MIB, transcendentals=0),
        name="forward",
    )(tokens, mine, gains_mine, ff_mine, cos_table, sin_table)


class Spread:
    def __init__(self, buffer, sends, recvs):
        tensor = lax.axis_index("tensor")
        self.buffer, self.sends, self.recvs = buffer, sends, recvs
        self.z, self.y = tensor // 2, tensor % 2
        self.started = {}

    def at(self, dz, dy):
        return ((self.z + dz) % 4) * 2 + (self.y + dy) % 2

    def send(self, k, block, to, half=None):
        ref = self.buffer.at[block]
        if half is not None:
            rows = self.buffer.shape[1] // 2
            ref = self.buffer.at[block, pl.ds(half * rows, rows)]
        copy = remote(ref, ref, self.sends, self.recvs, k, {"tensor": to})
        copy.start()
        self.started[k] = copy

    def pass_partner(self):
        self.send(3, self.at(0, 1), self.at(1, 0))
        self.send(4, self.at(0, 1), self.at(3, 0))

    def pass_on(self, dy):
        if dy:
            self.started[3].wait_recv()
        self.send(5 + 2 * dy, self.at(3, dy), self.at(1, 0), 0)
        if dy:
            self.started[4].wait_recv()
        self.send(6 + 2 * dy, self.at(1, dy), self.at(3, 0), 1)

    def finish(self):
        for k in range(5, 9):
            self.started[k].wait_recv()

    def drain(self):
        for copy in self.started.values():
            copy.wait_send()


def feed_forward_kernel(
    own, cotangent, weights, mid, gain,
    branch, grad_mid, grad_gain, mlp_out, grads_out,
    gate_up, down, cot, normed, grad_hidden, grad_units, hidden, second,
    over_z, from_partner, ready, second_in, own_first, last_first, mlp, grads,
    sends, recvs, back_sends, back_recvs, local, cot_sems, out_sems, mlp_sem,
):
    tensor = lax.axis_index("tensor")
    units = down.shape[3]
    width = 16 * 128
    dp = lax.axis_index("dp")
    load_down = pltpu.make_async_copy(
        weights.at[:, :, :, pl.ds(2 * units, units)], down, local.at[0]
    )
    load_gate_up = pltpu.make_async_copy(
        weights.at[:, :, :, pl.ds(0, 2 * units)], gate_up, local.at[1]
    )
    load_down.start()
    load_cot = [
        pltpu.make_async_copy(cotangent.at[:, t], cot.at[t], cot_sems.at[t]) for t in range(8)
    ]
    for copy in load_cot:
        copy.start()
    load_gate_up.start()
    greet([{"tensor": peer} for peer in tensor_peers()])
    spread = Spread(normed, sends, recvs)
    for k, (dz, dy) in enumerate(((0, 0), (0, 1), (3, 0), (1, 0))):
        normed[spread.at(dz, dy)] = own[k]
    spread.pass_partner()
    spread.pass_on(0)
    for copy in load_cot:
        copy.wait()
    load_down.wait()

    def hidden_step(tile, carry):
        at = columns(tile, 256)
        product = jnp.dot(
            cot[...].reshape(8 * 96, width),
            down[:, :, :, at].reshape(width, 256),
            preferred_element_type=f32,
        )
        grad_hidden[:, :, at] = product.reshape(8, 96, 256)
        return carry

    lax.fori_loop(0, units // 256, hidden_step, 0)
    load_gate_up.wait()

    def own_term(dz, dy, at):
        return second[(spread.z + dz) % 4, (spread.y + dy) % 2, at, :].astype(f32)

    fold = Fold(
        second,
        own_term,
        (over_z, from_partner, ready, second_in, own_first, last_first),
        back_sends,
        back_recvs,
        0,
    )

    def block(dz):
        first = ((spread.z + dz) % 4) * 2
        both = pl.ds(first, 2)

        def units_step(tile, carry):
            at = columns(tile, 256)
            up_at = pl.ds(pl.multiple_of(units + tile * 256, 256), 256)
            rows = normed[both].reshape(192, width)
            gate_columns = gate_up[:, :, :, at].reshape(width, 256)
            up_columns = gate_up[:, :, :, up_at].reshape(width, 256)
            gate_in = jnp.dot(rows, gate_columns, preferred_element_type=f32)
            up_in = jnp.dot(rows, up_columns, preferred_element_type=f32)
            grad = grad_hidden[both, :, at].reshape(192, 256)
            sigmoid = jax.nn.sigmoid(gate_in)
            silu = gate_in * sigmoid
            hidden[both, :, at] = (silu * up_in).astype(bf16).reshape(2, 96, 256)
            grad_gate = grad * up_in * sigmoid * (1.0 + gate_in * (1.0 - sigmoid))
            grad_units[both, :, at] = grad_gate.astype(bf16).reshape(2, 96, 256)
            grad_units[both, :, up_at] = (grad * silu).astype(bf16).reshape(2, 96, 256)
            return carry

        lax.fori_loop(0, units // 256, units_step, 0)

        def second_step(tile, carry):
            at = columns(tile, 512)
            rows = grad_units[both].reshape(192, 2 * units)
            weight_rows = gate_up[tile // 2, pl.ds((tile % 2) * 4, 4)].reshape(512, 2 * units)
            product = nt(rows, weight_rows).astype(bf16)
            second[first // 2, :, :, at] = product.reshape(2, 96, 512)
            return carry

        lax.fori_loop(0, width // 512, second_step, 0)
        fold.begin(dz)

    block(0)
    spread.pass_on(1)
    block(1)
    fold.pass_z(0)
    block(3)
    fold.pass_z(1)
    spread.finish()
    block(2)
    fold.pass_z(3)

    def mlp_step(tile, carry):
        at = columns(tile, 256)
        rows = hidden[...].reshape(8 * 96, units)
        weight_rows = down[tile // 4, pl.ds((tile % 4) * 2, 2)].reshape(256, units)
        mlp[:, :, at] = nt(rows, weight_rows).astype(bf16).reshape(8, 96, 256)
        return carry

    lax.fori_loop(0, width // 512, mlp_step, 0)
    fold.pass_z(2)
    lax.fori_loop(width // 512, width // 256, mlp_step, 0)
    store_mlp = pltpu.make_async_copy(mlp, mlp_out, mlp_sem)
    store_mlp.start()

    def store(tile, slot):
        place = grads_out.at[pl.ds((tile % 4) * 2, 2), (tile // 4 + dp) % 2]
        return pltpu.make_async_copy(grads.at[slot], place, out_sems.at[slot])

    def grads_pair(pair, carry):
        for slot in range(2):
            tile = 2 * pair + slot
            at = columns(tile, 256)

            @pl.when(pair > 0)
            def _():
                store(tile - 2, slot).wait()

            wide = tn(
                normed[:, :, at].reshape(8 * 96, 256), grad_units[...].reshape(8 * 96, 2 * units)
            )
            grads[slot, :, :, : 2 * units] = wide.astype(bf16).reshape(2, 128, 2 * units)
            narrow = tn(cot[:, :, :, at].reshape(8 * 96, 256), hidden[...].reshape(8 * 96, units))
            grads[slot, :, :, 2 * units :] = narrow.astype(bf16).reshape(2, 128, units)
            store(tile, slot).start()
        return carry

    tiles = width // 256
    lax.fori_loop(0, tiles // 2 - 1, grads_pair, 0)
    fold.pass_partner()
    lax.fori_loop(tiles // 2 - 1, tiles // 2, grads_pair, 0)
    for slot in range(2):
        store(tiles - 2 + slot, slot).wait()
    store_mlp.wait()
    spread.drain()
    fold.finish()
    grad_gain[...] = jnp.zeros_like(grad_gain)

    def chunk(k, carry):
        at = pl.ds(pl.multiple_of(k * 16, 16), 16)
        grad = fold.total(at)
        rows = mid[at, :]
        inverse = inverse_rms(rows)
        normed_rows = rows * inverse
        product = grad * normed_rows
        grad_gain[...] += product[:8] + product[8:]
        inner = jnp.mean(product * gain[...], axis=-1, keepdims=True)
        own_cot = cot[tensor, k // 2, pl.ds(pl.multiple_of((k % 2) * 16, 16), 16), :].astype(f32)
        result = own_cot + inverse * (grad * gain[...] - normed_rows * inner)
        grad_mid[at, :] = result
        branch[at, :] = result.astype(bf16)
        return carry

    lax.fori_loop(0, 6, chunk, 0)


def feed_forward(own, cotangent, weights, mid, gain):
    rows, width = mid.shape
    units = weights.shape[3] // 3
    dma = pltpu.SemaphoreType.DMA
    return pl.pallas_call(
        feed_forward_kernel,
        out_shape=(
            jax.ShapeDtypeStruct((rows, width), bf16),
            jax.ShapeDtypeStruct((rows, width), f32),
            jax.ShapeDtypeStruct((8, width), f32),
            jax.ShapeDtypeStruct((8, rows, width), bf16),
            jax.ShapeDtypeStruct((8, 2) + weights.shape[2:], bf16),
        ),
        in_specs=[VMEM, ANY, ANY, VMEM, VMEM],
        out_specs=(VMEM, VMEM, VMEM, ANY, ANY),
        scratch_shapes=[
            pltpu.VMEM((2, 8, 128, 2 * units), bf16),
            pltpu.VMEM((2, 8, 128, units), bf16),
            pltpu.VMEM((8, 3, 32, width), bf16),
            pltpu.VMEM((8, rows, width), bf16),
            pltpu.VMEM((8, rows, units), f32),
            pltpu.VMEM((8, rows, 2 * units), bf16),
            pltpu.VMEM((8, rows, units), bf16),
            pltpu.VMEM((4, 2, rows, width), bf16),
            *fold_scratch((), rows, width),
            pltpu.VMEM((8, rows, width), bf16),
            pltpu.VMEM((2, 2, 128, 3 * units), bf16),
            dma((9,)), dma((9,)), dma((11,)), dma((11,)), dma((2,)), dma((8,)), dma((2,)), dma,
        ],
        compiler_params=params(5, 60),
        cost_estimate=pl.CostEstimate(
            flops=18 * 8 * rows * width * units, bytes_accessed=120 * MIB, transcendentals=0
        ),
        name="feed_forward",
    )(own, cotangent, weights, mid, gain)


def backward_kernel(
    branch, query_hbm, pairs_hbm, kept_hbm, mixed_hbm, packed_hbm, first_hbm, mlp_part, mid_hbm,
    cos_table, sin_table,
    part, ready, block_out,
    query, pairs, kept, mixed, packed, h_first, mid,
    whole, attended, raw, grad_pairs, near_pairs, ready_pairs, landed_pairs, bias, total, weights,
    near, mlp_own, mlp_pair, over_z, from_partner, ready_rows, second, own_first, last_first,
    out_sends, out_recvs, pair_near_sends, pair_near_recvs, pair_sends, pair_recvs, near_sends,
    near_recvs, mlp_sends, mlp_recvs, local,
):
    dp, seq, tensor = lax.axis_index("dp"), lax.axis_index("seq"), lax.axis_index("tensor")
    x, core = seq // 2, seq % 2
    peers = tensor_peers()
    rows_beside = row_peers()
    beside = {"seq": sibling()}
    z, y = tensor // 2, tensor % 2
    count, width = whole.shape[0], whole.shape[2]
    rows, keys = bias.shape
    loads = [
        pltpu.make_async_copy(source, place, local.at[k])
        for k, (source, place) in enumerate(
            (
                (packed_hbm, packed),
                (pairs_hbm, pairs),
                (query_hbm, query),
                (kept_hbm, kept),
                (mixed_hbm, mixed),
                (first_hbm, h_first),
                (mid_hbm, mid),
                (mlp_part.at[:, y], mlp_own),
                (mlp_part.at[z, 1 - y], mlp_pair),
            )
        )
    ]
    for copy in loads:
        copy.start()
    greet(
        [{"tensor": peer} for peer in peers]
        + [{"seq": 2 * px + c} for px, c in rows_beside]
        + [beside]
    )
    mine = pl.ds(pl.multiple_of(tensor * 32, 32), 32)
    spread = [
        remote(
            branch.at[pl.ds(32 * i, 32)], whole.at[i, mine], out_sends, out_recvs, 7 * i + k,
            {"tensor": peer},
        )
        for i in range(count)
        for k, peer in enumerate(peers)
    ]
    for copy in spread:
        copy.start()

    def mlp_term(dz, dy, at):
        rows_here = mlp_pair[at, :] if dy else mlp_own[(z + dz) % 4, at, :]
        return rows_here.astype(f32)

    fold = Fold(
        mlp_part,
        mlp_term,
        (over_z, from_partner, ready_rows, second, own_first, last_first),
        mlp_sends,
        mlp_recvs,
        0,
    )
    for dz in (2, 1, 3, 0):
        fold.begin(dz)
    for i in range(count):
        whole[i, mine, :] = branch[32 * i : 32 * i + 32, :]
    causal_bias(bias)
    for copy in loads:
        copy.wait()
    lane = lax.broadcasted_iota(jnp.int32, (rows, 2 * HEAD_SIZE), 1)
    scale = HEAD_SIZE ** (-0.5)

    def sequence(i):
        for copy in spread[7 * i : 7 * i + 7]:
            copy.wait_recv()
        attended[...] = (
            jnp.dot(
                whole[i], packed[:, :, 384:640].reshape(width, 256), preferred_element_type=f32
            )
            .astype(bf16)
            .astype(f32)
        )
        total[...] = jnp.zeros_like(total)

        def head_pair(at, carry):
            columns_at = columns(at, 2 * HEAD_SIZE)
            grads_here = attended[:, columns_at]
            grad_query = []
            for odd in range(2):
                pair = pairs[:, i].reshape(keys, 2 * HEAD_SIZE)
                placed = grads_here if odd else pltpu.roll(grads_here, HEAD_SIZE, 1)
                placed = jnp.where(lane >= HEAD_SIZE, placed, 0.0)
                grad_rows = placed.astype(bf16)
                query_rows = query[i, 2 * at + odd]
                kept_rows = kept[i, 2 * at + odd]
                probs = jnp.exp(nt(query_rows, pair) + bias[...] - kept_rows[:, :1])
                inner = jnp.sum(kept_rows * placed, axis=-1, keepdims=True)
                grad_scores = (probs * (nt(grad_rows, pair) - inner)).astype(bf16)
                grad_query.append(jnp.dot(grad_scores, pair, preferred_element_type=f32))
                total[...] += jnp.dot(
                    query_rows.T, grad_scores, preferred_element_type=f32
                ) + jnp.dot(grad_rows.T, probs.astype(bf16), preferred_element_type=f32)
            both = jnp.where(lane < HEAD_SIZE, grad_query[0], pltpu.roll(grad_query[1], HEAD_SIZE, 1))
            both = turn(both * scale, cos_table[...], sin_table[...])
            raw[i, :, columns_at] = both.astype(bf16)
            return carry

        lax.fori_loop(0, GROUP // 2, head_pair, 0)
        for block in range(8):
            grad_pairs[block // 2, block % 2, i] = (
                total[:, block * rows : (block + 1) * rows].T.astype(bf16)
            )

    def cross(i):
        copy = remote(
            grad_pairs.at[:, 1 - core, i], near_pairs.at[i], pair_near_sends, pair_near_recvs, i,
            beside,
        )
        copy.start()
        return copy

    def onward(i, crossing):
        crossing.wait()
        out = []
        for k, (px, c) in enumerate(rows_beside):
            both = grad_pairs[px, core, i].astype(f32) + near_pairs[i, px].astype(f32)
            ready_pairs[i, k] = both.astype(bf16)
            copy = remote(
                ready_pairs.at[i, k], landed_pairs.at[i, k], pair_sends, pair_recvs, 3 * i + k,
                {"seq": 2 * px + c},
            )
            copy.start()
            out.append(copy)
        return out

    def settle(i, moving):
        mine_pairs = grad_pairs[x, core, i].astype(f32) + near_pairs[i, x].astype(f32)
        for k, copy in enumerate(moving):
            copy.wait()
            mine_pairs = mine_pairs + landed_pairs[i, k].astype(f32)
        turned = turn(mine_pairs, cos_table[...], sin_table[...])
        raw[i, :, 256:] = jnp.where(lane < HEAD_SIZE, turned, mine_pairs).astype(bf16)

        def term(tile, carry):
            at = columns(tile, 512)
            weight_rows = packed[pl.ds(tile * 4, 4), :, :384].reshape(512, 384)
            product = nt(raw[i], weight_rows).astype(bf16)
            part[i, :, :, :, at] = product.reshape(4, 2, 32, 512)
            return carry

        lax.fori_loop(0, width // 512, term, 0)

    def outer(tile, carry):
        at = columns(tile, 256)
        product = tn(
            whole[:, :, at].reshape(count * rows, 256), mixed[...].reshape(count * rows, 256)
        )
        weights[tile, :, :, 256:512] = product.astype(bf16).reshape(2, 128, 256)
        return carry

    def query_weights(tile, carry):
        at = columns(tile, 256)
        product = tn(
            h_first[:, :, at].reshape(count * rows, 256), raw[:, :, :256].reshape(count * rows, 256)
        )
        weights[tile, :, :, :256] = product.astype(bf16).reshape(2, 128, 256)
        return carry

    def pair_weights(tile, carry):
        at = columns(tile, 512)
        product = tn(
            h_first[:, :, at].reshape(count * rows, 512), raw[:, :, 256:].reshape(count * rows, 128)
        )
        weights[pl.ds(2 * tile, 2), :, :, 512:] = product.astype(bf16).reshape(2, 2, 128, 128)
        return carry

    sequence(0)
    crossing = cross(0)
    sequence(1)
    moving = onward(0, crossing)
    crossing = cross(1)
    settle(0, moving)
    sequence(2)
    crossing_last = cross(2)
    moving = onward(1, crossing)
    for dz in (2, 1, 3, 0):
        fold.pass_z(dz)
    lax.fori_loop(0, width // 256, outer, 0)
    moving_last = onward(2, crossing_last)
    settle(1, moving)
    lax.fori_loop(0, width // 256, query_weights, 0)
    settle(2, moving_last)
    fold.pass_partner()
    lax.fori_loop(0, width // 512, pair_weights, 0)
    across = remote(weights.at[:, 1 - core], near, near_sends, near_recvs, 0, beside)
    across.start()
    for copy in spread:
        copy.wait_send()
    across.wait()
    for at in range(8):
        ready[at] = (weights[at, core].astype(f32) + near[at].astype(f32)).astype(bf16)
    fold.finish()

    def finish_rows(i, row):
        at = pl.ds(pl.multiple_of(i * 32 + row, 16), 16)
        result = mid[at, :] + fold.total(at)
        block_out[i, pl.ds(row, 16), :] = result.astype(bf16)

    own_chunks(finish_rows)


def backward(
    branch, query, pairs, kept, mixed, packed, h_first, mlp_part, mid, cos_table, sin_table
):
    count, rows, width = h_first.shape
    mlp_part = mlp_part.reshape((4, 2) + mlp_part.shape[1:])
    keys = pairs.shape[0] * rows
    pair_rows = (rows, 2 * HEAD_SIZE)
    own = mid.shape[0]
    dma = pltpu.SemaphoreType.DMA
    vmem = pltpu.VMEM
    return pl.pallas_call(
        backward_kernel,
        out_shape=(
            jax.ShapeDtypeStruct((count, 4, 2, 32, width), bf16),
            jax.ShapeDtypeStruct((8, 128, 640), bf16),
            jax.ShapeDtypeStruct((count, 32, width), bf16),
        ),
        in_specs=[VMEM] + [ANY] * 8 + [VMEM] * 2,
        out_specs=(VMEM,) * 3,
        scratch_shapes=[
            vmem(query.shape, bf16),
            vmem(pairs.shape, bf16),
            vmem(kept.shape, f32),
            vmem(mixed.shape, bf16),
            vmem(packed.shape, bf16),
            vmem(h_first.shape, bf16),
            vmem(mid.shape, f32),
            vmem((count, rows, width), bf16),
            vmem((rows, GROUP * HEAD_SIZE), f32),
            vmem((count, rows, 384), bf16),
            vmem((4, 2, count) + pair_rows, bf16),
            vmem((count, 4) + pair_rows, bf16),
            vmem((count, 3) + pair_rows, bf16),
            vmem((count, 3) + pair_rows, bf16),
            vmem((rows, keys), f32),
            vmem((2 * HEAD_SIZE, keys), f32),
            vmem((8, 2, 128, 640), bf16),
            vmem((8, 128, 640), bf16),
            vmem((4, own, width), bf16),
            vmem((own, width), bf16),
            *fold_scratch((), own, width),
            dma((21,)), dma((21,)), dma((3,)), dma((3,)), dma((9,)), dma((9,)), dma((1,)), dma((1,)),
            dma((11,)), dma((11,)), dma((9,)),
        ],
        compiler_params=params(7, 62),
        cost_estimate=pl.CostEstimate(flops=40000 * MIB, bytes_accessed=200 * MIB, transcendentals=0),
        name="backward",
    )(
        branch, query, pairs, kept, mixed, packed, h_first, mlp_part, mid, cos_table, sin_table
    )


def ending_kernel(
    part, weights, ff, tokens, grad_mid, gain, gain_two,
    input_grad, share_query, share_pair, share_output, gain_sum, share_gate_up, share_down,
    part_own, weights_own, ff_own, landed, ours, partner, landed_last, shares, ff_in, grads, gains, gains_in, gains_near,
    sends, recvs, last_sends, last_recvs, far_sends, far_recvs, ff_sends, ff_recvs,
    gain_sends, gain_recvs, gain_last_sends, gain_last_recvs, local,
):
    dp, seq, tensor = lax.axis_index("dp"), lax.axis_index("seq"), lax.axis_index("tensor")
    z, y = tensor // 2, tensor % 2
    peers = tensor_peers()
    chips = chip_peers()
    owners = [((dp + k // 8) % 2, (seq + k % 8) % 8) for k in range(1, 16)]
    count = part.shape[0]
    units = share_down.shape[0]
    here = dp * 4 + seq // 2
    loads = [
        pltpu.make_async_copy(source, place, local.at[k])
        for k, (source, place) in enumerate(
            ((part.at[:, z], part_own), (ff.at[0], ff_own), (weights.at[here], weights_own))
        )
    ]
    for copy in loads:
        copy.start()
    greet(
        [{"tensor": peer} for peer in peers] + [{"dp": d, "seq": s} for d, s in owners]
    )

    out = []
    for i in range(count):
        for k, dz in enumerate((2, 1, 3)):
            other = (z + dz) % 4
            copy = remote(
                part.at[i, other], landed.at[i, k], sends, recvs, 3 * i + k,
                {"tensor": 2 * other + y},
            )
            copy.start()
            out.append(copy)
    far = [
        remote(
            weights.at[d * 4 + px], shares.at[i], far_sends, far_recvs, i,
            {"dp": d, "seq": 2 * px + c},
        )
        for i, (d, px, c) in enumerate(chips)
    ]
    for copy in far:
        copy.start()
    swap = remote(ff.at[1], ff_in, ff_sends, ff_recvs, 0, {"dp": 1 - dp})
    swap.start()
    for copy in loads:
        copy.wait()
    grads[...] = jnp.zeros_like(grads)

    def collect(i):
        for copy in out[3 * i : 3 * i + 3]:
            copy.wait()

        def step(k, carry):
            row = pl.multiple_of(k * 16, 16)
            for own in (False, True):
                side = y if own else 1 - y
                at = pl.ds(row, 16)
                result = part_own[i, side, at, :].astype(f32)
                for j in range(3):
                    result = result + landed[i, j, side, at, :].astype(f32)
                if own:
                    ours[i, pl.ds(row, 16), :] = result
                else:
                    partner[i, pl.ds(row, 16), :] = result.astype(bf16)
            return carry

        lax.fori_loop(0, 2, step, 0)
        copy = remote(
            partner.at[i], landed_last.at[i], last_sends, last_recvs, i, {"tensor": 2 * z + 1 - y}
        )
        copy.start()
        return copy

    def conclude(i, copy):
        copy.wait()

        def step(k, carry):
            row = pl.ds(pl.multiple_of(k * 16, 16), 16)
            grad = ours[i, row, :] + landed_last[i, row, :].astype(f32)
            token_rows = tokens[i, row, :].astype(f32)
            inverse = inverse_rms(token_rows)
            normed = token_rows * inverse
            product = grad * normed
            grads[...] += product[:8] + product[8:]
            inner = jnp.mean(product * gain[...], axis=-1, keepdims=True)
            at = pl.ds(pl.multiple_of(i * 32 + k * 16, 16), 16)
            result = grad_mid[at, :] + inverse * (grad * gain[...] - normed * inner)
            input_grad[i, row, :] = result.astype(bf16)
            return carry

        lax.fori_loop(0, 2, step, 0)

    first = collect(0)
    second = collect(1)
    conclude(0, first)
    third = collect(2)
    conclude(1, second)
    conclude(2, third)
    gains[...] = jnp.zeros_like(gains)
    gains[0:1, :] = jnp.sum(grads[...], axis=0, keepdims=True)
    gains[1:2, :] = jnp.sum(gain_two[...], axis=0, keepdims=True)
    spread_gains = []
    for k, (d, s) in enumerate(owners):
        at = pl.ds(pl.multiple_of((d * 8 + s) * 128, 128), 128)
        copy = remote(gains.at[:, at], gains_in.at[k], gain_sends, gain_recvs, k, {"dp": d, "seq": s})
        copy.start()
        spread_gains.append(copy)
    own = gains[:, pl.ds(pl.multiple_of((dp * 8 + seq) * 128, 128), 128)]
    swap.wait()
    for tile in range(8):
        at = slice(128 * tile, 128 * tile + 128)
        share_gate_up[0, :, at] = ff_own[:, at].astype(f32) + ff_in[:, at].astype(f32)
        up_at = slice(units + 128 * tile, units + 128 * tile + 128)
        share_gate_up[1, :, at] = ff_own[:, up_at].astype(f32) + ff_in[:, up_at].astype(f32)
    for k, copy in enumerate(spread_gains):
        copy.wait()
        own = own + gains_in[k]
    gains_near[7] = own
    last = [
        remote(gains_near.at[7], gains_near.at[i], gain_last_sends, gain_last_recvs, i, {"tensor": peer})
        for i, peer in enumerate(peers)
    ]
    for copy in last:
        copy.start()
    for tile in range(8):
        at = slice(128 * tile, 128 * tile + 128)
        down_at = slice(2 * units + 128 * tile, 2 * units + 128 * tile + 128)
        both = ff_own[:, down_at].astype(f32) + ff_in[:, down_at].astype(f32)
        share_down[at, :] = both.T
    for copy in far:
        copy.wait()
    sums = weights_own[...].astype(f32)
    for i in range(7):
        sums = sums + shares[i].astype(f32)
    share_query[...] = sums[:, :256]
    share_pair[...] = sums[:, 512:]
    share_output[...] = sums[:, 256:512].T
    for copy in last:
        copy.wait()
    shifts = ((2, 1), (1, 1), (3, 1), (2, 0), (1, 0), (3, 0), (0, 1))
    sums = jnp.zeros_like(own)
    for t in range(8):
        slot = jnp.int32(7)
        for i, (dz, dy) in enumerate(shifts):
            source = ((z + 4 - dz) % 4) * 2 + (y + dy) % 2
            slot = jnp.where(source == t, i, slot)
        sums = sums + gains_near[slot]
    gain_sum[...] = sums[0:2, :]


def ending(part, weights, ff, tokens, grad_mid, gain, gain_two):
    count, width = part.shape[0], part.shape[4]
    units = ff.shape[2] // 3
    dma = pltpu.SemaphoreType.DMA
    vmem = pltpu.VMEM
    return pl.pallas_call(
        ending_kernel,
        out_shape=(
            jax.ShapeDtypeStruct((count, 32, width), bf16),
            jax.ShapeDtypeStruct((128, 256), f32),
            jax.ShapeDtypeStruct((128, 128), f32),
            jax.ShapeDtypeStruct((256, 128), f32),
            jax.ShapeDtypeStruct((2, 128), f32),
            jax.ShapeDtypeStruct((2, 128, units), f32),
            jax.ShapeDtypeStruct((units, 128), f32),
        ),
        in_specs=[ANY] * 3 + [VMEM] * 4,
        out_specs=(VMEM,) * 7,
        scratch_shapes=[
            vmem((count, 2, 32, width), bf16),
            vmem((128, 640), bf16),
            vmem((128, 3 * units), bf16),
            vmem((count, 3, 2, 32, width), bf16),
            vmem((count, 32, width), f32),
            vmem((count, 32, width), bf16),
            vmem((count, 32, width), bf16),
            vmem((7, 128, 640), bf16),
            vmem((128, 3 * units), bf16),
            vmem((8, width), f32),
            vmem((8, width), f32),
            vmem((15, 8, 128), f32),
            vmem((8, 8, 128), f32),
            dma((9,)), dma((9,)), dma((3,)), dma((3,)), dma((7,)), dma((7,)), dma((1,)), dma((1,)),
            dma((15,)), dma((15,)), dma((7,)), dma((7,)), dma((3,)),
        ],
        compiler_params=params(2, 48),
        cost_estimate=pl.CostEstimate(flops=MIB, bytes_accessed=150 * MIB, transcendentals=0),
        name="ending",
    )(part, weights, ff, tokens, grad_mid, gain, gain_two)


def shards(
    tokens,
    cotangent,
    query_weight,
    query_first,
    query_second,
    key_value_weight,
    key_value_first_moment,
    key_value_second_moment,
    output_weight,
    output_first,
    output_second,
    gate_up_weight,
    gate_up_first,
    gate_up_second,
    down_weight,
    down_first,
    down_second,
    norm_gains,
    gains_first,
    gains_second,
):
    count, local_len, width = tokens.shape
    tensor = lax.axis_index("tensor")

    def own_rows(values):
        return lax.dynamic_slice_in_dim(values, tensor * 32, 32, 1)

    packed = jnp.concatenate(
        [
            query_weight,
            key_value_weight.reshape(128, 2 * HEAD_SIZE),
            output_weight.T,
        ],
        axis=1,
    ).astype(bf16)
    ff_low = jnp.concatenate(
        [gate_up_weight[0], gate_up_weight[1], down_weight.T], axis=1
    ).astype(bf16)
    gains_low = jnp.pad(norm_gains.astype(bf16).astype(f32), ((0, 6), (0, 0)))
    positions = lax.axis_index("seq") * local_len + jnp.arange(local_len, dtype=jnp.int32)
    cos_table, sin_table = rotary(positions)
    cos_wide = jnp.tile(cos_table, (1, 4))
    sin_wide = jnp.tile(jnp.concatenate([sin_table, -sin_table], axis=1), (1, 2))
    query, pairs, kept, mixed, packed_all, h_first, mid, h_second, ff_all, gains_used = forward(
        tokens, packed, gains_low, ff_low, cos_wide, sin_wide
    )
    branch_own, grad_mid, gain_two, mlp_term, grads = feed_forward(
        h_second,
        cotangent.reshape(count, 8, 32, width),
        ff_all,
        mid,
        gains_used[1:2],
    )
    shares_ff = lax.psum_scatter(grads, "seq", scatter_dimension=0, tiled=False)
    part, grads_projection, block_out = backward(
        branch_own,
        query,
        pairs,
        kept,
        mixed,
        packed_all,
        h_first,
        mlp_term,
        mid,
        cos_wide,
        sin_wide,
    )
    (
        input_grad,
        share_query,
        share_pair,
        share_output,
        share_gains,
        share_gate_up,
        share_down,
    ) = ending(
        part,
        grads_projection,
        shares_ff,
        own_rows(tokens),
        grad_mid,
        gains_used[:1],
        gain_two,
    )

    query_new, query_first_new, query_second_new = adam(
        query_weight, share_query, query_first, query_second, rate_wide, weight_decay
    )
    pair_new, pair_first_new, pair_second_new = adam(
        key_value_weight,
        share_pair[:, None, :],
        key_value_first_moment,
        key_value_second_moment,
        rate_wide,
        weight_decay,
    )
    output_new, output_first_new, output_second_new = adam(
        output_weight,
        share_output,
        output_first,
        output_second,
        rate_output,
        weight_decay,
    )
    gate_up_new, gate_up_first_new, gate_up_second_new = adam(
        gate_up_weight,
        share_gate_up,
        gate_up_first,
        gate_up_second,
        rate_wide,
        weight_decay,
    )
    down_new, down_first_new, down_second_new = adam(
        down_weight, share_down, down_first, down_second, rate_down, weight_decay
    )
    gains_new, gains_first_new, gains_second_new = adam(
        norm_gains, share_gains, gains_first, gains_second, rate_gains, 0.0
    )
    return (
        block_out,
        input_grad,
        query_new,
        query_first_new,
        query_second_new,
        pair_new,
        pair_first_new,
        pair_second_new,
        output_new,
        output_first_new,
        output_second_new,
        gate_up_new,
        gate_up_first_new,
        gate_up_second_new,
        down_new,
        down_first_new,
        down_second_new,
        gains_new,
        gains_first_new,
        gains_second_new,
    )


def solution(mesh):
    return jax.shard_map(
        shards,
        mesh=mesh,
        in_specs=(
            P("dp", "seq", None),
            P("dp", "seq", None),
            P(("dp", "seq"), "tensor"),
            P(("dp", "seq"), "tensor"),
            P(("dp", "seq"), "tensor"),
            P(("dp", "seq"), "tensor", None),
            P(("dp", "seq"), "tensor", None),
            P(("dp", "seq"), "tensor", None),
            P("tensor", ("dp", "seq")),
            P("tensor", ("dp", "seq")),
            P("tensor", ("dp", "seq")),
            P(None, ("dp", "seq"), "tensor"),
            P(None, ("dp", "seq"), "tensor"),
            P(None, ("dp", "seq"), "tensor"),
            P("tensor", ("dp", "seq")),
            P("tensor", ("dp", "seq")),
            P("tensor", ("dp", "seq")),
            P(None, ("dp", "seq")),
            P(None, ("dp", "seq")),
            P(None, ("dp", "seq")),
        ),
        out_specs=(
            P("dp", ("seq", "tensor"), None),
            P("dp", ("seq", "tensor"), None),
            P(("dp", "seq"), "tensor"),
            P(("dp", "seq"), "tensor"),
            P(("dp", "seq"), "tensor"),
            P(("dp", "seq"), "tensor", None),
            P(("dp", "seq"), "tensor", None),
            P(("dp", "seq"), "tensor", None),
            P("tensor", ("dp", "seq")),
            P("tensor", ("dp", "seq")),
            P("tensor", ("dp", "seq")),
            P(None, ("dp", "seq"), "tensor"),
            P(None, ("dp", "seq"), "tensor"),
            P(None, ("dp", "seq"), "tensor"),
            P("tensor", ("dp", "seq")),
            P("tensor", ("dp", "seq")),
            P("tensor", ("dp", "seq")),
            P(None, ("dp", "seq")),
            P(None, ("dp", "seq")),
            P(None, ("dp", "seq")),
        ),
        check_vma=False,
    )
```

```python
import jax
import jax.numpy as jnp
from jax import lax
from jax.experimental import pallas as pl
from jax.experimental.pallas import tpu as pltpu
from jax.sharding import PartitionSpec as P

QUERY_HEADS = 32
KEY_VALUE_HEADS = 8
HEAD_SIZE = 64
STEP = 10
GROUP = QUERY_HEADS // KEY_VALUE_HEADS


norm_eps = 1e-05
rope_base = 500000.0
beta_first = 0.9
beta_second = 0.95
adam_eps = 1e-08
weight_decay = 0.1
rate_wide = 0.07
rate_down = 0.035
rate_output = 1.0
rate_gains = 0.7

bf16 = jnp.bfloat16
f32 = jnp.float32
MESH = pl.DeviceIdType.MESH
VMEM = pl.BlockSpec(memory_space=pltpu.VMEM)
ANY = pl.BlockSpec(memory_space=pl.ANY)
MIB = 1024 * 1024


def inverse_rms(values):
    return lax.rsqrt(jnp.mean(values * values, axis=-1, keepdims=True) + norm_eps)


def rotary(positions):
    half_size = HEAD_SIZE // 2
    lane = jnp.arange(2 * HEAD_SIZE, dtype=jnp.int32)
    freqs = rope_base ** (-2.0 * (lane % half_size).astype(jnp.float32) / HEAD_SIZE)
    angles = positions.astype(jnp.float32)[:, None] * freqs[None, :]
    signs = jnp.where(lane % HEAD_SIZE < half_size, 1.0, -1.0)
    return (jnp.cos(angles), jnp.sin(angles) * signs[None, :])


def adam(master, grad, moment_one, moment_two, rate, decay):
    new_one = beta_first * moment_one + (1.0 - beta_first) * grad
    new_two = beta_second * moment_two + (1.0 - beta_second) * grad * grad
    ahead = (
        new_one
        / (1.0 - beta_first**STEP)
        / (jnp.sqrt(new_two / (1.0 - beta_second**STEP)) + adam_eps)
    )
    return (master - rate * (ahead + decay * master), new_one, new_two)


def tensor_peers():
    me = lax.axis_index("tensor")
    z, y = me // 2, me % 2
    return [
        ((z + dz) % 4) * 2 + (y + dy) % 2
        for dz, dy in ((2, 1), (1, 1), (3, 1), (2, 0), (1, 0), (3, 0), (0, 1))
    ]


def chip_peers():
    dp, seq = lax.axis_index("dp"), lax.axis_index("seq")
    x, core = seq // 2, seq % 2
    return [
        ((dp + dd) % 2, (x + dx) % 4, core)
        for dx, dd in ((2, 1), (1, 1), (3, 1), (0, 1), (2, 0), (1, 0), (3, 0))
    ]


def row_peers():
    seq = lax.axis_index("seq")
    x, core = seq // 2, seq % 2
    return [((x + dx) % 4, core) for dx in (2, 1, 3)]


def sibling():
    seq = lax.axis_index("seq")
    return seq + 1 - 2 * (seq % 2)


def greet(devices):
    barrier = pltpu.get_barrier_semaphore()
    for device in devices:
        pl.semaphore_signal(barrier, inc=1, device_id=device, device_id_type=MESH)
    pl.semaphore_wait(barrier, len(devices))


def remote(src, dst, sends, recvs, at, device):
    return pltpu.make_async_remote_copy(src, dst, sends.at[at], recvs.at[at], device, MESH)


def params(collective_id, mib):
    return pltpu.CompilerParams(
        collective_id=collective_id, has_side_effects=True, vmem_limit_bytes=mib * MIB
    )


def causal_bias(bias):
    seq = lax.axis_index("seq")
    rows, keys = bias.shape
    row = lax.broadcasted_iota(jnp.int32, (rows, keys), 0) + seq * rows
    key = lax.broadcasted_iota(jnp.int32, (rows, keys), 1)
    bias[...] = jnp.where(key <= row, 0.0, -1e30).astype(f32)


def nt(left, right):
    return lax.dot_general(left, right, (((1,), (1,)), ((), ())), preferred_element_type=f32)


def tn(left, right):
    return lax.dot_general(left, right, (((0,), (0,)), ((), ())), preferred_element_type=f32)


def columns(tile, size):
    return pl.ds(pl.multiple_of(tile * size, size), size)


def turn(values, cos_table, sin_table):
    lane = lax.broadcasted_iota(jnp.int32, values.shape, 1)
    half = HEAD_SIZE // 2
    other = jnp.where(
        lane % HEAD_SIZE < half,
        pltpu.roll(values, values.shape[1] - half, 1),
        pltpu.roll(values, half, 1),
    )
    return values * cos_table + other * sin_table


def block_of(peer):
    return pl.ds(pl.multiple_of(peer * 32, 32), 32)


def own_chunks(body):
    def step(k, carry):
        body(k // 2, pl.multiple_of((k % 2) * 16, 16))
        return carry

    lax.fori_loop(0, 6, step, 0)


FIRST = 896
SHIFTS = (2, 1, 3)


def fold_scratch(lead, rows, width):
    rest = width - FIRST
    return [
        pltpu.VMEM(lead + shape, bf16)
        for shape in (
            (3, 2, rows, FIRST),
            (4, rows, rest),
            (3, rows, rest),
            (3, rows, rest),
            (rows, FIRST),
            (rows, FIRST),
        )
    ]


class Fold:
    def __init__(self, source, local, refs, sends, recvs, base):
        tensor = lax.axis_index("tensor")
        self.z, self.y = tensor // 2, tensor % 2
        self.source, self.local = source, local
        self.over_z, self.from_partner, self.ready, self.second, self.mine, self.last = refs
        self.rows, self.width = self.from_partner.shape[1], FIRST + self.from_partner.shape[2]
        self.sends, self.recvs, self.base = sends, recvs, base
        self.copies = {}

    def send(self, k, source, place, z, y):
        copy = remote(
            source, place, self.sends, self.recvs, self.base + k, {"tensor": 2 * (z % 4) + y}
        )
        copy.start()
        self.copies[k] = copy

    def begin(self, dz):
        to = (self.z + dz) % 4
        first, rest = pl.ds(0, FIRST), pl.ds(FIRST, self.width - FIRST)
        if dz:
            k = SHIFTS.index(dz)
            self.send(k, self.source.at[to, :, :, first], self.over_z.at[k], to, self.y)
        self.send(
            3 + dz, self.source.at[to, 1 - self.y, :, rest], self.from_partner.at[dz], self.z,
            1 - self.y,
        )

    def chunks(self, body):
        def step(k, carry):
            body(pl.ds(pl.multiple_of(k * 16, 16), 16))
            return carry

        lax.fori_loop(0, self.rows // 16, step, 0)

    def pass_z(self, dz):
        self.copies[3 + dz].wait_recv()
        if dz == 0:
            return
        k = SHIFTS.index(dz)

        def body(at):
            both = self.local(dz, 0, at)[:, FIRST:] + self.from_partner[dz, at, :].astype(f32)
            self.ready[k, at, :] = both.astype(bf16)

        self.chunks(body)
        self.send(8 + k, self.ready.at[k], self.second.at[k], self.z + dz, self.y)

    def pass_partner(self):
        for k in range(3):
            self.copies[k].wait_recv()

        def body(at):
            result = self.local(0, 1, at)[:, :FIRST]
            for k in range(3):
                result = result + self.over_z[k, 1 - self.y, at, :].astype(f32)
            self.mine[at, :] = result.astype(bf16)

        self.chunks(body)
        self.send(7, self.mine, self.last, self.z, 1 - self.y)

    def finish(self):
        for k in (7, 8, 9, 10):
            self.copies[k].wait_recv()
        for copy in self.copies.values():
            copy.wait_send()

    def total(self, at):
        own = self.local(0, 0, at)
        low = own[:, :FIRST] + self.last[at, :].astype(f32)
        high = own[:, FIRST:] + self.from_partner[0, at, :].astype(f32)
        for k in range(3):
            low = low + self.over_z[k, self.y, at, :].astype(f32)
            high = high + self.second[k, at, :].astype(f32)
        return jnp.concatenate([low, high], axis=1)


class Weights:
    def __init__(self, mine, whole, sends, recvs, near_sends, near_recvs):
        self.dp, self.seq = lax.axis_index("dp"), lax.axis_index("seq")
        self.mine, self.whole = mine, whole
        self.sends, self.recvs = sends, recvs
        self.near_sends, self.near_recvs = near_sends, near_recvs
        self.started, self.passed = {}, []

    def owner(self, dx, dd):
        x, core = self.seq // 2, self.seq % 2
        return (self.dp + dd) % 2, ((x + dx) % 4) * 2 + core

    def device(self, dx, dd):
        dp, seq = self.owner(dx, dd)
        return {"dp": dp, "seq": seq}

    def view(self, dx, dd, half=None):
        ref = self.whole.at[self.owner(dx, dd)]
        return ref if half is None else ref.at[pl.ds(64 * half, 64)]

    def send(self, k, block, to, half=None):
        place = self.view(*block, half)
        source = place
        if block == (0, 0):
            source = self.mine if half is None else self.mine.at[pl.ds(64 * half, 64)]
        copy = remote(source, place, self.sends, self.recvs, k, self.device(*to))
        copy.start()
        self.started[k] = copy

    def beside(self, k, block, half=None):
        place = self.view(*block, half)
        source = self.mine if block == (0, 0) else place
        copy = remote(source, place, self.near_sends, self.near_recvs, k, {"seq": sibling()})
        copy.start()
        self.passed.append(copy)

    def start(self):
        self.send(0, (0, 0), (0, 1))
        self.send(1, (0, 0), (1, 0), 0)
        self.send(2, (0, 0), (3, 0), 0)
        self.beside(0, (0, 0))

    def rest(self):
        self.send(3, (0, 0), (1, 0), 1)
        self.send(4, (0, 0), (3, 0), 1)

    def partner(self):
        self.started[0].wait_recv()
        self.send(5, (0, 1), (1, 0))
        self.send(6, (0, 1), (3, 0))
        self.beside(1, (0, 1))

    def own_ring(self):
        self.started[1].wait_recv()
        self.send(7, (3, 0), (1, 0), 0)
        self.started[4].wait_recv()
        self.send(8, (1, 0), (3, 0), 1)
        self.started[3].wait_recv()
        self.beside(2, (3, 0))
        self.started[2].wait_recv()
        self.beside(3, (1, 0))

    def partner_ring(self):
        self.started[5].wait_recv()
        self.send(9, (3, 1), (1, 0), 0)
        self.beside(4, (3, 1))
        self.started[6].wait_recv()
        self.send(10, (1, 1), (3, 0), 1)
        self.beside(5, (1, 1))

    def finish(self):
        for k, half, dd in ((7, 0, 0), (8, 1, 0), (9, 0, 1), (10, 1, 1)):
            self.started[k].wait_recv()
            self.beside(k - 1, (2, dd), half)
        for copy in self.started.values():
            copy.wait_send()
        for copy in self.passed:
            copy.wait()


def forward_kernel(
    tokens, mine, gains_mine, ff_mine, cos_table, sin_table,
    query_out, pairs_out, kept_out, mixed_out, packed_out, first_out, mid, rows_in, ff_all, gains,
    query, pairs, kept, mixed, packed, h_first, part, over_z, from_partner, ready, second, own_first, last_first, bias,
    sends, recvs, near_sends, near_recvs, late_sends, late_recvs, late_near_sends,
    late_near_recvs, gain_sends, gain_recvs, pair_sends, pair_recvs,
    pair_near_sends, pair_near_recvs, out_sends, out_recvs, ff_sends, ff_recvs, ff_near_sends,
    ff_near_recvs, row_sends, row_recvs, local, stores,
):
    dp, seq, tensor = lax.axis_index("dp"), lax.axis_index("seq"), lax.axis_index("tensor")
    me = dp * 8 + seq
    stored = []

    def store(source, place):
        copy = pltpu.make_async_copy(source, place, stores.at[len(stored)])
        copy.start()
        stored.append(copy)

    count, rows, width = tokens.shape
    keys = bias.shape[1]
    near = {"seq": sibling()}
    owners = [((dp + k // 8) % 2, (seq + k % 8) % 8) for k in range(1, 16)]
    greet(
        [{"tensor": peer} for peer in tensor_peers()] + [{"dp": d, "seq": s} for d, s in owners]
    )
    gain_at = pl.ds(pl.multiple_of(me * 128, 128), 128)
    gain_copies = [
        remote(gains_mine, gains.at[:, gain_at], gain_sends, gain_recvs, k, {"dp": d, "seq": s})
        for k, (d, s) in enumerate(owners)
    ]
    for copy in gain_copies:
        copy.start()
    early, late = pl.ds(0, 384), pl.ds(384, 256)
    out, out_late = [
        [
            remote(
                mine.at[:, at], packed.at[me, :, at], ss, rs, i, {"dp": d, "seq": 2 * x + c}
            )
            for i, (d, x, c) in enumerate(chip_peers())
        ]
        for at, ss, rs in ((early, sends, recvs), (late, late_sends, late_recvs))
    ]
    first, first_late = [
        remote(mine.at[:, at], packed.at[me, :, at], ss, rs, 7, near)
        for at, ss, rs in (
            (early, near_sends, near_recvs),
            (late, late_near_sends, late_near_recvs),
        )
    ]
    for copy in out + [first] + out_late + [first_late]:
        copy.start()
    ff = Weights(ff_mine, ff_all, ff_sends, ff_recvs, ff_near_sends, ff_near_recvs)
    ff.start()
    store_ff = pltpu.make_async_copy(ff_mine, ff_all.at[dp, seq], local)
    store_ff.start()
    packed[me] = mine[...]
    gains[:, gain_at] = gains_mine[...]
    causal_bias(bias)
    for copy in gain_copies:
        copy.wait()

    def normalize(k, carry):
        i = k // 16
        at = pl.ds(pl.multiple_of((k % 16) * 16, 16), 16)
        token_rows = tokens[i, at, :].astype(f32)
        h_first[i, at, :] = (token_rows * inverse_rms(token_rows) * gains[0:1, :]).astype(bf16)
        return carry

    lax.fori_loop(0, count * 16, normalize, 0)
    store(h_first, first_out)

    def pass_weights(out, first, at, ss, rs):
        passed = [first]
        for i, (dd, dx) in (
            (6, (0, 1)), (5, (0, 3)), (3, (1, 0)), (4, (0, 2)), (2, (1, 1)), (1, (1, 3)), (0, (1, 2)),
        ):
            out[i].wait_recv()
            owner = (((dp + dd) % 2) * 4 + (seq // 2 + dx) % 4) * 2 + seq % 2
            block = packed.at[owner, :, at]
            copy = remote(block, block, ss, rs, i, near)
            copy.start()
            passed.append(copy)
        return passed

    for copy in pass_weights(out, first, early, near_sends, near_recvs):
        copy.wait()
    scale = HEAD_SIZE ** (-0.5)
    lane = lax.broadcasted_iota(jnp.int32, (rows, 2 * HEAD_SIZE), 1)

    def project(i, carry):
        raw = jnp.dot(
            h_first[i], packed[:, :, :384].reshape(width, 384), preferred_element_type=f32
        )
        for at in range(GROUP // 2):
            both = raw[:, at * 2 * HEAD_SIZE : (at + 1) * 2 * HEAD_SIZE]
            both = turn(both, cos_table[...], -sin_table[...]) * scale
            query[i, 2 * at] = jnp.where(lane < HEAD_SIZE, both, 0.0).astype(bf16)
            moved = pltpu.roll(both, HEAD_SIZE, 1)
            query[i, 2 * at + 1] = jnp.where(lane < HEAD_SIZE, moved, 0.0).astype(bf16)
        pair = raw[:, GROUP * HEAD_SIZE :]
        turned = turn(pair, cos_table[...], -sin_table[...])
        pairs[seq, i] = jnp.where(lane < HEAD_SIZE, turned, pair).astype(bf16)
        return carry

    lax.fori_loop(0, count, project, 0)
    pair_out = [
        remote(pairs.at[seq], pairs.at[seq], pair_sends, pair_recvs, i, {"seq": 2 * x + c})
        for i, (x, c) in enumerate(row_peers())
    ]
    for copy in pair_out:
        copy.start()
    pair_first = remote(pairs.at[seq], pairs.at[seq], pair_near_sends, pair_near_recvs, 3, near)
    pair_first.start()
    ff.rest()
    pair_passed = []
    for i, dx in ((1, 3), (2, 1), (0, 2)):
        pair_out[i].wait_recv()
        owner = ((seq // 2 + dx) % 4) * 2 + seq % 2
        forward = remote(
            pairs.at[owner], pairs.at[owner], pair_near_sends, pair_near_recvs, i, near
        )
        forward.start()
        pair_passed.append(forward)
    pair_first.wait()
    for copy in pair_passed:
        copy.wait()
    store(query, query_out)
    store(pairs, pairs_out)
    passed_late = pass_weights(out_late, first_late, late, late_near_sends, late_near_recvs)
    ff.partner()

    def attend(i):
        upper = []
        pair = pairs[:, i].reshape(keys, 2 * HEAD_SIZE)
        for head in range(GROUP):
            scores = nt(query[i, head], pair) + bias[...]
            row_max = jnp.max(scores, axis=-1, keepdims=True)
            exps = jnp.exp(scores - row_max)
            row_sum = jnp.sum(exps, axis=-1, keepdims=True)
            mix = jnp.dot(exps.astype(bf16), pair, preferred_element_type=f32) / row_sum
            kept[i, head] = jnp.where(lane < HEAD_SIZE, row_max + jnp.log(row_sum), mix)
            upper.append(mix)
        for at in range(GROUP // 2):
            low = pltpu.roll(upper[2 * at], HEAD_SIZE, 1)
            both = jnp.where(lane < HEAD_SIZE, low, upper[2 * at + 1])
            mixed[i, :, at * 2 * HEAD_SIZE : (at + 1) * 2 * HEAD_SIZE] = both.astype(bf16)

    def attend_step(i, carry):
        attend(i)
        return carry

    def output_step(i, carry):
        def term(tile, inner_carry):
            weight_rows = packed[pl.ds(tile * 4, 4), :, 384:640].reshape(512, 256)
            product = nt(mixed[i], weight_rows).astype(bf16)
            part[i, :, :, :, columns(tile, 512)] = product.reshape(4, 2, 32, 512)
            return inner_carry

        lax.fori_loop(0, width // 512, term, 0)
        return carry

    def term_of(i):
        def local(dz, dy, at):
            return part[i, (tensor // 2 + dz) % 4, (tensor + dy) % 2, at, :].astype(f32)

        return local

    folds = []
    for i in range(count):
        lax.fori_loop(i, i + 1, attend_step, 0)
        if i == 0:
            for copy in passed_late:
                copy.wait()
            store(packed, packed_out)
        lax.fori_loop(i, i + 1, output_step, 0)
        fold = Fold(
            part.at[i],
            term_of(i),
            [ref.at[i] for ref in (over_z, from_partner, ready, second, own_first, last_first)],
            out_sends,
            out_recvs,
            11 * i,
        )
        for dz in (2, 1, 3, 0):
            fold.begin(dz)
        folds.append(fold)
        if i:
            for dz in (2, 1, 3, 0):
                folds[i - 1].pass_z(dz)
        if i == 1:
            ff.own_ring()
    store(kept, kept_out)
    store(mixed, mixed_out)
    folds[0].pass_partner()
    for dz in (2, 1, 3, 0):
        folds[2].pass_z(dz)
    folds[1].pass_partner()
    ff.partner_ring()
    folds[2].pass_partner()
    for i, fold in enumerate(folds):
        fold.finish()

        def chunk(k, carry, i=i, fold=fold):
            row = pl.multiple_of(k * 16, 16)
            at = pl.ds(pl.multiple_of(tensor * 32 + row, 16), 16)
            result = fold.total(pl.ds(row, 16)) + tokens[i, at, :].astype(f32)
            at = pl.ds(pl.multiple_of(i * 32 + row, 16), 16)
            mid[at, :] = result
            rows_in[0, at, :] = (result * inverse_rms(result) * gains[1:2, :]).astype(bf16)
            return carry

        lax.fori_loop(0, 2, chunk, 0)
    z, y = tensor // 2, tensor % 2
    row_copies = [
        remote(
            rows_in.at[0], rows_in.at[k + 1], row_sends, row_recvs, k,
            {"tensor": 2 * ((z + dz) % 4) + (y + dy) % 2},
        )
        for k, (dz, dy) in enumerate(((0, 1), (1, 0), (3, 0)))
    ]
    for copy in row_copies:
        copy.start()
    for copy in out + out_late + pair_out:
        copy.wait_send()
    store_ff.wait()
    ff.finish()
    for copy in row_copies + stored:
        copy.wait()


def forward(tokens, mine, gains_mine, ff_mine, cos_table, sin_table):
    count, rows, width = tokens.shape
    dma = pltpu.SemaphoreType.DMA
    lanes = 2 * HEAD_SIZE
    return pl.pallas_call(
        forward_kernel,
        out_shape=(
            jax.ShapeDtypeStruct((count, GROUP, rows, lanes), bf16),
            jax.ShapeDtypeStruct((8, count, rows, lanes), bf16),
            jax.ShapeDtypeStruct((count, GROUP, rows, lanes), f32),
            jax.ShapeDtypeStruct((count, rows, GROUP * HEAD_SIZE), bf16),
            jax.ShapeDtypeStruct((16,) + mine.shape, bf16),
            jax.ShapeDtypeStruct((count, rows, width), bf16),
            jax.ShapeDtypeStruct((count * 32, width), f32),
            jax.ShapeDtypeStruct((4, count * 32, width), bf16),
            jax.ShapeDtypeStruct((2, 8) + ff_mine.shape, bf16),
            jax.ShapeDtypeStruct((8, width), f32),
        ),
        in_specs=[VMEM] * 6,
        out_specs=(ANY,) * 6 + (VMEM, VMEM, ANY, VMEM),
        scratch_shapes=[
            pltpu.VMEM((count, GROUP, rows, lanes), bf16),
            pltpu.VMEM((8, count, rows, lanes), bf16),
            pltpu.VMEM((count, GROUP, rows, lanes), f32),
            pltpu.VMEM((count, rows, GROUP * HEAD_SIZE), bf16),
            pltpu.VMEM((16,) + mine.shape, bf16),
            pltpu.VMEM((count, rows, width), bf16),
            pltpu.VMEM((count, 4, 2, 32, width), bf16),
            *fold_scratch((count,), 32, width),
            pltpu.VMEM((rows, 8 * rows), f32),
            dma((7,)), dma((7,)), dma((8,)), dma((8,)), dma((7,)), dma((7,)), dma((8,)), dma((8,)),
            dma((15,)), dma((15,)), dma((3,)), dma((3,)),
            dma((4,)), dma((4,)), dma((33,)), dma((33,)), dma((11,)), dma((11,)), dma((10,)),
            dma((10,)), dma((3,)), dma((3,)), dma, dma((6,)),
        ],
        compiler_params=params(1, 60),
        cost_estimate=pl.CostEstimate(flops=40000 * MIB, bytes_accessed=200 * MIB, transcendentals=0),
        name="forward",
    )(tokens, mine, gains_mine, ff_mine, cos_table, sin_table)


class Spread:
    def __init__(self, buffer, sends, recvs):
        tensor = lax.axis_index("tensor")
        self.buffer, self.sends, self.recvs = buffer, sends, recvs
        self.z, self.y = tensor // 2, tensor % 2
        self.started = {}

    def at(self, dz, dy):
        return ((self.z + dz) % 4) * 2 + (self.y + dy) % 2

    def send(self, k, block, to, half=None):
        ref = self.buffer.at[block]
        if half is not None:
            rows = self.buffer.shape[1] // 2
            ref = self.buffer.at[block, pl.ds(half * rows, rows)]
        copy = remote(ref, ref, self.sends, self.recvs, k, {"tensor": to})
        copy.start()
        self.started[k] = copy

    def pass_partner(self):
        self.send(3, self.at(0, 1), self.at(1, 0))
        self.send(4, self.at(0, 1), self.at(3, 0))

    def pass_on(self, dy):
        if dy:
            self.started[3].wait_recv()
        self.send(5 + 2 * dy, self.at(3, dy), self.at(1, 0), 0)
        if dy:
            self.started[4].wait_recv()
        self.send(6 + 2 * dy, self.at(1, dy), self.at(3, 0), 1)

    def finish(self):
        for k in range(5, 9):
            self.started[k].wait_recv()

    def drain(self):
        for copy in self.started.values():
            copy.wait_send()


def feed_forward_kernel(
    own, cotangent, weights, mid, gain,
    branch, grad_mid, grad_gain, mlp_out, grads_out,
    gate_up, down, cot, normed, grad_hidden, grad_units, hidden, second,
    over_z, from_partner, ready, second_in, own_first, last_first, mlp, grads,
    sends, recvs, back_sends, back_recvs, local, cot_sems, out_sems, mlp_sem,
):
    tensor = lax.axis_index("tensor")
    units = down.shape[3]
    width = 16 * 128
    dp = lax.axis_index("dp")
    load_down = pltpu.make_async_copy(
        weights.at[:, :, :, pl.ds(2 * units, units)], down, local.at[0]
    )
    load_gate_up = pltpu.make_async_copy(
        weights.at[:, :, :, pl.ds(0, 2 * units)], gate_up, local.at[1]
    )
    load_down.start()
    load_cot = [
        pltpu.make_async_copy(cotangent.at[:, t], cot.at[t], cot_sems.at[t]) for t in range(8)
    ]
    for copy in load_cot:
        copy.start()
    load_gate_up.start()
    greet([{"tensor": peer} for peer in tensor_peers()])
    spread = Spread(normed, sends, recvs)
    for k, (dz, dy) in enumerate(((0, 0), (0, 1), (3, 0), (1, 0))):
        normed[spread.at(dz, dy)] = own[k]
    spread.pass_partner()
    spread.pass_on(0)
    for copy in load_cot:
        copy.wait()
    load_down.wait()

    def hidden_step(tile, carry):
        at = columns(tile, 256)
        product = jnp.dot(
            cot[...].reshape(8 * 96, width),
            down[:, :, :, at].reshape(width, 256),
            preferred_element_type=f32,
        )
        grad_hidden[:, :, at] = product.reshape(8, 96, 256)
        return carry

    lax.fori_loop(0, units // 256, hidden_step, 0)
    load_gate_up.wait()

    def own_term(dz, dy, at):
        return second[(spread.z + dz) % 4, (spread.y + dy) % 2, at, :].astype(f32)

    fold = Fold(
        second,
        own_term,
        (over_z, from_partner, ready, second_in, own_first, last_first),
        back_sends,
        back_recvs,
        0,
    )

    def block(dz):
        first = ((spread.z + dz) % 4) * 2
        both = pl.ds(first, 2)

        def units_step(tile, carry):
            at = columns(tile, 256)
            up_at = pl.ds(pl.multiple_of(units + tile * 256, 256), 256)
            rows = normed[both].reshape(192, width)
            gate_columns = gate_up[:, :, :, at].reshape(width, 256)
            up_columns = gate_up[:, :, :, up_at].reshape(width, 256)
            gate_in = jnp.dot(rows, gate_columns, preferred_element_type=f32)
            up_in = jnp.dot(rows, up_columns, preferred_element_type=f32)
            grad = grad_hidden[both, :, at].reshape(192, 256)
            sigmoid = jax.nn.sigmoid(gate_in)
            silu = gate_in * sigmoid
            hidden[both, :, at] = (silu * up_in).astype(bf16).reshape(2, 96, 256)
            grad_gate = grad * up_in * sigmoid * (1.0 + gate_in * (1.0 - sigmoid))
            grad_units[both, :, at] = grad_gate.astype(bf16).reshape(2, 96, 256)
            grad_units[both, :, up_at] = (grad * silu).astype(bf16).reshape(2, 96, 256)
            return carry

        lax.fori_loop(0, units // 256, units_step, 0)

        def second_step(tile, carry):
            at = columns(tile, 512)
            rows = grad_units[both].reshape(192, 2 * units)
            weight_rows = gate_up[tile // 2, pl.ds((tile % 2) * 4, 4)].reshape(512, 2 * units)
            product = nt(rows, weight_rows).astype(bf16)
            second[first // 2, :, :, at] = product.reshape(2, 96, 512)
            return carry

        lax.fori_loop(0, width // 512, second_step, 0)
        fold.begin(dz)

    block(0)
    spread.pass_on(1)
    block(1)
    fold.pass_z(0)
    block(3)
    fold.pass_z(1)
    spread.finish()
    block(2)
    fold.pass_z(3)

    def mlp_step(tile, carry):
        at = columns(tile, 256)
        rows = hidden[...].reshape(8 * 96, units)
        weight_rows = down[tile // 4, pl.ds((tile % 4) * 2, 2)].reshape(256, units)
        mlp[:, :, at] = nt(rows, weight_rows).astype(bf16).reshape(8, 96, 256)
        return carry

    lax.fori_loop(0, width // 512, mlp_step, 0)
    fold.pass_z(2)
    lax.fori_loop(width // 512, width // 256, mlp_step, 0)
    store_mlp = pltpu.make_async_copy(mlp, mlp_out, mlp_sem)
    store_mlp.start()

    def store(tile, slot):
        place = grads_out.at[pl.ds((tile % 4) * 2, 2), (tile // 4 + dp) % 2]
        return pltpu.make_async_copy(grads.at[slot], place, out_sems.at[slot])

    def grads_pair(pair, carry):
        for slot in range(2):
            tile = 2 * pair + slot
            at = columns(tile, 256)

            @pl.when(pair > 0)
            def _():
                store(tile - 2, slot).wait()

            wide = tn(
                normed[:, :, at].reshape(8 * 96, 256), grad_units[...].reshape(8 * 96, 2 * units)
            )
            grads[slot, :, :, : 2 * units] = wide.astype(bf16).reshape(2, 128, 2 * units)
            narrow = tn(cot[:, :, :, at].reshape(8 * 96, 256), hidden[...].reshape(8 * 96, units))
            grads[slot, :, :, 2 * units :] = narrow.astype(bf16).reshape(2, 128, units)
            store(tile, slot).start()
        return carry

    tiles = width // 256
    lax.fori_loop(0, tiles // 2 - 1, grads_pair, 0)
    fold.pass_partner()
    lax.fori_loop(tiles // 2 - 1, tiles // 2, grads_pair, 0)
    for slot in range(2):
        store(tiles - 2 + slot, slot).wait()
    store_mlp.wait()
    spread.drain()
    fold.finish()
    grad_gain[...] = jnp.zeros_like(grad_gain)

    def chunk(k, carry):
        at = pl.ds(pl.multiple_of(k * 16, 16), 16)
        grad = fold.total(at)
        rows = mid[at, :]
        inverse = inverse_rms(rows)
        normed_rows = rows * inverse
        product = grad * normed_rows
        grad_gain[...] += product[:8] + product[8:]
        inner = jnp.mean(product * gain[1:2, :], axis=-1, keepdims=True)
        own_cot = cot[tensor, k // 2, pl.ds(pl.multiple_of((k % 2) * 16, 16), 16), :].astype(f32)
        result = own_cot + inverse * (grad * gain[1:2, :] - normed_rows * inner)
        grad_mid[at, :] = result
        branch[at, :] = result.astype(bf16)
        return carry

    lax.fori_loop(0, 6, chunk, 0)


def feed_forward(own, cotangent, weights, mid, gain):
    rows, width = mid.shape
    units = weights.shape[3] // 3
    dma = pltpu.SemaphoreType.DMA
    return pl.pallas_call(
        feed_forward_kernel,
        out_shape=(
            jax.ShapeDtypeStruct((rows, width), bf16),
            jax.ShapeDtypeStruct((rows, width), f32),
            jax.ShapeDtypeStruct((8, width), f32),
            jax.ShapeDtypeStruct((8, rows, width), bf16),
            jax.ShapeDtypeStruct((8, 2) + weights.shape[2:], bf16),
        ),
        in_specs=[VMEM, ANY, ANY, VMEM, VMEM],
        out_specs=(VMEM, VMEM, VMEM, ANY, ANY),
        scratch_shapes=[
            pltpu.VMEM((2, 8, 128, 2 * units), bf16),
            pltpu.VMEM((2, 8, 128, units), bf16),
            pltpu.VMEM((8, 3, 32, width), bf16),
            pltpu.VMEM((8, rows, width), bf16),
            pltpu.VMEM((8, rows, units), f32),
            pltpu.VMEM((8, rows, 2 * units), bf16),
            pltpu.VMEM((8, rows, units), bf16),
            pltpu.VMEM((4, 2, rows, width), bf16),
            *fold_scratch((), rows, width),
            pltpu.VMEM((8, rows, width), bf16),
            pltpu.VMEM((2, 2, 128, 3 * units), bf16),
            dma((9,)), dma((9,)), dma((11,)), dma((11,)), dma((2,)), dma((8,)), dma((2,)), dma,
        ],
        compiler_params=params(5, 60),
        cost_estimate=pl.CostEstimate(
            flops=18 * 8 * rows * width * units, bytes_accessed=120 * MIB, transcendentals=0
        ),
        name="feed_forward",
    )(own, cotangent, weights, mid, gain)


def backward_kernel(
    branch, query_hbm, pairs_hbm, kept_hbm, mixed_hbm, packed_hbm, first_hbm, mlp_part, mid_hbm,
    cos_table, sin_table,
    part, ready, block_out,
    query, pairs, kept, mixed, packed, h_first, mid,
    whole, attended, raw, grad_pairs, near_pairs, ready_pairs, landed_pairs, bias, total, weights,
    near, mlp_own, mlp_pair, over_z, from_partner, ready_rows, second, own_first, last_first,
    out_sends, out_recvs, pair_near_sends, pair_near_recvs, pair_sends, pair_recvs, near_sends,
    near_recvs, mlp_sends, mlp_recvs, local,
):
    dp, seq, tensor = lax.axis_index("dp"), lax.axis_index("seq"), lax.axis_index("tensor")
    x, core = seq // 2, seq % 2
    peers = tensor_peers()
    rows_beside = row_peers()
    beside = {"seq": sibling()}
    z, y = tensor // 2, tensor % 2
    count, width = whole.shape[0], whole.shape[2]
    rows, keys = bias.shape
    loads = [
        pltpu.make_async_copy(source, place, local.at[k])
        for k, (source, place) in enumerate(
            (
                (packed_hbm, packed),
                (pairs_hbm, pairs),
                (query_hbm, query),
                (kept_hbm, kept),
                (mixed_hbm, mixed),
                (first_hbm, h_first),
                (mid_hbm, mid),
                (mlp_part.at[:, y], mlp_own),
                (mlp_part.at[z, 1 - y], mlp_pair),
            )
        )
    ]
    for copy in loads:
        copy.start()
    greet(
        [{"tensor": peer} for peer in peers]
        + [{"seq": 2 * px + c} for px, c in rows_beside]
        + [beside]
    )
    mine = pl.ds(pl.multiple_of(tensor * 32, 32), 32)
    spread = [
        remote(
            branch.at[pl.ds(32 * i, 32)], whole.at[i, mine], out_sends, out_recvs, 7 * i + k,
            {"tensor": peer},
        )
        for i in range(count)
        for k, peer in enumerate(peers)
    ]
    for copy in spread:
        copy.start()

    def mlp_term(dz, dy, at):
        rows_here = mlp_pair[at, :] if dy else mlp_own[(z + dz) % 4, at, :]
        return rows_here.astype(f32)

    fold = Fold(
        mlp_part,
        mlp_term,
        (over_z, from_partner, ready_rows, second, own_first, last_first),
        mlp_sends,
        mlp_recvs,
        0,
    )
    for dz in (2, 1, 3, 0):
        fold.begin(dz)
    for i in range(count):
        whole[i, mine, :] = branch[32 * i : 32 * i + 32, :]
    causal_bias(bias)
    for copy in loads:
        copy.wait()
    lane = lax.broadcasted_iota(jnp.int32, (rows, 2 * HEAD_SIZE), 1)
    scale = HEAD_SIZE ** (-0.5)

    def sequence(i):
        for copy in spread[7 * i : 7 * i + 7]:
            copy.wait_recv()
        attended[...] = (
            jnp.dot(
                whole[i], packed[:, :, 384:640].reshape(width, 256), preferred_element_type=f32
            )
            .astype(bf16)
            .astype(f32)
        )
        total[...] = jnp.zeros_like(total)

        def head_pair(at, carry):
            columns_at = columns(at, 2 * HEAD_SIZE)
            grads_here = attended[:, columns_at]
            grad_query = []
            for odd in range(2):
                pair = pairs[:, i].reshape(keys, 2 * HEAD_SIZE)
                placed = grads_here if odd else pltpu.roll(grads_here, HEAD_SIZE, 1)
                placed = jnp.where(lane >= HEAD_SIZE, placed, 0.0)
                grad_rows = placed.astype(bf16)
                query_rows = query[i, 2 * at + odd]
                kept_rows = kept[i, 2 * at + odd]
                probs = jnp.exp(nt(query_rows, pair) + bias[...] - kept_rows[:, :1])
                inner = jnp.sum(kept_rows * placed, axis=-1, keepdims=True)
                grad_scores = (probs * (nt(grad_rows, pair) - inner)).astype(bf16)
                grad_query.append(jnp.dot(grad_scores, pair, preferred_element_type=f32))
                total[...] += jnp.dot(
                    query_rows.T, grad_scores, preferred_element_type=f32
                ) + jnp.dot(grad_rows.T, probs.astype(bf16), preferred_element_type=f32)
            both = jnp.where(lane < HEAD_SIZE, grad_query[0], pltpu.roll(grad_query[1], HEAD_SIZE, 1))
            both = turn(both * scale, cos_table[...], sin_table[...])
            raw[i, :, columns_at] = both.astype(bf16)
            return carry

        lax.fori_loop(0, GROUP // 2, head_pair, 0)
        for block in range(8):
            grad_pairs[block // 2, block % 2, i] = (
                total[:, block * rows : (block + 1) * rows].T.astype(bf16)
            )

    def cross(i):
        copy = remote(
            grad_pairs.at[:, 1 - core, i], near_pairs.at[i], pair_near_sends, pair_near_recvs, i,
            beside,
        )
        copy.start()
        return copy

    def onward(i, crossing):
        crossing.wait()
        out = []
        for k, (px, c) in enumerate(rows_beside):
            both = grad_pairs[px, core, i].astype(f32) + near_pairs[i, px].astype(f32)
            ready_pairs[i, k] = both.astype(bf16)
            copy = remote(
                ready_pairs.at[i, k], landed_pairs.at[i, k], pair_sends, pair_recvs, 3 * i + k,
                {"seq": 2 * px + c},
            )
            copy.start()
            out.append(copy)
        return out

    def settle(i, moving):
        mine_pairs = grad_pairs[x, core, i].astype(f32) + near_pairs[i, x].astype(f32)
        for k, copy in enumerate(moving):
            copy.wait()
            mine_pairs = mine_pairs + landed_pairs[i, k].astype(f32)
        turned = turn(mine_pairs, cos_table[...], sin_table[...])
        raw[i, :, 256:] = jnp.where(lane < HEAD_SIZE, turned, mine_pairs).astype(bf16)

        def term(tile, carry):
            at = columns(tile, 512)
            weight_rows = packed[pl.ds(tile * 4, 4), :, :384].reshape(512, 384)
            product = nt(raw[i], weight_rows).astype(bf16)
            part[i, :, :, :, at] = product.reshape(4, 2, 32, 512)
            return carry

        lax.fori_loop(0, width // 512, term, 0)

    def outer(tile, carry):
        at = columns(tile, 256)
        product = tn(
            whole[:, :, at].reshape(count * rows, 256), mixed[...].reshape(count * rows, 256)
        )
        weights[tile, :, :, 256:512] = product.astype(bf16).reshape(2, 128, 256)
        return carry

    def query_weights(tile, carry):
        at = columns(tile, 256)
        product = tn(
            h_first[:, :, at].reshape(count * rows, 256), raw[:, :, :256].reshape(count * rows, 256)
        )
        weights[tile, :, :, :256] = product.astype(bf16).reshape(2, 128, 256)
        return carry

    def pair_weights(tile, carry):
        at = columns(tile, 512)
        product = tn(
            h_first[:, :, at].reshape(count * rows, 512), raw[:, :, 256:].reshape(count * rows, 128)
        )
        weights[pl.ds(2 * tile, 2), :, :, 512:] = product.astype(bf16).reshape(2, 2, 128, 128)
        return carry

    sequence(0)
    crossing = cross(0)
    sequence(1)
    moving = onward(0, crossing)
    crossing = cross(1)
    settle(0, moving)
    sequence(2)
    crossing_last = cross(2)
    moving = onward(1, crossing)
    for dz in (2, 1, 3, 0):
        fold.pass_z(dz)
    lax.fori_loop(0, width // 256, outer, 0)
    moving_last = onward(2, crossing_last)
    settle(1, moving)
    lax.fori_loop(0, width // 256, query_weights, 0)
    settle(2, moving_last)
    fold.pass_partner()
    lax.fori_loop(0, width // 512, pair_weights, 0)
    across = remote(weights.at[:, 1 - core], near, near_sends, near_recvs, 0, beside)
    across.start()
    for copy in spread:
        copy.wait_send()
    across.wait()
    for at in range(8):
        ready[at] = (weights[at, core].astype(f32) + near[at].astype(f32)).astype(bf16)
    fold.finish()

    def finish_rows(i, row):
        at = pl.ds(pl.multiple_of(i * 32 + row, 16), 16)
        result = mid[at, :] + fold.total(at)
        block_out[i, pl.ds(row, 16), :] = result.astype(bf16)

    own_chunks(finish_rows)


def backward(
    branch, query, pairs, kept, mixed, packed, h_first, mlp_part, mid, cos_table, sin_table
):
    count, rows, width = h_first.shape
    mlp_part = mlp_part.reshape((4, 2) + mlp_part.shape[1:])
    keys = pairs.shape[0] * rows
    pair_rows = (rows, 2 * HEAD_SIZE)
    own = mid.shape[0]
    dma = pltpu.SemaphoreType.DMA
    vmem = pltpu.VMEM
    return pl.pallas_call(
        backward_kernel,
        out_shape=(
            jax.ShapeDtypeStruct((count, 4, 2, 32, width), bf16),
            jax.ShapeDtypeStruct((8, 128, 640), bf16),
            jax.ShapeDtypeStruct((count, 32, width), bf16),
        ),
        in_specs=[VMEM] + [ANY] * 8 + [VMEM] * 2,
        out_specs=(VMEM,) * 3,
        scratch_shapes=[
            vmem(query.shape, bf16),
            vmem(pairs.shape, bf16),
            vmem(kept.shape, f32),
            vmem(mixed.shape, bf16),
            vmem(packed.shape, bf16),
            vmem(h_first.shape, bf16),
            vmem(mid.shape, f32),
            vmem((count, rows, width), bf16),
            vmem((rows, GROUP * HEAD_SIZE), f32),
            vmem((count, rows, 384), bf16),
            vmem((4, 2, count) + pair_rows, bf16),
            vmem((count, 4) + pair_rows, bf16),
            vmem((count, 3) + pair_rows, bf16),
            vmem((count, 3) + pair_rows, bf16),
            vmem((rows, keys), f32),
            vmem((2 * HEAD_SIZE, keys), f32),
            vmem((8, 2, 128, 640), bf16),
            vmem((8, 128, 640), bf16),
            vmem((4, own, width), bf16),
            vmem((own, width), bf16),
            *fold_scratch((), own, width),
            dma((21,)), dma((21,)), dma((3,)), dma((3,)), dma((9,)), dma((9,)), dma((1,)), dma((1,)),
            dma((11,)), dma((11,)), dma((9,)),
        ],
        compiler_params=params(7, 62),
        cost_estimate=pl.CostEstimate(flops=40000 * MIB, bytes_accessed=200 * MIB, transcendentals=0),
        name="backward",
    )(
        branch, query, pairs, kept, mixed, packed, h_first, mlp_part, mid, cos_table, sin_table
    )


def ending_kernel(
    part, weights, ff, tokens_hbm, grad_mid_hbm, gain, gain_two,
    input_grad, share_query, share_pair, share_output, gain_sum, share_gate_up, share_down,
    part_own, weights_own, ff_own, tokens, grad_mid, landed, ours, partner, landed_last, shares, ff_in, grads, gains, gains_in, gains_near,
    sends, recvs, last_sends, last_recvs, far_sends, far_recvs, ff_sends, ff_recvs,
    gain_sends, gain_recvs, gain_last_sends, gain_last_recvs, local,
):
    dp, seq, tensor = lax.axis_index("dp"), lax.axis_index("seq"), lax.axis_index("tensor")
    z, y = tensor // 2, tensor % 2
    peers = tensor_peers()
    chips = chip_peers()
    owners = [((dp + k // 8) % 2, (seq + k % 8) % 8) for k in range(1, 16)]
    count = part.shape[0]
    units = share_down.shape[0]
    here = dp * 4 + seq // 2
    loads = [
        pltpu.make_async_copy(source, place, local.at[k])
        for k, (source, place) in enumerate(
            (
                (part.at[:, z], part_own),
                (ff.at[0], ff_own),
                (weights.at[here], weights_own),
                (tokens_hbm.at[:, block_of(tensor)], tokens),
                (grad_mid_hbm, grad_mid),
            )
        )
    ]
    for copy in loads:
        copy.start()
    greet(
        [{"tensor": peer} for peer in peers] + [{"dp": d, "seq": s} for d, s in owners]
    )

    out = []
    for i in range(count):
        for k, dz in enumerate((2, 1, 3)):
            other = (z + dz) % 4
            copy = remote(
                part.at[i, other], landed.at[i, k], sends, recvs, 3 * i + k,
                {"tensor": 2 * other + y},
            )
            copy.start()
            out.append(copy)
    far = [
        remote(
            weights.at[d * 4 + px], shares.at[i], far_sends, far_recvs, i,
            {"dp": d, "seq": 2 * px + c},
        )
        for i, (d, px, c) in enumerate(chips)
    ]
    for copy in far:
        copy.start()
    swap = remote(ff.at[1], ff_in, ff_sends, ff_recvs, 0, {"dp": 1 - dp})
    swap.start()
    for copy in loads:
        copy.wait()
    grads[...] = jnp.zeros_like(grads)

    def collect(i):
        for copy in out[3 * i : 3 * i + 3]:
            copy.wait()

        def step(k, carry):
            row = pl.multiple_of(k * 16, 16)
            for own in (False, True):
                side = y if own else 1 - y
                at = pl.ds(row, 16)
                result = part_own[i, side, at, :].astype(f32)
                for j in range(3):
                    result = result + landed[i, j, side, at, :].astype(f32)
                if own:
                    ours[i, pl.ds(row, 16), :] = result
                else:
                    partner[i, pl.ds(row, 16), :] = result.astype(bf16)
            return carry

        lax.fori_loop(0, 2, step, 0)
        copy = remote(
            partner.at[i], landed_last.at[i], last_sends, last_recvs, i, {"tensor": 2 * z + 1 - y}
        )
        copy.start()
        return copy

    def conclude(i, copy):
        copy.wait()

        def step(k, carry):
            row = pl.ds(pl.multiple_of(k * 16, 16), 16)
            grad = ours[i, row, :] + landed_last[i, row, :].astype(f32)
            token_rows = tokens[i, row, :].astype(f32)
            inverse = inverse_rms(token_rows)
            normed = token_rows * inverse
            product = grad * normed
            grads[...] += product[:8] + product[8:]
            inner = jnp.mean(product * gain[0:1, :], axis=-1, keepdims=True)
            at = pl.ds(pl.multiple_of(i * 32 + k * 16, 16), 16)
            result = grad_mid[at, :] + inverse * (grad * gain[0:1, :] - normed * inner)
            input_grad[i, row, :] = result.astype(bf16)
            return carry

        lax.fori_loop(0, 2, step, 0)

    first = collect(0)
    second = collect(1)
    conclude(0, first)
    third = collect(2)
    conclude(1, second)
    conclude(2, third)
    gains[...] = jnp.zeros_like(gains)
    gains[0:1, :] = jnp.sum(grads[...], axis=0, keepdims=True)
    gains[1:2, :] = jnp.sum(gain_two[...], axis=0, keepdims=True)
    spread_gains = []
    for k, (d, s) in enumerate(owners):
        at = pl.ds(pl.multiple_of((d * 8 + s) * 128, 128), 128)
        copy = remote(gains.at[:, at], gains_in.at[k], gain_sends, gain_recvs, k, {"dp": d, "seq": s})
        copy.start()
        spread_gains.append(copy)
    own = gains[:, pl.ds(pl.multiple_of((dp * 8 + seq) * 128, 128), 128)]
    swap.wait()
    for tile in range(8):
        at = slice(128 * tile, 128 * tile + 128)
        share_gate_up[0, :, at] = ff_own[:, at].astype(f32) + ff_in[:, at].astype(f32)
        up_at = slice(units + 128 * tile, units + 128 * tile + 128)
        share_gate_up[1, :, at] = ff_own[:, up_at].astype(f32) + ff_in[:, up_at].astype(f32)
    for k, copy in enumerate(spread_gains):
        copy.wait()
        own = own + gains_in[k]
    gains_near[7] = own
    last = [
        remote(gains_near.at[7], gains_near.at[i], gain_last_sends, gain_last_recvs, i, {"tensor": peer})
        for i, peer in enumerate(peers)
    ]
    for copy in last:
        copy.start()
    for tile in range(8):
        at = slice(128 * tile, 128 * tile + 128)
        down_at = slice(2 * units + 128 * tile, 2 * units + 128 * tile + 128)
        both = ff_own[:, down_at].astype(f32) + ff_in[:, down_at].astype(f32)
        share_down[at, :] = both.T
    for copy in far:
        copy.wait()
    sums = weights_own[...].astype(f32)
    for i in range(7):
        sums = sums + shares[i].astype(f32)
    share_query[...] = sums[:, :256]
    share_pair[...] = sums[:, 512:]
    share_output[...] = sums[:, 256:512].T
    for copy in last:
        copy.wait()
    shifts = ((2, 1), (1, 1), (3, 1), (2, 0), (1, 0), (3, 0), (0, 1))
    sums = jnp.zeros_like(own)
    for t in range(8):
        slot = jnp.int32(7)
        for i, (dz, dy) in enumerate(shifts):
            source = ((z + 4 - dz) % 4) * 2 + (y + dy) % 2
            slot = jnp.where(source == t, i, slot)
        sums = sums + gains_near[slot]
    gain_sum[...] = sums[0:2, :]


def ending(part, weights, ff, tokens, grad_mid, gain, gain_two):
    count, width = part.shape[0], part.shape[4]
    units = ff.shape[2] // 3
    dma = pltpu.SemaphoreType.DMA
    vmem = pltpu.VMEM
    return pl.pallas_call(
        ending_kernel,
        out_shape=(
            jax.ShapeDtypeStruct((count, 32, width), bf16),
            jax.ShapeDtypeStruct((128, 256), f32),
            jax.ShapeDtypeStruct((128, 128), f32),
            jax.ShapeDtypeStruct((256, 128), f32),
            jax.ShapeDtypeStruct((2, 128), f32),
            jax.ShapeDtypeStruct((2, 128, units), f32),
            jax.ShapeDtypeStruct((units, 128), f32),
        ),
        in_specs=[ANY] * 5 + [VMEM] * 2,
        out_specs=(VMEM,) * 7,
        scratch_shapes=[
            vmem((count, 2, 32, width), bf16),
            vmem((128, 640), bf16),
            vmem((128, 3 * units), bf16),
            vmem((count, 32, width), bf16),
            vmem((count * 32, width), f32),
            vmem((count, 3, 2, 32, width), bf16),
            vmem((count, 32, width), f32),
            vmem((count, 32, width), bf16),
            vmem((count, 32, width), bf16),
            vmem((7, 128, 640), bf16),
            vmem((128, 3 * units), bf16),
            vmem((8, width), f32),
            vmem((8, width), f32),
            vmem((15, 8, 128), f32),
            vmem((8, 8, 128), f32),
            dma((9,)), dma((9,)), dma((3,)), dma((3,)), dma((7,)), dma((7,)), dma((1,)), dma((1,)),
            dma((15,)), dma((15,)), dma((7,)), dma((7,)), dma((5,)),
        ],
        compiler_params=params(2, 48),
        cost_estimate=pl.CostEstimate(flops=MIB, bytes_accessed=150 * MIB, transcendentals=0),
        name="ending",
    )(part, weights, ff, tokens, grad_mid, gain, gain_two)


def shards(
    tokens,
    cotangent,
    query_weight,
    query_first,
    query_second,
    key_value_weight,
    key_value_first_moment,
    key_value_second_moment,
    output_weight,
    output_first,
    output_second,
    gate_up_weight,
    gate_up_first,
    gate_up_second,
    down_weight,
    down_first,
    down_second,
    norm_gains,
    gains_first,
    gains_second,
):
    count, local_len, width = tokens.shape
    packed = jnp.concatenate(
        [
            query_weight,
            key_value_weight.reshape(128, 2 * HEAD_SIZE),
            output_weight.T,
        ],
        axis=1,
    ).astype(bf16)
    ff_low = jnp.concatenate(
        [gate_up_weight[0], gate_up_weight[1], down_weight.T], axis=1
    ).astype(bf16)
    gains_low = jnp.pad(norm_gains.astype(bf16).astype(f32), ((0, 6), (0, 0)))
    positions = lax.axis_index("seq") * local_len + jnp.arange(local_len, dtype=jnp.int32)
    cos_wide, sin_wide = rotary(positions)
    query, pairs, kept, mixed, packed_all, h_first, mid, h_second, ff_all, gains_used = forward(
        tokens, packed, gains_low, ff_low, cos_wide, sin_wide
    )
    branch_own, grad_mid, gain_two, mlp_term, grads = feed_forward(
        h_second,
        cotangent.reshape(count, 8, 32, width),
        ff_all,
        mid,
        gains_used,
    )
    shares_ff = lax.psum_scatter(grads, "seq", scatter_dimension=0, tiled=False)
    part, grads_projection, block_out = backward(
        branch_own,
        query,
        pairs,
        kept,
        mixed,
        packed_all,
        h_first,
        mlp_term,
        mid,
        cos_wide,
        sin_wide,
    )
    (
        input_grad,
        share_query,
        share_pair,
        share_output,
        share_gains,
        share_gate_up,
        share_down,
    ) = ending(
        part,
        grads_projection,
        shares_ff,
        tokens,
        grad_mid,
        gains_used,
        gain_two,
    )

    query_new, query_first_new, query_second_new = adam(
        query_weight, share_query, query_first, query_second, rate_wide, weight_decay
    )
    pair_new, pair_first_new, pair_second_new = adam(
        key_value_weight,
        share_pair[:, None, :],
        key_value_first_moment,
        key_value_second_moment,
        rate_wide,
        weight_decay,
    )
    output_new, output_first_new, output_second_new = adam(
        output_weight,
        share_output,
        output_first,
        output_second,
        rate_output,
        weight_decay,
    )
    gate_up_new, gate_up_first_new, gate_up_second_new = adam(
        gate_up_weight,
        share_gate_up,
        gate_up_first,
        gate_up_second,
        rate_wide,
        weight_decay,
    )
    down_new, down_first_new, down_second_new = adam(
        down_weight, share_down, down_first, down_second, rate_down, weight_decay
    )
    gains_new, gains_first_new, gains_second_new = adam(
        norm_gains, share_gains, gains_first, gains_second, rate_gains, 0.0
    )
    return (
        block_out,
        input_grad,
        query_new,
        query_first_new,
        query_second_new,
        pair_new,
        pair_first_new,
        pair_second_new,
        output_new,
        output_first_new,
        output_second_new,
        gate_up_new,
        gate_up_first_new,
        gate_up_second_new,
        down_new,
        down_first_new,
        down_second_new,
        gains_new,
        gains_first_new,
        gains_second_new,
    )


def solution(mesh):
    return jax.shard_map(
        shards,
        mesh=mesh,
        in_specs=(
            P("dp", "seq", None),
            P("dp", "seq", None),
            P(("dp", "seq"), "tensor"),
            P(("dp", "seq"), "tensor"),
            P(("dp", "seq"), "tensor"),
            P(("dp", "seq"), "tensor", None),
            P(("dp", "seq"), "tensor", None),
            P(("dp", "seq"), "tensor", None),
            P("tensor", ("dp", "seq")),
            P("tensor", ("dp", "seq")),
            P("tensor", ("dp", "seq")),
            P(None, ("dp", "seq"), "tensor"),
            P(None, ("dp", "seq"), "tensor"),
            P(None, ("dp", "seq"), "tensor"),
            P("tensor", ("dp", "seq")),
            P("tensor", ("dp", "seq")),
            P("tensor", ("dp", "seq")),
            P(None, ("dp", "seq")),
            P(None, ("dp", "seq")),
            P(None, ("dp", "seq")),
        ),
        out_specs=(
            P("dp", ("seq", "tensor"), None),
            P("dp", ("seq", "tensor"), None),
            P(("dp", "seq"), "tensor"),
            P(("dp", "seq"), "tensor"),
            P(("dp", "seq"), "tensor"),
            P(("dp", "seq"), "tensor", None),
            P(("dp", "seq"), "tensor", None),
            P(("dp", "seq"), "tensor", None),
            P("tensor", ("dp", "seq")),
            P("tensor", ("dp", "seq")),
            P("tensor", ("dp", "seq")),
            P(None, ("dp", "seq"), "tensor"),
            P(None, ("dp", "seq"), "tensor"),
            P(None, ("dp", "seq"), "tensor"),
            P("tensor", ("dp", "seq")),
            P("tensor", ("dp", "seq")),
            P("tensor", ("dp", "seq")),
            P(None, ("dp", "seq")),
            P(None, ("dp", "seq")),
            P(None, ("dp", "seq")),
        ),
        check_vma=False,
    )
```

```python
import jax
import jax.numpy as jnp
from jax import lax
from jax.experimental import pallas as pl
from jax.experimental.pallas import tpu as pltpu
from jax.sharding import PartitionSpec as P

QUERY_HEADS = 32
KEY_VALUE_HEADS = 8
HEAD_SIZE = 64
STEP = 10
GROUP = QUERY_HEADS // KEY_VALUE_HEADS


norm_eps = 1e-05
rope_base = 500000.0
beta_first = 0.9
beta_second = 0.95
adam_eps = 1e-08
weight_decay = 0.1
rate_wide = 0.07
rate_down = 0.035
rate_output = 1.0
rate_gains = 0.7

bf16 = jnp.bfloat16
f32 = jnp.float32
MESH = pl.DeviceIdType.MESH
VMEM = pl.BlockSpec(memory_space=pltpu.VMEM)
ANY = pl.BlockSpec(memory_space=pl.ANY)
MIB = 1024 * 1024


def inverse_rms(values):
    return lax.rsqrt(jnp.mean(values * values, axis=-1, keepdims=True) + norm_eps)


def rotary(positions):
    half_size = HEAD_SIZE // 2
    freqs = rope_base ** (-2.0 * jnp.arange(half_size, dtype=jnp.float32) / HEAD_SIZE)
    angles = positions.astype(jnp.float32)[:, None] * freqs[None, :]
    return (jnp.cos(angles), jnp.sin(angles))


def adam(master, grad, moment_one, moment_two, rate, decay):
    new_one = beta_first * moment_one + (1.0 - beta_first) * grad
    new_two = beta_second * moment_two + (1.0 - beta_second) * grad * grad
    ahead = (
        new_one
        / (1.0 - beta_first**STEP)
        / (jnp.sqrt(new_two / (1.0 - beta_second**STEP)) + adam_eps)
    )
    return (master - rate * (ahead + decay * master), new_one, new_two)


def tensor_peers():
    me = lax.axis_index("tensor")
    z, y = me // 2, me % 2
    return [
        ((z + dz) % 4) * 2 + (y + dy) % 2
        for dz, dy in ((2, 1), (1, 1), (3, 1), (2, 0), (1, 0), (3, 0), (0, 1))
    ]


def chip_peers():
    dp, seq = lax.axis_index("dp"), lax.axis_index("seq")
    x, core = seq // 2, seq % 2
    return [
        ((dp + dd) % 2, (x + dx) % 4, core)
        for dx, dd in ((2, 1), (1, 1), (3, 1), (0, 1), (2, 0), (1, 0), (3, 0))
    ]


def row_peers():
    seq = lax.axis_index("seq")
    x, core = seq // 2, seq % 2
    return [((x + dx) % 4, core) for dx in (2, 1, 3)]


def sibling():
    seq = lax.axis_index("seq")
    return seq + 1 - 2 * (seq % 2)


def greet(devices):
    barrier = pltpu.get_barrier_semaphore()
    for device in devices:
        pl.semaphore_signal(barrier, inc=1, device_id=device, device_id_type=MESH)
    pl.semaphore_wait(barrier, len(devices))


def remote(src, dst, sends, recvs, at, device):
    return pltpu.make_async_remote_copy(src, dst, sends.at[at], recvs.at[at], device, MESH)


def params(collective_id, mib):
    return pltpu.CompilerParams(
        collective_id=collective_id, has_side_effects=True, vmem_limit_bytes=mib * MIB
    )


def causal_bias(bias):
    seq = lax.axis_index("seq")
    rows, keys = bias.shape
    row = lax.broadcasted_iota(jnp.int32, (rows, keys), 0) + seq * rows
    key = lax.broadcasted_iota(jnp.int32, (rows, keys), 1)
    bias[...] = jnp.where(key <= row, 0.0, -1e30).astype(f32)


def nt(left, right):
    return lax.dot_general(left, right, (((1,), (1,)), ((), ())), preferred_element_type=f32)


def tn(left, right):
    return lax.dot_general(left, right, (((0,), (0,)), ((), ())), preferred_element_type=f32)


def columns(tile, size):
    return pl.ds(pl.multiple_of(tile * size, size), size)


def turn(values, cos_table, sin_table):
    lane = lax.broadcasted_iota(jnp.int32, values.shape, 1)
    half = HEAD_SIZE // 2
    other = jnp.where(
        lane % HEAD_SIZE < half,
        pltpu.roll(values, values.shape[1] - half, 1),
        pltpu.roll(values, half, 1),
    )
    return values * cos_table + other * sin_table


def block_of(peer):
    return pl.ds(pl.multiple_of(peer * 32, 32), 32)


def own_chunks(body):
    def step(k, carry):
        body(k // 2, pl.multiple_of((k % 2) * 16, 16))
        return carry

    lax.fori_loop(0, 6, step, 0)


FIRST = 896
SHIFTS = (2, 1, 3)


def fold_scratch(lead, rows, width):
    rest = width - FIRST
    return [
        pltpu.VMEM(lead + shape, bf16)
        for shape in (
            (3, 2, rows, FIRST),
            (4, rows, rest),
            (3, rows, rest),
            (3, rows, rest),
            (rows, FIRST),
            (rows, FIRST),
        )
    ]


class Fold:
    def __init__(self, source, local, refs, sends, recvs, base):
        tensor = lax.axis_index("tensor")
        self.z, self.y = tensor // 2, tensor % 2
        self.source, self.local = source, local
        self.over_z, self.from_partner, self.ready, self.second, self.mine, self.last = refs
        self.rows, self.width = self.from_partner.shape[1], FIRST + self.from_partner.shape[2]
        self.sends, self.recvs, self.base = sends, recvs, base
        self.copies = {}

    def send(self, k, source, place, z, y):
        copy = remote(
            source, place, self.sends, self.recvs, self.base + k, {"tensor": 2 * (z % 4) + y}
        )
        copy.start()
        self.copies[k] = copy

    def begin(self, dz):
        to = (self.z + dz) % 4
        first, rest = pl.ds(0, FIRST), pl.ds(FIRST, self.width - FIRST)
        if dz:
            k = SHIFTS.index(dz)
            self.send(k, self.source.at[to, :, :, first], self.over_z.at[k], to, self.y)
        self.send(
            3 + dz, self.source.at[to, 1 - self.y, :, rest], self.from_partner.at[dz], self.z,
            1 - self.y,
        )

    def chunks(self, body):
        def step(k, carry):
            body(pl.ds(pl.multiple_of(k * 16, 16), 16))
            return carry

        lax.fori_loop(0, self.rows // 16, step, 0)

    def pass_z(self, dz):
        self.copies[3 + dz].wait_recv()
        if dz == 0:
            return
        k = SHIFTS.index(dz)

        def body(at):
            both = self.local(dz, 0, at)[:, FIRST:] + self.from_partner[dz, at, :].astype(f32)
            self.ready[k, at, :] = both.astype(bf16)

        self.chunks(body)
        self.send(8 + k, self.ready.at[k], self.second.at[k], self.z + dz, self.y)

    def pass_partner(self):
        for k in range(3):
            self.copies[k].wait_recv()

        def body(at):
            result = self.local(0, 1, at)[:, :FIRST]
            for k in range(3):
                result = result + self.over_z[k, 1 - self.y, at, :].astype(f32)
            self.mine[at, :] = result.astype(bf16)

        self.chunks(body)
        self.send(7, self.mine, self.last, self.z, 1 - self.y)

    def finish(self):
        for k in (7, 8, 9, 10):
            self.copies[k].wait_recv()
        for copy in self.copies.values():
            copy.wait_send()

    def total(self, at):
        own = self.local(0, 0, at)
        low = own[:, :FIRST] + self.last[at, :].astype(f32)
        high = own[:, FIRST:] + self.from_partner[0, at, :].astype(f32)
        for k in range(3):
            low = low + self.over_z[k, self.y, at, :].astype(f32)
            high = high + self.second[k, at, :].astype(f32)
        return jnp.concatenate([low, high], axis=1)


class Weights:
    def __init__(self, mine, whole, sends, recvs, near_sends, near_recvs):
        self.dp, self.seq = lax.axis_index("dp"), lax.axis_index("seq")
        self.mine, self.whole = mine, whole
        self.sends, self.recvs = sends, recvs
        self.near_sends, self.near_recvs = near_sends, near_recvs
        self.started, self.passed = {}, []

    def owner(self, dx, dd):
        x, core = self.seq // 2, self.seq % 2
        return (self.dp + dd) % 2, ((x + dx) % 4) * 2 + core

    def device(self, dx, dd):
        dp, seq = self.owner(dx, dd)
        return {"dp": dp, "seq": seq}

    def view(self, dx, dd, half=None):
        ref = self.whole.at[self.owner(dx, dd)]
        return ref if half is None else ref.at[pl.ds(64 * half, 64)]

    def send(self, k, block, to, half=None):
        place = self.view(*block, half)
        source = place
        if block == (0, 0):
            source = self.mine if half is None else self.mine.at[pl.ds(64 * half, 64)]
        copy = remote(source, place, self.sends, self.recvs, k, self.device(*to))
        copy.start()
        self.started[k] = copy

    def beside(self, k, block, half=None):
        place = self.view(*block, half)
        source = self.mine if block == (0, 0) else place
        copy = remote(source, place, self.near_sends, self.near_recvs, k, {"seq": sibling()})
        copy.start()
        self.passed.append(copy)

    def start(self):
        self.send(0, (0, 0), (0, 1))
        self.send(1, (0, 0), (1, 0), 0)
        self.send(2, (0, 0), (3, 0), 0)
        self.beside(0, (0, 0))

    def rest(self):
        self.send(3, (0, 0), (1, 0), 1)
        self.send(4, (0, 0), (3, 0), 1)

    def partner(self):
        self.started[0].wait_recv()
        self.send(5, (0, 1), (1, 0))
        self.send(6, (0, 1), (3, 0))
        self.beside(1, (0, 1))

    def own_ring(self):
        self.started[1].wait_recv()
        self.send(7, (3, 0), (1, 0), 0)
        self.started[4].wait_recv()
        self.send(8, (1, 0), (3, 0), 1)
        self.started[3].wait_recv()
        self.beside(2, (3, 0))
        self.started[2].wait_recv()
        self.beside(3, (1, 0))

    def partner_ring(self):
        self.started[5].wait_recv()
        self.send(9, (3, 1), (1, 0), 0)
        self.beside(4, (3, 1))
        self.started[6].wait_recv()
        self.send(10, (1, 1), (3, 0), 1)
        self.beside(5, (1, 1))

    def finish(self):
        for k, half, dd in ((7, 0, 0), (8, 1, 0), (9, 0, 1), (10, 1, 1)):
            self.started[k].wait_recv()
            self.beside(k - 1, (2, dd), half)
        for copy in self.started.values():
            copy.wait_send()
        for copy in self.passed:
            copy.wait()


def forward_kernel(
    tokens, mine, gains_mine, ff_mine, cos_table, sin_table,
    query_out, pairs_out, kept_out, mixed_out, packed_out, first_out, mid, rows_in, ff_all, gains,
    query, pairs, kept, mixed, packed, h_first, part, over_z, from_partner, ready, second, own_first, last_first, bias,
    sends, recvs, near_sends, near_recvs, late_sends, late_recvs, late_near_sends,
    late_near_recvs, gain_sends, gain_recvs, pair_sends, pair_recvs,
    pair_near_sends, pair_near_recvs, out_sends, out_recvs, ff_sends, ff_recvs, ff_near_sends,
    ff_near_recvs, row_sends, row_recvs, local, stores,
):
    dp, seq, tensor = lax.axis_index("dp"), lax.axis_index("seq"), lax.axis_index("tensor")
    me = dp * 8 + seq
    stored = []

    def store(source, place):
        copy = pltpu.make_async_copy(source, place, stores.at[len(stored)])
        copy.start()
        stored.append(copy)

    count, rows, width = tokens.shape
    keys = bias.shape[1]
    near = {"seq": sibling()}
    owners = [((dp + k // 8) % 2, (seq + k % 8) % 8) for k in range(1, 16)]
    greet(
        [{"tensor": peer} for peer in tensor_peers()] + [{"dp": d, "seq": s} for d, s in owners]
    )
    gain_at = pl.ds(pl.multiple_of(me * 128, 128), 128)
    gain_copies = [
        remote(gains_mine, gains.at[:, gain_at], gain_sends, gain_recvs, k, {"dp": d, "seq": s})
        for k, (d, s) in enumerate(owners)
    ]
    for copy in gain_copies:
        copy.start()
    early, late = pl.ds(0, 384), pl.ds(384, 256)
    out, out_late = [
        [
            remote(
                mine.at[:, at], packed.at[me, :, at], ss, rs, i, {"dp": d, "seq": 2 * x + c}
            )
            for i, (d, x, c) in enumerate(chip_peers())
        ]
        for at, ss, rs in ((early, sends, recvs), (late, late_sends, late_recvs))
    ]
    first, first_late = [
        remote(mine.at[:, at], packed.at[me, :, at], ss, rs, 7, near)
        for at, ss, rs in (
            (early, near_sends, near_recvs),
            (late, late_near_sends, late_near_recvs),
        )
    ]
    for copy in out + [first] + out_late + [first_late]:
        copy.start()
    ff = Weights(ff_mine, ff_all, ff_sends, ff_recvs, ff_near_sends, ff_near_recvs)
    ff.start()
    store_ff = pltpu.make_async_copy(ff_mine, ff_all.at[dp, seq], local)
    store_ff.start()
    packed[me] = mine[...]
    gains[:, gain_at] = gains_mine[...]
    causal_bias(bias)
    for copy in gain_copies:
        copy.wait()

    def normalize(k, carry):
        i = k // 16
        at = pl.ds(pl.multiple_of((k % 16) * 16, 16), 16)
        token_rows = tokens[i, at, :].astype(f32)
        h_first[i, at, :] = (token_rows * inverse_rms(token_rows) * gains[0:1, :]).astype(bf16)
        return carry

    lax.fori_loop(0, count * 16, normalize, 0)
    store(h_first, first_out)

    def pass_weights(out, first, at, ss, rs):
        passed = [first]
        for i, (dd, dx) in (
            (6, (0, 1)), (5, (0, 3)), (3, (1, 0)), (4, (0, 2)), (2, (1, 1)), (1, (1, 3)), (0, (1, 2)),
        ):
            out[i].wait_recv()
            owner = (((dp + dd) % 2) * 4 + (seq // 2 + dx) % 4) * 2 + seq % 2
            block = packed.at[owner, :, at]
            copy = remote(block, block, ss, rs, i, near)
            copy.start()
            passed.append(copy)
        return passed

    for copy in pass_weights(out, first, early, near_sends, near_recvs):
        copy.wait()
    scale = HEAD_SIZE ** (-0.5)
    lane = lax.broadcasted_iota(jnp.int32, (rows, 2 * HEAD_SIZE), 1)

    def project(i, carry):
        raw = jnp.dot(
            h_first[i], packed[:, :, :384].reshape(width, 384), preferred_element_type=f32
        )
        for at in range(GROUP // 2):
            both = raw[:, at * 2 * HEAD_SIZE : (at + 1) * 2 * HEAD_SIZE]
            both = turn(both, cos_table[...], -sin_table[...]) * scale
            query[i, 2 * at] = jnp.where(lane < HEAD_SIZE, both, 0.0).astype(bf16)
            moved = pltpu.roll(both, HEAD_SIZE, 1)
            query[i, 2 * at + 1] = jnp.where(lane < HEAD_SIZE, moved, 0.0).astype(bf16)
        pair = raw[:, GROUP * HEAD_SIZE :]
        turned = turn(pair, cos_table[...], -sin_table[...])
        pairs[seq, i] = jnp.where(lane < HEAD_SIZE, turned, pair).astype(bf16)
        return carry

    lax.fori_loop(0, count, project, 0)
    pair_out = [
        remote(pairs.at[seq], pairs.at[seq], pair_sends, pair_recvs, i, {"seq": 2 * x + c})
        for i, (x, c) in enumerate(row_peers())
    ]
    for copy in pair_out:
        copy.start()
    pair_first = remote(pairs.at[seq], pairs.at[seq], pair_near_sends, pair_near_recvs, 3, near)
    pair_first.start()
    ff.rest()
    pair_passed = []
    for i, dx in ((1, 3), (2, 1), (0, 2)):
        pair_out[i].wait_recv()
        owner = ((seq // 2 + dx) % 4) * 2 + seq % 2
        forward = remote(
            pairs.at[owner], pairs.at[owner], pair_near_sends, pair_near_recvs, i, near
        )
        forward.start()
        pair_passed.append(forward)
    pair_first.wait()
    for copy in pair_passed:
        copy.wait()
    store(query, query_out)
    store(pairs, pairs_out)
    passed_late = pass_weights(out_late, first_late, late, late_near_sends, late_near_recvs)
    ff.partner()

    def attend(i):
        upper = []
        pair = pairs[:, i].reshape(keys, 2 * HEAD_SIZE)
        for head in range(GROUP):
            scores = nt(query[i, head], pair) + bias[...]
            row_max = jnp.max(scores, axis=-1, keepdims=True)
            exps = jnp.exp(scores - row_max)
            row_sum = jnp.sum(exps, axis=-1, keepdims=True)
            mix = jnp.dot(exps.astype(bf16), pair, preferred_element_type=f32) / row_sum
            kept[i, head] = jnp.where(lane < HEAD_SIZE, row_max + jnp.log(row_sum), mix)
            upper.append(mix)
        for at in range(GROUP // 2):
            low = pltpu.roll(upper[2 * at], HEAD_SIZE, 1)
            both = jnp.where(lane < HEAD_SIZE, low, upper[2 * at + 1])
            mixed[i, :, at * 2 * HEAD_SIZE : (at + 1) * 2 * HEAD_SIZE] = both.astype(bf16)

    def attend_step(i, carry):
        attend(i)
        return carry

    def output_step(i, carry):
        def term(tile, inner_carry):
            weight_rows = packed[pl.ds(tile * 4, 4), :, 384:640].reshape(512, 256)
            product = nt(mixed[i], weight_rows).astype(bf16)
            part[i, :, :, :, columns(tile, 512)] = product.reshape(4, 2, 32, 512)
            return inner_carry

        lax.fori_loop(0, width // 512, term, 0)
        return carry

    def term_of(i):
        def local(dz, dy, at):
            return part[i, (tensor // 2 + dz) % 4, (tensor + dy) % 2, at, :].astype(f32)

        return local

    folds = []
    for i in range(count):
        lax.fori_loop(i, i + 1, attend_step, 0)
        if i == 0:
            for copy in passed_late:
                copy.wait()
            store(packed, packed_out)
        lax.fori_loop(i, i + 1, output_step, 0)
        fold = Fold(
            part.at[i],
            term_of(i),
            [ref.at[i] for ref in (over_z, from_partner, ready, second, own_first, last_first)],
            out_sends,
            out_recvs,
            11 * i,
        )
        for dz in (2, 1, 3, 0):
            fold.begin(dz)
        folds.append(fold)
        if i:
            for dz in (2, 1, 3, 0):
                folds[i - 1].pass_z(dz)
        if i == 1:
            ff.own_ring()
    store(kept, kept_out)
    store(mixed, mixed_out)
    folds[0].pass_partner()
    for dz in (2, 1, 3, 0):
        folds[2].pass_z(dz)
    folds[1].pass_partner()
    ff.partner_ring()
    folds[2].pass_partner()
    for i, fold in enumerate(folds):
        fold.finish()

        def chunk(k, carry, i=i, fold=fold):
            row = pl.multiple_of(k * 16, 16)
            at = pl.ds(pl.multiple_of(tensor * 32 + row, 16), 16)
            result = fold.total(pl.ds(row, 16)) + tokens[i, at, :].astype(f32)
            at = pl.ds(pl.multiple_of(i * 32 + row, 16), 16)
            mid[at, :] = result
            rows_in[0, at, :] = (result * inverse_rms(result) * gains[1:2, :]).astype(bf16)
            return carry

        lax.fori_loop(0, 2, chunk, 0)
    z, y = tensor // 2, tensor % 2
    row_copies = [
        remote(
            rows_in.at[0], rows_in.at[k + 1], row_sends, row_recvs, k,
            {"tensor": 2 * ((z + dz) % 4) + (y + dy) % 2},
        )
        for k, (dz, dy) in enumerate(((0, 1), (1, 0), (3, 0)))
    ]
    for copy in row_copies:
        copy.start()
    for copy in out + out_late + pair_out:
        copy.wait_send()
    store_ff.wait()
    ff.finish()
    for copy in row_copies + stored:
        copy.wait()


def forward(tokens, mine, gains_mine, ff_mine, cos_table, sin_table):
    count, rows, width = tokens.shape
    dma = pltpu.SemaphoreType.DMA
    lanes = 2 * HEAD_SIZE
    return pl.pallas_call(
        forward_kernel,
        out_shape=(
            jax.ShapeDtypeStruct((count, GROUP, rows, lanes), bf16),
            jax.ShapeDtypeStruct((8, count, rows, lanes), bf16),
            jax.ShapeDtypeStruct((count, GROUP, rows, lanes), f32),
            jax.ShapeDtypeStruct((count, rows, GROUP * HEAD_SIZE), bf16),
            jax.ShapeDtypeStruct((16,) + mine.shape, bf16),
            jax.ShapeDtypeStruct((count, rows, width), bf16),
            jax.ShapeDtypeStruct((count * 32, width), f32),
            jax.ShapeDtypeStruct((4, count * 32, width), bf16),
            jax.ShapeDtypeStruct((2, 8) + ff_mine.shape, bf16),
            jax.ShapeDtypeStruct((8, width), f32),
        ),
        in_specs=[VMEM] * 6,
        out_specs=(ANY,) * 6 + (VMEM, VMEM, ANY, VMEM),
        scratch_shapes=[
            pltpu.VMEM((count, GROUP, rows, lanes), bf16),
            pltpu.VMEM((8, count, rows, lanes), bf16),
            pltpu.VMEM((count, GROUP, rows, lanes), f32),
            pltpu.VMEM((count, rows, GROUP * HEAD_SIZE), bf16),
            pltpu.VMEM((16,) + mine.shape, bf16),
            pltpu.VMEM((count, rows, width), bf16),
            pltpu.VMEM((count, 4, 2, 32, width), bf16),
            *fold_scratch((count,), 32, width),
            pltpu.VMEM((rows, 8 * rows), f32),
            dma((7,)), dma((7,)), dma((8,)), dma((8,)), dma((7,)), dma((7,)), dma((8,)), dma((8,)),
            dma((15,)), dma((15,)), dma((3,)), dma((3,)),
            dma((4,)), dma((4,)), dma((33,)), dma((33,)), dma((11,)), dma((11,)), dma((10,)),
            dma((10,)), dma((3,)), dma((3,)), dma, dma((6,)),
        ],
        compiler_params=params(1, 60),
        cost_estimate=pl.CostEstimate(flops=40000 * MIB, bytes_accessed=200 * MIB, transcendentals=0),
        name="forward",
    )(tokens, mine, gains_mine, ff_mine, cos_table, sin_table)


class Spread:
    def __init__(self, buffer, sends, recvs):
        tensor = lax.axis_index("tensor")
        self.buffer, self.sends, self.recvs = buffer, sends, recvs
        self.z, self.y = tensor // 2, tensor % 2
        self.started = {}

    def at(self, dz, dy):
        return ((self.z + dz) % 4) * 2 + (self.y + dy) % 2

    def send(self, k, block, to, half=None):
        ref = self.buffer.at[block]
        if half is not None:
            rows = self.buffer.shape[1] // 2
            ref = self.buffer.at[block, pl.ds(half * rows, rows)]
        copy = remote(ref, ref, self.sends, self.recvs, k, {"tensor": to})
        copy.start()
        self.started[k] = copy

    def pass_partner(self):
        self.send(3, self.at(0, 1), self.at(1, 0))
        self.send(4, self.at(0, 1), self.at(3, 0))

    def pass_on(self, dy):
        if dy:
            self.started[3].wait_recv()
        self.send(5 + 2 * dy, self.at(3, dy), self.at(1, 0), 0)
        if dy:
            self.started[4].wait_recv()
        self.send(6 + 2 * dy, self.at(1, dy), self.at(3, 0), 1)

    def finish(self):
        for k in range(5, 9):
            self.started[k].wait_recv()

    def drain(self):
        for copy in self.started.values():
            copy.wait_send()


def feed_forward_kernel(
    own, cotangent, weights, mid, gain,
    branch, grad_mid, grad_gain, mlp_out, grads_out,
    gate_up, down, cot, normed, grad_hidden, grad_units, hidden, second,
    over_z, from_partner, ready, second_in, own_first, last_first, mlp, grads,
    sends, recvs, back_sends, back_recvs, local, cot_sems, out_sems, mlp_sem,
):
    tensor = lax.axis_index("tensor")
    units = down.shape[3]
    width = 16 * 128
    dp = lax.axis_index("dp")
    load_down = pltpu.make_async_copy(
        weights.at[:, :, :, pl.ds(2 * units, units)], down, local.at[0]
    )
    load_gate_up = pltpu.make_async_copy(
        weights.at[:, :, :, pl.ds(0, 2 * units)], gate_up, local.at[1]
    )
    load_down.start()
    load_cot = [
        pltpu.make_async_copy(cotangent.at[:, t], cot.at[t], cot_sems.at[t]) for t in range(8)
    ]
    for copy in load_cot:
        copy.start()
    load_gate_up.start()
    greet([{"tensor": peer} for peer in tensor_peers()])
    spread = Spread(normed, sends, recvs)
    for k, (dz, dy) in enumerate(((0, 0), (0, 1), (3, 0), (1, 0))):
        normed[spread.at(dz, dy)] = own[k]
    spread.pass_partner()
    spread.pass_on(0)
    for copy in load_cot:
        copy.wait()
    load_down.wait()

    def hidden_step(tile, carry):
        at = columns(tile, 256)
        product = jnp.dot(
            cot[...].reshape(8 * 96, width),
            down[:, :, :, at].reshape(width, 256),
            preferred_element_type=f32,
        )
        grad_hidden[:, :, at] = product.reshape(8, 96, 256)
        return carry

    lax.fori_loop(0, units // 256, hidden_step, 0)
    load_gate_up.wait()

    def own_term(dz, dy, at):
        return second[(spread.z + dz) % 4, (spread.y + dy) % 2, at, :].astype(f32)

    fold = Fold(
        second,
        own_term,
        (over_z, from_partner, ready, second_in, own_first, last_first),
        back_sends,
        back_recvs,
        0,
    )

    def block(dz):
        first = ((spread.z + dz) % 4) * 2
        both = pl.ds(first, 2)

        def units_step(tile, carry):
            at = columns(tile, 256)
            up_at = pl.ds(pl.multiple_of(units + tile * 256, 256), 256)
            rows = normed[both].reshape(192, width)
            gate_columns = gate_up[:, :, :, at].reshape(width, 256)
            up_columns = gate_up[:, :, :, up_at].reshape(width, 256)
            gate_in = jnp.dot(rows, gate_columns, preferred_element_type=f32)
            up_in = jnp.dot(rows, up_columns, preferred_element_type=f32)
            grad = grad_hidden[both, :, at].reshape(192, 256)
            sigmoid = jax.nn.sigmoid(gate_in)
            silu = gate_in * sigmoid
            hidden[both, :, at] = (silu * up_in).astype(bf16).reshape(2, 96, 256)
            grad_gate = grad * up_in * sigmoid * (1.0 + gate_in * (1.0 - sigmoid))
            grad_units[both, :, at] = grad_gate.astype(bf16).reshape(2, 96, 256)
            grad_units[both, :, up_at] = (grad * silu).astype(bf16).reshape(2, 96, 256)
            return carry

        lax.fori_loop(0, units // 256, units_step, 0)

        def second_step(tile, carry):
            at = columns(tile, 512)
            rows = grad_units[both].reshape(192, 2 * units)
            weight_rows = gate_up[tile // 2, pl.ds((tile % 2) * 4, 4)].reshape(512, 2 * units)
            product = nt(rows, weight_rows).astype(bf16)
            second[first // 2, :, :, at] = product.reshape(2, 96, 512)
            return carry

        lax.fori_loop(0, width // 512, second_step, 0)
        fold.begin(dz)

    block(0)
    spread.pass_on(1)
    block(1)
    fold.pass_z(0)
    block(3)
    fold.pass_z(1)
    spread.finish()
    block(2)
    fold.pass_z(3)

    def mlp_step(tile, carry):
        at = columns(tile, 256)
        rows = hidden[...].reshape(8 * 96, units)
        weight_rows = down[tile // 4, pl.ds((tile % 4) * 2, 2)].reshape(256, units)
        mlp[:, :, at] = nt(rows, weight_rows).astype(bf16).reshape(8, 96, 256)
        return carry

    lax.fori_loop(0, width // 512, mlp_step, 0)
    fold.pass_z(2)
    lax.fori_loop(width // 512, width // 256, mlp_step, 0)
    store_mlp = pltpu.make_async_copy(mlp, mlp_out, mlp_sem)
    store_mlp.start()

    def store(tile, slot):
        place = grads_out.at[pl.ds((tile % 4) * 2, 2), (tile // 4 + dp) % 2]
        return pltpu.make_async_copy(grads.at[slot], place, out_sems.at[slot])

    def grads_pair(pair, carry):
        for slot in range(2):
            tile = 2 * pair + slot
            at = columns(tile, 256)

            @pl.when(pair > 0)
            def _():
                store(tile - 2, slot).wait()

            wide = tn(
                normed[:, :, at].reshape(8 * 96, 256), grad_units[...].reshape(8 * 96, 2 * units)
            )
            grads[slot, :, :, : 2 * units] = wide.astype(bf16).reshape(2, 128, 2 * units)
            narrow = tn(cot[:, :, :, at].reshape(8 * 96, 256), hidden[...].reshape(8 * 96, units))
            grads[slot, :, :, 2 * units :] = narrow.astype(bf16).reshape(2, 128, units)
            store(tile, slot).start()
        return carry

    tiles = width // 256
    lax.fori_loop(0, tiles // 2 - 1, grads_pair, 0)
    fold.pass_partner()
    lax.fori_loop(tiles // 2 - 1, tiles // 2, grads_pair, 0)
    for slot in range(2):
        store(tiles - 2 + slot, slot).wait()
    store_mlp.wait()
    spread.drain()
    fold.finish()
    grad_gain[...] = jnp.zeros_like(grad_gain)

    def chunk(k, carry):
        at = pl.ds(pl.multiple_of(k * 16, 16), 16)
        grad = fold.total(at)
        rows = mid[at, :]
        inverse = inverse_rms(rows)
        normed_rows = rows * inverse
        product = grad * normed_rows
        grad_gain[...] += product[:8] + product[8:]
        inner = jnp.mean(product * gain[1:2, :], axis=-1, keepdims=True)
        own_cot = cot[tensor, k // 2, pl.ds(pl.multiple_of((k % 2) * 16, 16), 16), :].astype(f32)
        result = own_cot + inverse * (grad * gain[1:2, :] - normed_rows * inner)
        grad_mid[at, :] = result
        branch[at, :] = result.astype(bf16)
        return carry

    lax.fori_loop(0, 6, chunk, 0)


def feed_forward(own, cotangent, weights, mid, gain):
    rows, width = mid.shape
    units = weights.shape[3] // 3
    dma = pltpu.SemaphoreType.DMA
    return pl.pallas_call(
        feed_forward_kernel,
        out_shape=(
            jax.ShapeDtypeStruct((rows, width), bf16),
            jax.ShapeDtypeStruct((rows, width), f32),
            jax.ShapeDtypeStruct((8, width), f32),
            jax.ShapeDtypeStruct((8, rows, width), bf16),
            jax.ShapeDtypeStruct((8, 2) + weights.shape[2:], bf16),
        ),
        in_specs=[VMEM, ANY, ANY, VMEM, VMEM],
        out_specs=(VMEM, VMEM, VMEM, ANY, ANY),
        scratch_shapes=[
            pltpu.VMEM((2, 8, 128, 2 * units), bf16),
            pltpu.VMEM((2, 8, 128, units), bf16),
            pltpu.VMEM((8, 3, 32, width), bf16),
            pltpu.VMEM((8, rows, width), bf16),
            pltpu.VMEM((8, rows, units), f32),
            pltpu.VMEM((8, rows, 2 * units), bf16),
            pltpu.VMEM((8, rows, units), bf16),
            pltpu.VMEM((4, 2, rows, width), bf16),
            *fold_scratch((), rows, width),
            pltpu.VMEM((8, rows, width), bf16),
            pltpu.VMEM((2, 2, 128, 3 * units), bf16),
            dma((9,)), dma((9,)), dma((11,)), dma((11,)), dma((2,)), dma((8,)), dma((2,)), dma,
        ],
        compiler_params=params(5, 60),
        cost_estimate=pl.CostEstimate(
            flops=18 * 8 * rows * width * units, bytes_accessed=120 * MIB, transcendentals=0
        ),
        name="feed_forward",
    )(own, cotangent, weights, mid, gain)


def backward_kernel(
    branch, query_hbm, pairs_hbm, kept_hbm, mixed_hbm, packed_hbm, first_hbm, mlp_part, mid_hbm,
    cos_table, sin_table,
    part, ready, block_out,
    query, pairs, kept, mixed, packed, h_first, mid,
    whole, attended, raw, grad_pairs, near_pairs, ready_pairs, landed_pairs, bias, total, weights,
    near, mlp_own, mlp_pair, over_z, from_partner, ready_rows, second, own_first, last_first,
    out_sends, out_recvs, pair_near_sends, pair_near_recvs, pair_sends, pair_recvs, near_sends,
    near_recvs, mlp_sends, mlp_recvs, local,
):
    dp, seq, tensor = lax.axis_index("dp"), lax.axis_index("seq"), lax.axis_index("tensor")
    x, core = seq // 2, seq % 2
    peers = tensor_peers()
    rows_beside = row_peers()
    beside = {"seq": sibling()}
    z, y = tensor // 2, tensor % 2
    count, width = whole.shape[0], whole.shape[2]
    rows, keys = bias.shape
    loads = [
        pltpu.make_async_copy(source, place, local.at[k])
        for k, (source, place) in enumerate(
            (
                (packed_hbm, packed),
                (pairs_hbm, pairs),
                (query_hbm, query),
                (kept_hbm, kept),
                (mixed_hbm, mixed),
                (first_hbm, h_first),
                (mid_hbm, mid),
                (mlp_part.at[:, y], mlp_own),
                (mlp_part.at[z, 1 - y], mlp_pair),
            )
        )
    ]
    for copy in loads:
        copy.start()
    greet(
        [{"tensor": peer} for peer in peers]
        + [{"seq": 2 * px + c} for px, c in rows_beside]
        + [beside]
    )
    mine = pl.ds(pl.multiple_of(tensor * 32, 32), 32)
    spread = [
        remote(
            branch.at[pl.ds(32 * i, 32)], whole.at[i, mine], out_sends, out_recvs, 7 * i + k,
            {"tensor": peer},
        )
        for i in range(count)
        for k, peer in enumerate(peers)
    ]
    for copy in spread:
        copy.start()

    def mlp_term(dz, dy, at):
        rows_here = mlp_pair[at, :] if dy else mlp_own[(z + dz) % 4, at, :]
        return rows_here.astype(f32)

    fold = Fold(
        mlp_part,
        mlp_term,
        (over_z, from_partner, ready_rows, second, own_first, last_first),
        mlp_sends,
        mlp_recvs,
        0,
    )
    for dz in (2, 1, 3, 0):
        fold.begin(dz)
    for i in range(count):
        whole[i, mine, :] = branch[32 * i : 32 * i + 32, :]
    causal_bias(bias)
    for copy in loads:
        copy.wait()
    lane = lax.broadcasted_iota(jnp.int32, (rows, 2 * HEAD_SIZE), 1)
    scale = HEAD_SIZE ** (-0.5)

    def sequence(i):
        for copy in spread[7 * i : 7 * i + 7]:
            copy.wait_recv()
        attended[...] = (
            jnp.dot(
                whole[i], packed[:, :, 384:640].reshape(width, 256), preferred_element_type=f32
            )
            .astype(bf16)
            .astype(f32)
        )
        total[...] = jnp.zeros_like(total)

        def head_pair(at, carry):
            columns_at = columns(at, 2 * HEAD_SIZE)
            grads_here = attended[:, columns_at]
            grad_query = []
            for odd in range(2):
                pair = pairs[:, i].reshape(keys, 2 * HEAD_SIZE)
                placed = grads_here if odd else pltpu.roll(grads_here, HEAD_SIZE, 1)
                placed = jnp.where(lane >= HEAD_SIZE, placed, 0.0)
                grad_rows = placed.astype(bf16)
                query_rows = query[i, 2 * at + odd]
                kept_rows = kept[i, 2 * at + odd]
                probs = jnp.exp(nt(query_rows, pair) + bias[...] - kept_rows[:, :1])
                inner = jnp.sum(kept_rows * placed, axis=-1, keepdims=True)
                grad_scores = (probs * (nt(grad_rows, pair) - inner)).astype(bf16)
                grad_query.append(jnp.dot(grad_scores, pair, preferred_element_type=f32))
                total[...] += jnp.dot(
                    query_rows.T, grad_scores, preferred_element_type=f32
                ) + jnp.dot(grad_rows.T, probs.astype(bf16), preferred_element_type=f32)
            both = jnp.where(lane < HEAD_SIZE, grad_query[0], pltpu.roll(grad_query[1], HEAD_SIZE, 1))
            both = turn(both * scale, cos_table[...], sin_table[...])
            raw[i, :, columns_at] = both.astype(bf16)
            return carry

        lax.fori_loop(0, GROUP // 2, head_pair, 0)
        for block in range(8):
            grad_pairs[block // 2, block % 2, i] = (
                total[:, block * rows : (block + 1) * rows].T.astype(bf16)
            )

    def cross(i):
        copy = remote(
            grad_pairs.at[:, 1 - core, i], near_pairs.at[i], pair_near_sends, pair_near_recvs, i,
            beside,
        )
        copy.start()
        return copy

    def onward(i, crossing):
        crossing.wait()
        out = []
        for k, (px, c) in enumerate(rows_beside):
            both = grad_pairs[px, core, i].astype(f32) + near_pairs[i, px].astype(f32)
            ready_pairs[i, k] = both.astype(bf16)
            copy = remote(
                ready_pairs.at[i, k], landed_pairs.at[i, k], pair_sends, pair_recvs, 3 * i + k,
                {"seq": 2 * px + c},
            )
            copy.start()
            out.append(copy)
        return out

    def settle(i, moving):
        mine_pairs = grad_pairs[x, core, i].astype(f32) + near_pairs[i, x].astype(f32)
        for k, copy in enumerate(moving):
            copy.wait()
            mine_pairs = mine_pairs + landed_pairs[i, k].astype(f32)
        turned = turn(mine_pairs, cos_table[...], sin_table[...])
        raw[i, :, 256:] = jnp.where(lane < HEAD_SIZE, turned, mine_pairs).astype(bf16)

        def term(tile, carry):
            at = columns(tile, 512)
            weight_rows = packed[pl.ds(tile * 4, 4), :, :384].reshape(512, 384)
            product = nt(raw[i], weight_rows).astype(bf16)
            part[i, :, :, :, at] = product.reshape(4, 2, 32, 512)
            return carry

        lax.fori_loop(0, width // 512, term, 0)

    def outer(tile, carry):
        at = columns(tile, 256)
        product = tn(
            whole[:, :, at].reshape(count * rows, 256), mixed[...].reshape(count * rows, 256)
        )
        weights[tile, :, :, 256:512] = product.astype(bf16).reshape(2, 128, 256)
        return carry

    def query_weights(tile, carry):
        at = columns(tile, 256)
        product = tn(
            h_first[:, :, at].reshape(count * rows, 256), raw[:, :, :256].reshape(count * rows, 256)
        )
        weights[tile, :, :, :256] = product.astype(bf16).reshape(2, 128, 256)
        return carry

    def pair_weights(tile, carry):
        at = columns(tile, 512)
        product = tn(
            h_first[:, :, at].reshape(count * rows, 512), raw[:, :, 256:].reshape(count * rows, 128)
        )
        weights[pl.ds(2 * tile, 2), :, :, 512:] = product.astype(bf16).reshape(2, 2, 128, 128)
        return carry

    sequence(0)
    crossing = cross(0)
    sequence(1)
    moving = onward(0, crossing)
    crossing = cross(1)
    settle(0, moving)
    sequence(2)
    crossing_last = cross(2)
    moving = onward(1, crossing)
    for dz in (2, 1, 3, 0):
        fold.pass_z(dz)
    lax.fori_loop(0, width // 256, outer, 0)
    moving_last = onward(2, crossing_last)
    settle(1, moving)
    lax.fori_loop(0, width // 256, query_weights, 0)
    settle(2, moving_last)
    fold.pass_partner()
    lax.fori_loop(0, width // 512, pair_weights, 0)
    across = remote(weights.at[:, 1 - core], near, near_sends, near_recvs, 0, beside)
    across.start()
    for copy in spread:
        copy.wait_send()
    across.wait()
    for at in range(8):
        ready[at] = (weights[at, core].astype(f32) + near[at].astype(f32)).astype(bf16)
    fold.finish()

    def finish_rows(i, row):
        at = pl.ds(pl.multiple_of(i * 32 + row, 16), 16)
        result = mid[at, :] + fold.total(at)
        block_out[i, pl.ds(row, 16), :] = result.astype(bf16)

    own_chunks(finish_rows)


def backward(
    branch, query, pairs, kept, mixed, packed, h_first, mlp_part, mid, cos_table, sin_table
):
    count, rows, width = h_first.shape
    mlp_part = mlp_part.reshape((4, 2) + mlp_part.shape[1:])
    keys = pairs.shape[0] * rows
    pair_rows = (rows, 2 * HEAD_SIZE)
    own = mid.shape[0]
    dma = pltpu.SemaphoreType.DMA
    vmem = pltpu.VMEM
    return pl.pallas_call(
        backward_kernel,
        out_shape=(
            jax.ShapeDtypeStruct((count, 4, 2, 32, width), bf16),
            jax.ShapeDtypeStruct((8, 128, 640), bf16),
            jax.ShapeDtypeStruct((count, 32, width), bf16),
        ),
        in_specs=[VMEM] + [ANY] * 8 + [VMEM] * 2,
        out_specs=(VMEM,) * 3,
        scratch_shapes=[
            vmem(query.shape, bf16),
            vmem(pairs.shape, bf16),
            vmem(kept.shape, f32),
            vmem(mixed.shape, bf16),
            vmem(packed.shape, bf16),
            vmem(h_first.shape, bf16),
            vmem(mid.shape, f32),
            vmem((count, rows, width), bf16),
            vmem((rows, GROUP * HEAD_SIZE), f32),
            vmem((count, rows, 384), bf16),
            vmem((4, 2, count) + pair_rows, bf16),
            vmem((count, 4) + pair_rows, bf16),
            vmem((count, 3) + pair_rows, bf16),
            vmem((count, 3) + pair_rows, bf16),
            vmem((rows, keys), f32),
            vmem((2 * HEAD_SIZE, keys), f32),
            vmem((8, 2, 128, 640), bf16),
            vmem((8, 128, 640), bf16),
            vmem((4, own, width), bf16),
            vmem((own, width), bf16),
            *fold_scratch((), own, width),
            dma((21,)), dma((21,)), dma((3,)), dma((3,)), dma((9,)), dma((9,)), dma((1,)), dma((1,)),
            dma((11,)), dma((11,)), dma((9,)),
        ],
        compiler_params=params(7, 62),
        cost_estimate=pl.CostEstimate(flops=40000 * MIB, bytes_accessed=200 * MIB, transcendentals=0),
        name="backward",
    )(
        branch, query, pairs, kept, mixed, packed, h_first, mlp_part, mid, cos_table, sin_table
    )


def ending_kernel(
    part, weights, ff, tokens_hbm, grad_mid_hbm, gain, gain_two,
    input_grad, share_query, share_pair, share_output, gain_sum, share_gate_up, share_down,
    part_own, weights_own, ff_own, tokens, grad_mid, landed, ours, partner, landed_last, shares, ff_in, grads, gains, gains_in, gains_near,
    sends, recvs, last_sends, last_recvs, far_sends, far_recvs, ff_sends, ff_recvs,
    gain_sends, gain_recvs, gain_last_sends, gain_last_recvs, local,
):
    dp, seq, tensor = lax.axis_index("dp"), lax.axis_index("seq"), lax.axis_index("tensor")
    z, y = tensor // 2, tensor % 2
    peers = tensor_peers()
    chips = chip_peers()
    owners = [((dp + k // 8) % 2, (seq + k % 8) % 8) for k in range(1, 16)]
    count = part.shape[0]
    units = share_down.shape[0]
    here = dp * 4 + seq // 2
    loads = [
        pltpu.make_async_copy(source, place, local.at[k])
        for k, (source, place) in enumerate(
            (
                (part.at[:, z], part_own),
                (ff.at[0], ff_own),
                (weights.at[here], weights_own),
                (tokens_hbm.at[:, block_of(tensor)], tokens),
                (grad_mid_hbm, grad_mid),
            )
        )
    ]
    for copy in loads:
        copy.start()
    greet(
        [{"tensor": peer} for peer in peers] + [{"dp": d, "seq": s} for d, s in owners]
    )

    out = []
    for i in range(count):
        for k, dz in enumerate((2, 1, 3)):
            other = (z + dz) % 4
            copy = remote(
                part.at[i, other], landed.at[i, k], sends, recvs, 3 * i + k,
                {"tensor": 2 * other + y},
            )
            copy.start()
            out.append(copy)
    far = [
        remote(
            weights.at[d * 4 + px], shares.at[i], far_sends, far_recvs, i,
            {"dp": d, "seq": 2 * px + c},
        )
        for i, (d, px, c) in enumerate(chips)
    ]
    for copy in far:
        copy.start()
    swap = remote(ff.at[1], ff_in, ff_sends, ff_recvs, 0, {"dp": 1 - dp})
    swap.start()
    for copy in loads:
        copy.wait()
    grads[...] = jnp.zeros_like(grads)

    def collect(i):
        for copy in out[3 * i : 3 * i + 3]:
            copy.wait()

        def step(k, carry):
            row = pl.multiple_of(k * 16, 16)
            for own in (False, True):
                side = y if own else 1 - y
                at = pl.ds(row, 16)
                result = part_own[i, side, at, :].astype(f32)
                for j in range(3):
                    result = result + landed[i, j, side, at, :].astype(f32)
                if own:
                    ours[i, pl.ds(row, 16), :] = result
                else:
                    partner[i, pl.ds(row, 16), :] = result.astype(bf16)
            return carry

        lax.fori_loop(0, 2, step, 0)
        copy = remote(
            partner.at[i], landed_last.at[i], last_sends, last_recvs, i, {"tensor": 2 * z + 1 - y}
        )
        copy.start()
        return copy

    def conclude(i, copy):
        copy.wait()

        def step(k, carry):
            row = pl.ds(pl.multiple_of(k * 16, 16), 16)
            grad = ours[i, row, :] + landed_last[i, row, :].astype(f32)
            token_rows = tokens[i, row, :].astype(f32)
            inverse = inverse_rms(token_rows)
            normed = token_rows * inverse
            product = grad * normed
            grads[...] += product[:8] + product[8:]
            inner = jnp.mean(product * gain[0:1, :], axis=-1, keepdims=True)
            at = pl.ds(pl.multiple_of(i * 32 + k * 16, 16), 16)
            result = grad_mid[at, :] + inverse * (grad * gain[0:1, :] - normed * inner)
            input_grad[i, row, :] = result.astype(bf16)
            return carry

        lax.fori_loop(0, 2, step, 0)

    first = collect(0)
    second = collect(1)
    conclude(0, first)
    third = collect(2)
    conclude(1, second)
    conclude(2, third)
    gains[...] = jnp.zeros_like(gains)
    gains[0:1, :] = jnp.sum(grads[...], axis=0, keepdims=True)
    gains[1:2, :] = jnp.sum(gain_two[...], axis=0, keepdims=True)
    spread_gains = []
    for k, (d, s) in enumerate(owners):
        at = pl.ds(pl.multiple_of((d * 8 + s) * 128, 128), 128)
        copy = remote(gains.at[:, at], gains_in.at[k], gain_sends, gain_recvs, k, {"dp": d, "seq": s})
        copy.start()
        spread_gains.append(copy)
    own = gains[:, pl.ds(pl.multiple_of((dp * 8 + seq) * 128, 128), 128)]
    swap.wait()
    for tile in range(8):
        at = slice(128 * tile, 128 * tile + 128)
        share_gate_up[0, :, at] = ff_own[:, at].astype(f32) + ff_in[:, at].astype(f32)
        up_at = slice(units + 128 * tile, units + 128 * tile + 128)
        share_gate_up[1, :, at] = ff_own[:, up_at].astype(f32) + ff_in[:, up_at].astype(f32)
    for k, copy in enumerate(spread_gains):
        copy.wait()
        own = own + gains_in[k]
    gains_near[7] = own
    last = [
        remote(gains_near.at[7], gains_near.at[i], gain_last_sends, gain_last_recvs, i, {"tensor": peer})
        for i, peer in enumerate(peers)
    ]
    for copy in last:
        copy.start()
    for tile in range(8):
        at = slice(128 * tile, 128 * tile + 128)
        down_at = slice(2 * units + 128 * tile, 2 * units + 128 * tile + 128)
        both = ff_own[:, down_at].astype(f32) + ff_in[:, down_at].astype(f32)
        share_down[at, :] = both.T
    for copy in far:
        copy.wait()
    sums = weights_own[...].astype(f32)
    for i in range(7):
        sums = sums + shares[i].astype(f32)
    share_query[...] = sums[:, :256]
    share_pair[...] = sums[:, 512:]
    share_output[...] = sums[:, 256:512].T
    for copy in last:
        copy.wait()
    shifts = ((2, 1), (1, 1), (3, 1), (2, 0), (1, 0), (3, 0), (0, 1))
    sums = jnp.zeros_like(own)
    for t in range(8):
        slot = jnp.int32(7)
        for i, (dz, dy) in enumerate(shifts):
            source = ((z + 4 - dz) % 4) * 2 + (y + dy) % 2
            slot = jnp.where(source == t, i, slot)
        sums = sums + gains_near[slot]
    gain_sum[...] = sums[0:2, :]


def ending(part, weights, ff, tokens, grad_mid, gain, gain_two):
    count, width = part.shape[0], part.shape[4]
    units = ff.shape[2] // 3
    dma = pltpu.SemaphoreType.DMA
    vmem = pltpu.VMEM
    return pl.pallas_call(
        ending_kernel,
        out_shape=(
            jax.ShapeDtypeStruct((count, 32, width), bf16),
            jax.ShapeDtypeStruct((128, 256), f32),
            jax.ShapeDtypeStruct((128, 128), f32),
            jax.ShapeDtypeStruct((256, 128), f32),
            jax.ShapeDtypeStruct((2, 128), f32),
            jax.ShapeDtypeStruct((2, 128, units), f32),
            jax.ShapeDtypeStruct((units, 128), f32),
        ),
        in_specs=[ANY] * 5 + [VMEM] * 2,
        out_specs=(VMEM,) * 7,
        scratch_shapes=[
            vmem((count, 2, 32, width), bf16),
            vmem((128, 640), bf16),
            vmem((128, 3 * units), bf16),
            vmem((count, 32, width), bf16),
            vmem((count * 32, width), f32),
            vmem((count, 3, 2, 32, width), bf16),
            vmem((count, 32, width), f32),
            vmem((count, 32, width), bf16),
            vmem((count, 32, width), bf16),
            vmem((7, 128, 640), bf16),
            vmem((128, 3 * units), bf16),
            vmem((8, width), f32),
            vmem((8, width), f32),
            vmem((15, 8, 128), f32),
            vmem((8, 8, 128), f32),
            dma((9,)), dma((9,)), dma((3,)), dma((3,)), dma((7,)), dma((7,)), dma((1,)), dma((1,)),
            dma((15,)), dma((15,)), dma((7,)), dma((7,)), dma((5,)),
        ],
        compiler_params=params(2, 62),
        cost_estimate=pl.CostEstimate(flops=MIB, bytes_accessed=150 * MIB, transcendentals=0),
        name="ending",
    )(part, weights, ff, tokens, grad_mid, gain, gain_two)


def shards(
    tokens,
    cotangent,
    query_weight,
    query_first,
    query_second,
    key_value_weight,
    key_value_first_moment,
    key_value_second_moment,
    output_weight,
    output_first,
    output_second,
    gate_up_weight,
    gate_up_first,
    gate_up_second,
    down_weight,
    down_first,
    down_second,
    norm_gains,
    gains_first,
    gains_second,
):
    count, local_len, width = tokens.shape
    packed = jnp.concatenate(
        [
            query_weight,
            key_value_weight.reshape(128, 2 * HEAD_SIZE),
            output_weight.T,
        ],
        axis=1,
    ).astype(bf16)
    ff_low = jnp.concatenate(
        [gate_up_weight[0], gate_up_weight[1], down_weight.T], axis=1
    ).astype(bf16)
    gains_low = jnp.pad(norm_gains.astype(bf16).astype(f32), ((0, 6), (0, 0)))
    positions = lax.axis_index("seq") * local_len + jnp.arange(local_len, dtype=jnp.int32)
    cos_table, sin_table = rotary(positions)
    cos_wide = jnp.tile(cos_table, (1, 4))
    sin_wide = jnp.tile(jnp.concatenate([sin_table, -sin_table], axis=1), (1, 2))
    query, pairs, kept, mixed, packed_all, h_first, mid, h_second, ff_all, gains_used = forward(
        tokens, packed, gains_low, ff_low, cos_wide, sin_wide
    )
    branch_own, grad_mid, gain_two, mlp_term, grads = feed_forward(
        h_second,
        cotangent.reshape(count, 8, 32, width),
        ff_all,
        mid,
        gains_used,
    )
    shares_ff = lax.psum_scatter(grads, "seq", scatter_dimension=0, tiled=False)
    part, grads_projection, block_out = backward(
        branch_own,
        query,
        pairs,
        kept,
        mixed,
        packed_all,
        h_first,
        mlp_term,
        mid,
        cos_wide,
        sin_wide,
    )
    (
        input_grad,
        share_query,
        share_pair,
        share_output,
        share_gains,
        share_gate_up,
        share_down,
    ) = ending(
        part,
        grads_projection,
        shares_ff,
        tokens,
        grad_mid,
        gains_used,
        gain_two,
    )

    query_new, query_first_new, query_second_new = adam(
        query_weight, share_query, query_first, query_second, rate_wide, weight_decay
    )
    pair_new, pair_first_new, pair_second_new = adam(
        key_value_weight,
        share_pair[:, None, :],
        key_value_first_moment,
        key_value_second_moment,
        rate_wide,
        weight_decay,
    )
    output_new, output_first_new, output_second_new = adam(
        output_weight,
        share_output,
        output_first,
        output_second,
        rate_output,
        weight_decay,
    )
    gate_up_new, gate_up_first_new, gate_up_second_new = adam(
        gate_up_weight,
        share_gate_up,
        gate_up_first,
        gate_up_second,
        rate_wide,
        weight_decay,
    )
    down_new, down_first_new, down_second_new = adam(
        down_weight, share_down, down_first, down_second, rate_down, weight_decay
    )
    gains_new, gains_first_new, gains_second_new = adam(
        norm_gains, share_gains, gains_first, gains_second, rate_gains, 0.0
    )
    return (
        block_out,
        input_grad,
        query_new,
        query_first_new,
        query_second_new,
        pair_new,
        pair_first_new,
        pair_second_new,
        output_new,
        output_first_new,
        output_second_new,
        gate_up_new,
        gate_up_first_new,
        gate_up_second_new,
        down_new,
        down_first_new,
        down_second_new,
        gains_new,
        gains_first_new,
        gains_second_new,
    )


def solution(mesh):
    return jax.shard_map(
        shards,
        mesh=mesh,
        in_specs=(
            P("dp", "seq", None),
            P("dp", "seq", None),
            P(("dp", "seq"), "tensor"),
            P(("dp", "seq"), "tensor"),
            P(("dp", "seq"), "tensor"),
            P(("dp", "seq"), "tensor", None),
            P(("dp", "seq"), "tensor", None),
            P(("dp", "seq"), "tensor", None),
            P("tensor", ("dp", "seq")),
            P("tensor", ("dp", "seq")),
            P("tensor", ("dp", "seq")),
            P(None, ("dp", "seq"), "tensor"),
            P(None, ("dp", "seq"), "tensor"),
            P(None, ("dp", "seq"), "tensor"),
            P("tensor", ("dp", "seq")),
            P("tensor", ("dp", "seq")),
            P("tensor", ("dp", "seq")),
            P(None, ("dp", "seq")),
            P(None, ("dp", "seq")),
            P(None, ("dp", "seq")),
        ),
        out_specs=(
            P("dp", ("seq", "tensor"), None),
            P("dp", ("seq", "tensor"), None),
            P(("dp", "seq"), "tensor"),
            P(("dp", "seq"), "tensor"),
            P(("dp", "seq"), "tensor"),
            P(("dp", "seq"), "tensor", None),
            P(("dp", "seq"), "tensor", None),
            P(("dp", "seq"), "tensor", None),
            P("tensor", ("dp", "seq")),
            P("tensor", ("dp", "seq")),
            P("tensor", ("dp", "seq")),
            P(None, ("dp", "seq"), "tensor"),
            P(None, ("dp", "seq"), "tensor"),
            P(None, ("dp", "seq"), "tensor"),
            P("tensor", ("dp", "seq")),
            P("tensor", ("dp", "seq")),
            P("tensor", ("dp", "seq")),
            P(None, ("dp", "seq")),
            P(None, ("dp", "seq")),
            P(None, ("dp", "seq")),
        ),
        check_vma=False,
    )
```

```python
import jax
import jax.numpy as jnp
from jax import lax
from jax.experimental import pallas as pl
from jax.experimental.pallas import tpu as pltpu
from jax.sharding import PartitionSpec as P

QUERY_HEADS = 32
KEY_VALUE_HEADS = 8
HEAD_SIZE = 64
STEP = 10
GROUP = QUERY_HEADS // KEY_VALUE_HEADS


norm_eps = 1e-05
rope_base = 500000.0
beta_first = 0.9
beta_second = 0.95
adam_eps = 1e-08
weight_decay = 0.1
rate_wide = 0.07
rate_down = 0.035
rate_output = 1.0
rate_gains = 0.7

bf16 = jnp.bfloat16
f32 = jnp.float32
MESH = pl.DeviceIdType.MESH
VMEM = pl.BlockSpec(memory_space=pltpu.VMEM)
ANY = pl.BlockSpec(memory_space=pl.ANY)
MIB = 1024 * 1024


def inverse_rms(values):
    return lax.rsqrt(jnp.mean(values * values, axis=-1, keepdims=True) + norm_eps)


def rotary(positions):
    half_size = HEAD_SIZE // 2
    freqs = rope_base ** (-2.0 * jnp.arange(half_size, dtype=jnp.float32) / HEAD_SIZE)
    angles = positions.astype(jnp.float32)[:, None] * freqs[None, :]
    return (jnp.cos(angles), jnp.sin(angles))


def adam(master, grad, moment_one, moment_two, rate, decay):
    new_one = beta_first * moment_one + (1.0 - beta_first) * grad
    new_two = beta_second * moment_two + (1.0 - beta_second) * grad * grad
    ahead = (
        new_one
        / (1.0 - beta_first**STEP)
        / (jnp.sqrt(new_two / (1.0 - beta_second**STEP)) + adam_eps)
    )
    return (master - rate * (ahead + decay * master), new_one, new_two)


def tensor_peers():
    me = lax.axis_index("tensor")
    z, y = me // 2, me % 2
    return [
        ((z + dz) % 4) * 2 + (y + dy) % 2
        for dz, dy in ((2, 1), (1, 1), (3, 1), (2, 0), (1, 0), (3, 0), (0, 1))
    ]


def chip_peers():
    dp, seq = lax.axis_index("dp"), lax.axis_index("seq")
    x, core = seq // 2, seq % 2
    return [
        ((dp + dd) % 2, (x + dx) % 4, core)
        for dx, dd in ((2, 1), (1, 1), (3, 1), (0, 1), (2, 0), (1, 0), (3, 0))
    ]


def row_peers():
    seq = lax.axis_index("seq")
    x, core = seq // 2, seq % 2
    return [((x + dx) % 4, core) for dx in (2, 1, 3)]


def sibling():
    seq = lax.axis_index("seq")
    return seq + 1 - 2 * (seq % 2)


def greet(devices):
    barrier = pltpu.get_barrier_semaphore()
    for device in devices:
        pl.semaphore_signal(barrier, inc=1, device_id=device, device_id_type=MESH)
    pl.semaphore_wait(barrier, len(devices))


def remote(src, dst, sends, recvs, at, device):
    return pltpu.make_async_remote_copy(src, dst, sends.at[at], recvs.at[at], device, MESH)


def params(collective_id, mib):
    return pltpu.CompilerParams(
        collective_id=collective_id, has_side_effects=True, vmem_limit_bytes=mib * MIB
    )


def causal_bias(bias):
    seq = lax.axis_index("seq")
    rows, keys = bias.shape
    row = lax.broadcasted_iota(jnp.int32, (rows, keys), 0) + seq * rows
    key = lax.broadcasted_iota(jnp.int32, (rows, keys), 1)
    bias[...] = jnp.where(key <= row, 0.0, -1e30).astype(f32)


def nt(left, right):
    return lax.dot_general(left, right, (((1,), (1,)), ((), ())), preferred_element_type=f32)


def tn(left, right):
    return lax.dot_general(left, right, (((0,), (0,)), ((), ())), preferred_element_type=f32)


def columns(tile, size):
    return pl.ds(pl.multiple_of(tile * size, size), size)


def turn(values, cos_table, sin_table):
    lane = lax.broadcasted_iota(jnp.int32, values.shape, 1)
    half = HEAD_SIZE // 2
    other = jnp.where(
        lane % HEAD_SIZE < half,
        pltpu.roll(values, values.shape[1] - half, 1),
        pltpu.roll(values, half, 1),
    )
    return values * cos_table + other * sin_table


def block_of(peer):
    return pl.ds(pl.multiple_of(peer * 32, 32), 32)


def own_chunks(body):
    def step(k, carry):
        body(k // 2, pl.multiple_of((k % 2) * 16, 16))
        return carry

    lax.fori_loop(0, 6, step, 0)


FIRST = 896
SHIFTS = (2, 1, 3)


def fold_scratch(lead, rows, width):
    rest = width - FIRST
    return [
        pltpu.VMEM(lead + shape, bf16)
        for shape in (
            (3, 2, rows, FIRST),
            (4, rows, rest),
            (3, rows, rest),
            (3, rows, rest),
            (rows, FIRST),
            (rows, FIRST),
        )
    ]


class Fold:
    def __init__(self, source, local, refs, sends, recvs, base):
        tensor = lax.axis_index("tensor")
        self.z, self.y = tensor // 2, tensor % 2
        self.source, self.local = source, local
        self.over_z, self.from_partner, self.ready, self.second, self.mine, self.last = refs
        self.rows, self.width = self.from_partner.shape[1], FIRST + self.from_partner.shape[2]
        self.sends, self.recvs, self.base = sends, recvs, base
        self.copies = {}

    def send(self, k, source, place, z, y):
        copy = remote(
            source, place, self.sends, self.recvs, self.base + k, {"tensor": 2 * (z % 4) + y}
        )
        copy.start()
        self.copies[k] = copy

    def begin(self, dz):
        to = (self.z + dz) % 4
        first, rest = pl.ds(0, FIRST), pl.ds(FIRST, self.width - FIRST)
        if dz:
            k = SHIFTS.index(dz)
            self.send(k, self.source.at[to, :, :, first], self.over_z.at[k], to, self.y)
        self.send(
            3 + dz, self.source.at[to, 1 - self.y, :, rest], self.from_partner.at[dz], self.z,
            1 - self.y,
        )

    def chunks(self, body):
        def step(k, carry):
            body(pl.ds(pl.multiple_of(k * 16, 16), 16))
            return carry

        lax.fori_loop(0, self.rows // 16, step, 0)

    def pass_z(self, dz):
        self.copies[3 + dz].wait_recv()
        if dz == 0:
            return
        k = SHIFTS.index(dz)

        def body(at):
            both = self.local(dz, 0, at)[:, FIRST:] + self.from_partner[dz, at, :].astype(f32)
            self.ready[k, at, :] = both.astype(bf16)

        self.chunks(body)
        self.send(8 + k, self.ready.at[k], self.second.at[k], self.z + dz, self.y)

    def pass_partner(self):
        for k in range(3):
            self.copies[k].wait_recv()

        def body(at):
            result = self.local(0, 1, at)[:, :FIRST]
            for k in range(3):
                result = result + self.over_z[k, 1 - self.y, at, :].astype(f32)
            self.mine[at, :] = result.astype(bf16)

        self.chunks(body)
        self.send(7, self.mine, self.last, self.z, 1 - self.y)

    def finish(self):
        for k in (7, 8, 9, 10):
            self.copies[k].wait_recv()
        for copy in self.copies.values():
            copy.wait_send()

    def total(self, at):
        own = self.local(0, 0, at)
        low = own[:, :FIRST] + self.last[at, :].astype(f32)
        high = own[:, FIRST:] + self.from_partner[0, at, :].astype(f32)
        for k in range(3):
            low = low + self.over_z[k, self.y, at, :].astype(f32)
            high = high + self.second[k, at, :].astype(f32)
        return jnp.concatenate([low, high], axis=1)


class Weights:
    def __init__(self, mine, whole, sends, recvs, near_sends, near_recvs):
        self.dp, self.seq = lax.axis_index("dp"), lax.axis_index("seq")
        self.mine, self.whole = mine, whole
        self.sends, self.recvs = sends, recvs
        self.near_sends, self.near_recvs = near_sends, near_recvs
        self.started, self.passed = {}, []

    def owner(self, dx, dd):
        x, core = self.seq // 2, self.seq % 2
        return (self.dp + dd) % 2, ((x + dx) % 4) * 2 + core

    def device(self, dx, dd):
        dp, seq = self.owner(dx, dd)
        return {"dp": dp, "seq": seq}

    def view(self, dx, dd, half=None):
        ref = self.whole.at[self.owner(dx, dd)]
        return ref if half is None else ref.at[pl.ds(64 * half, 64)]

    def send(self, k, block, to, half=None):
        place = self.view(*block, half)
        source = place
        if block == (0, 0):
            source = self.mine if half is None else self.mine.at[pl.ds(64 * half, 64)]
        copy = remote(source, place, self.sends, self.recvs, k, self.device(*to))
        copy.start()
        self.started[k] = copy

    def beside(self, k, block, half=None):
        place = self.view(*block, half)
        source = self.mine if block == (0, 0) else place
        copy = remote(source, place, self.near_sends, self.near_recvs, k, {"seq": sibling()})
        copy.start()
        self.passed.append(copy)

    def start(self):
        self.send(0, (0, 0), (0, 1))
        self.send(1, (0, 0), (1, 0), 0)
        self.send(2, (0, 0), (3, 0), 0)
        self.beside(0, (0, 0))

    def rest(self):
        self.send(3, (0, 0), (1, 0), 1)
        self.send(4, (0, 0), (3, 0), 1)

    def partner(self):
        self.started[0].wait_recv()
        self.send(5, (0, 1), (1, 0))
        self.send(6, (0, 1), (3, 0))
        self.beside(1, (0, 1))

    def own_ring(self):
        self.started[1].wait_recv()
        self.send(7, (3, 0), (1, 0), 0)
        self.started[4].wait_recv()
        self.send(8, (1, 0), (3, 0), 1)
        self.started[3].wait_recv()
        self.beside(2, (3, 0))
        self.started[2].wait_recv()
        self.beside(3, (1, 0))

    def partner_ring(self):
        self.started[5].wait_recv()
        self.send(9, (3, 1), (1, 0), 0)
        self.beside(4, (3, 1))
        self.started[6].wait_recv()
        self.send(10, (1, 1), (3, 0), 1)
        self.beside(5, (1, 1))

    def finish(self):
        for k, half, dd in ((7, 0, 0), (8, 1, 0), (9, 0, 1), (10, 1, 1)):
            self.started[k].wait_recv()
            self.beside(k - 1, (2, dd), half)
        for copy in self.started.values():
            copy.wait_send()
        for copy in self.passed:
            copy.wait()


def forward_kernel(
    tokens, mine, gains_mine, ff_mine, cos_table, sin_table,
    query_out, pairs_out, kept_out, mixed_out, packed_out, first_out, mid, rows_in, ff_all, gains,
    query, pairs, kept, mixed, packed, h_first, part, over_z, from_partner, ready, second, own_first, last_first, bias,
    sends, recvs, near_sends, near_recvs, late_sends, late_recvs, late_near_sends,
    late_near_recvs, gain_sends, gain_recvs, pair_sends, pair_recvs,
    pair_near_sends, pair_near_recvs, out_sends, out_recvs, ff_sends, ff_recvs, ff_near_sends,
    ff_near_recvs, row_sends, row_recvs, local, stores,
):
    dp, seq, tensor = lax.axis_index("dp"), lax.axis_index("seq"), lax.axis_index("tensor")
    me = dp * 8 + seq
    stored = []

    def store(source, place):
        copy = pltpu.make_async_copy(source, place, stores.at[len(stored)])
        copy.start()
        stored.append(copy)

    count, rows, width = tokens.shape
    keys = bias.shape[1]
    near = {"seq": sibling()}
    owners = [((dp + k // 8) % 2, (seq + k % 8) % 8) for k in range(1, 16)]
    greet(
        [{"tensor": peer} for peer in tensor_peers()] + [{"dp": d, "seq": s} for d, s in owners]
    )
    gain_at = pl.ds(pl.multiple_of(me * 128, 128), 128)
    gain_copies = [
        remote(gains_mine, gains.at[:, gain_at], gain_sends, gain_recvs, k, {"dp": d, "seq": s})
        for k, (d, s) in enumerate(owners)
    ]
    for copy in gain_copies:
        copy.start()
    early, late = pl.ds(0, 384), pl.ds(384, 256)
    out, out_late = [
        [
            remote(
                mine.at[:, at], packed.at[me, :, at], ss, rs, i, {"dp": d, "seq": 2 * x + c}
            )
            for i, (d, x, c) in enumerate(chip_peers())
        ]
        for at, ss, rs in ((early, sends, recvs), (late, late_sends, late_recvs))
    ]
    first, first_late = [
        remote(mine.at[:, at], packed.at[me, :, at], ss, rs, 7, near)
        for at, ss, rs in (
            (early, near_sends, near_recvs),
            (late, late_near_sends, late_near_recvs),
        )
    ]
    for copy in out + [first] + out_late + [first_late]:
        copy.start()
    ff = Weights(ff_mine, ff_all, ff_sends, ff_recvs, ff_near_sends, ff_near_recvs)
    ff.start()
    store_ff = pltpu.make_async_copy(ff_mine, ff_all.at[dp, seq], local)
    store_ff.start()
    packed[me] = mine[...]
    gains[:, gain_at] = gains_mine[...]
    causal_bias(bias)
    for copy in gain_copies:
        copy.wait()

    def normalize(k, carry):
        i = k // 16
        at = pl.ds(pl.multiple_of((k % 16) * 16, 16), 16)
        token_rows = tokens[i, at, :].astype(f32)
        h_first[i, at, :] = (token_rows * inverse_rms(token_rows) * gains[0:1, :]).astype(bf16)
        return carry

    lax.fori_loop(0, count * 16, normalize, 0)
    store(h_first, first_out)

    def pass_weights(out, first, at, ss, rs):
        passed = [first]
        for i, (dd, dx) in (
            (6, (0, 1)), (5, (0, 3)), (3, (1, 0)), (4, (0, 2)), (2, (1, 1)), (1, (1, 3)), (0, (1, 2)),
        ):
            out[i].wait_recv()
            owner = (((dp + dd) % 2) * 4 + (seq // 2 + dx) % 4) * 2 + seq % 2
            block = packed.at[owner, :, at]
            copy = remote(block, block, ss, rs, i, near)
            copy.start()
            passed.append(copy)
        return passed

    for copy in pass_weights(out, first, early, near_sends, near_recvs):
        copy.wait()
    scale = HEAD_SIZE ** (-0.5)
    lane = lax.broadcasted_iota(jnp.int32, (rows, 2 * HEAD_SIZE), 1)

    def project(i, carry):
        raw = jnp.dot(
            h_first[i], packed[:, :, :384].reshape(width, 384), preferred_element_type=f32
        )
        for at in range(GROUP // 2):
            both = raw[:, at * 2 * HEAD_SIZE : (at + 1) * 2 * HEAD_SIZE]
            both = turn(both, cos_table[...], -sin_table[...]) * scale
            query[i, 2 * at] = jnp.where(lane < HEAD_SIZE, both, 0.0).astype(bf16)
            moved = pltpu.roll(both, HEAD_SIZE, 1)
            query[i, 2 * at + 1] = jnp.where(lane < HEAD_SIZE, moved, 0.0).astype(bf16)
        pair = raw[:, GROUP * HEAD_SIZE :]
        turned = turn(pair, cos_table[...], -sin_table[...])
        pairs[seq, i] = jnp.where(lane < HEAD_SIZE, turned, pair).astype(bf16)
        return carry

    lax.fori_loop(0, count, project, 0)
    pair_out = [
        remote(pairs.at[seq], pairs.at[seq], pair_sends, pair_recvs, i, {"seq": 2 * x + c})
        for i, (x, c) in enumerate(row_peers())
    ]
    for copy in pair_out:
        copy.start()
    pair_first = remote(pairs.at[seq], pairs.at[seq], pair_near_sends, pair_near_recvs, 3, near)
    pair_first.start()
    ff.rest()
    pair_passed = []
    for i, dx in ((1, 3), (2, 1), (0, 2)):
        pair_out[i].wait_recv()
        owner = ((seq // 2 + dx) % 4) * 2 + seq % 2
        forward = remote(
            pairs.at[owner], pairs.at[owner], pair_near_sends, pair_near_recvs, i, near
        )
        forward.start()
        pair_passed.append(forward)
    pair_first.wait()
    for copy in pair_passed:
        copy.wait()
    store(query, query_out)
    store(pairs, pairs_out)
    passed_late = pass_weights(out_late, first_late, late, late_near_sends, late_near_recvs)
    ff.partner()

    def attend(i):
        upper = []
        pair = pairs[:, i].reshape(keys, 2 * HEAD_SIZE)
        for head in range(GROUP):
            scores = nt(query[i, head], pair) + bias[...]
            row_max = jnp.max(scores, axis=-1, keepdims=True)
            exps = jnp.exp(scores - row_max)
            row_sum = jnp.sum(exps, axis=-1, keepdims=True)
            mix = jnp.dot(exps.astype(bf16), pair, preferred_element_type=f32) / row_sum
            kept[i, head] = jnp.where(lane < HEAD_SIZE, row_max + jnp.log(row_sum), mix)
            upper.append(mix)
        for at in range(GROUP // 2):
            low = pltpu.roll(upper[2 * at], HEAD_SIZE, 1)
            both = jnp.where(lane < HEAD_SIZE, low, upper[2 * at + 1])
            mixed[i, :, at * 2 * HEAD_SIZE : (at + 1) * 2 * HEAD_SIZE] = both.astype(bf16)

    def attend_step(i, carry):
        attend(i)
        return carry

    def output_step(i, carry):
        def term(tile, inner_carry):
            weight_rows = packed[pl.ds(tile * 4, 4), :, 384:640].reshape(512, 256)
            product = nt(mixed[i], weight_rows).astype(bf16)
            part[i, :, :, :, columns(tile, 512)] = product.reshape(4, 2, 32, 512)
            return inner_carry

        lax.fori_loop(0, width // 512, term, 0)
        return carry

    def term_of(i):
        def local(dz, dy, at):
            return part[i, (tensor // 2 + dz) % 4, (tensor + dy) % 2, at, :].astype(f32)

        return local

    folds = []
    for i in range(count):
        lax.fori_loop(i, i + 1, attend_step, 0)
        if i == 0:
            for copy in passed_late:
                copy.wait()
            store(packed, packed_out)
        lax.fori_loop(i, i + 1, output_step, 0)
        fold = Fold(
            part.at[i],
            term_of(i),
            [ref.at[i] for ref in (over_z, from_partner, ready, second, own_first, last_first)],
            out_sends,
            out_recvs,
            11 * i,
        )
        for dz in (2, 1, 3, 0):
            fold.begin(dz)
        folds.append(fold)
        if i:
            for dz in (2, 1, 3, 0):
                folds[i - 1].pass_z(dz)
        if i == 1:
            ff.own_ring()
    store(kept, kept_out)
    store(mixed, mixed_out)
    folds[0].pass_partner()
    for dz in (2, 1, 3, 0):
        folds[2].pass_z(dz)
    folds[1].pass_partner()
    ff.partner_ring()
    folds[2].pass_partner()
    for i, fold in enumerate(folds):
        fold.finish()

        def chunk(k, carry, i=i, fold=fold):
            row = pl.multiple_of(k * 16, 16)
            at = pl.ds(pl.multiple_of(tensor * 32 + row, 16), 16)
            result = fold.total(pl.ds(row, 16)) + tokens[i, at, :].astype(f32)
            at = pl.ds(pl.multiple_of(i * 32 + row, 16), 16)
            mid[at, :] = result
            rows_in[0, at, :] = (result * inverse_rms(result) * gains[1:2, :]).astype(bf16)
            return carry

        lax.fori_loop(0, 2, chunk, 0)
    z, y = tensor // 2, tensor % 2
    row_copies = [
        remote(
            rows_in.at[0], rows_in.at[k + 1], row_sends, row_recvs, k,
            {"tensor": 2 * ((z + dz) % 4) + (y + dy) % 2},
        )
        for k, (dz, dy) in enumerate(((0, 1), (1, 0), (3, 0)))
    ]
    for copy in row_copies:
        copy.start()
    for copy in out + out_late + pair_out:
        copy.wait_send()
    store_ff.wait()
    ff.finish()
    for copy in row_copies + stored:
        copy.wait()


def forward(tokens, mine, gains_mine, ff_mine, cos_table, sin_table):
    count, rows, width = tokens.shape
    dma = pltpu.SemaphoreType.DMA
    lanes = 2 * HEAD_SIZE
    return pl.pallas_call(
        forward_kernel,
        out_shape=(
            jax.ShapeDtypeStruct((count, GROUP, rows, lanes), bf16),
            jax.ShapeDtypeStruct((8, count, rows, lanes), bf16),
            jax.ShapeDtypeStruct((count, GROUP, rows, lanes), f32),
            jax.ShapeDtypeStruct((count, rows, GROUP * HEAD_SIZE), bf16),
            jax.ShapeDtypeStruct((16,) + mine.shape, bf16),
            jax.ShapeDtypeStruct((count, rows, width), bf16),
            jax.ShapeDtypeStruct((count * 32, width), f32),
            jax.ShapeDtypeStruct((4, count * 32, width), bf16),
            jax.ShapeDtypeStruct((2, 8) + ff_mine.shape, bf16),
            jax.ShapeDtypeStruct((8, width), f32),
        ),
        in_specs=[VMEM] * 6,
        out_specs=(ANY,) * 6 + (VMEM, VMEM, ANY, VMEM),
        scratch_shapes=[
            pltpu.VMEM((count, GROUP, rows, lanes), bf16),
            pltpu.VMEM((8, count, rows, lanes), bf16),
            pltpu.VMEM((count, GROUP, rows, lanes), f32),
            pltpu.VMEM((count, rows, GROUP * HEAD_SIZE), bf16),
            pltpu.VMEM((16,) + mine.shape, bf16),
            pltpu.VMEM((count, rows, width), bf16),
            pltpu.VMEM((count, 4, 2, 32, width), bf16),
            *fold_scratch((count,), 32, width),
            pltpu.VMEM((rows, 8 * rows), f32),
            dma((7,)), dma((7,)), dma((8,)), dma((8,)), dma((7,)), dma((7,)), dma((8,)), dma((8,)),
            dma((15,)), dma((15,)), dma((3,)), dma((3,)),
            dma((4,)), dma((4,)), dma((33,)), dma((33,)), dma((11,)), dma((11,)), dma((10,)),
            dma((10,)), dma((3,)), dma((3,)), dma, dma((6,)),
        ],
        compiler_params=params(1, 60),
        cost_estimate=pl.CostEstimate(flops=40000 * MIB, bytes_accessed=200 * MIB, transcendentals=0),
        name="forward",
    )(tokens, mine, gains_mine, ff_mine, cos_table, sin_table)


class Spread:
    def __init__(self, buffer, sends, recvs):
        tensor = lax.axis_index("tensor")
        self.buffer, self.sends, self.recvs = buffer, sends, recvs
        self.z, self.y = tensor // 2, tensor % 2
        self.started = {}

    def at(self, dz, dy):
        return ((self.z + dz) % 4) * 2 + (self.y + dy) % 2

    def send(self, k, block, to, half=None):
        ref = self.buffer.at[block]
        if half is not None:
            rows = self.buffer.shape[1] // 2
            ref = self.buffer.at[block, pl.ds(half * rows, rows)]
        copy = remote(ref, ref, self.sends, self.recvs, k, {"tensor": to})
        copy.start()
        self.started[k] = copy

    def pass_partner(self):
        self.send(3, self.at(0, 1), self.at(1, 0))
        self.send(4, self.at(0, 1), self.at(3, 0))

    def pass_on(self, dy):
        if dy:
            self.started[3].wait_recv()
        self.send(5 + 2 * dy, self.at(3, dy), self.at(1, 0), 0)
        if dy:
            self.started[4].wait_recv()
        self.send(6 + 2 * dy, self.at(1, dy), self.at(3, 0), 1)

    def finish(self):
        for k in range(5, 9):
            self.started[k].wait_recv()

    def drain(self):
        for copy in self.started.values():
            copy.wait_send()


def feed_forward_kernel(
    own, cotangent, weights, mid, gain,
    branch, grad_mid, grad_gain, mlp_out, grads_out,
    gate_up, down, cot, normed, grad_hidden, grad_units, hidden, second,
    over_z, from_partner, ready, second_in, own_first, last_first, mlp, grads,
    sends, recvs, back_sends, back_recvs, local, cot_sems, out_sems, mlp_sem,
):
    tensor = lax.axis_index("tensor")
    units = down.shape[3]
    width = 16 * 128
    dp = lax.axis_index("dp")
    load_down = pltpu.make_async_copy(
        weights.at[:, :, :, pl.ds(2 * units, units)], down, local.at[0]
    )
    load_gate_up = pltpu.make_async_copy(
        weights.at[:, :, :, pl.ds(0, 2 * units)], gate_up, local.at[1]
    )
    load_down.start()
    load_cot = [
        pltpu.make_async_copy(cotangent.at[:, t], cot.at[t], cot_sems.at[t]) for t in range(8)
    ]
    for copy in load_cot:
        copy.start()
    load_gate_up.start()
    greet([{"tensor": peer} for peer in tensor_peers()])
    spread = Spread(normed, sends, recvs)
    for k, (dz, dy) in enumerate(((0, 0), (0, 1), (3, 0), (1, 0))):
        normed[spread.at(dz, dy)] = own[k]
    spread.pass_partner()
    spread.pass_on(0)
    for copy in load_cot:
        copy.wait()
    load_down.wait()

    def hidden_step(tile, carry):
        at = columns(tile, 256)
        product = jnp.dot(
            cot[...].reshape(8 * 96, width),
            down[:, :, :, at].reshape(width, 256),
            preferred_element_type=f32,
        )
        grad_hidden[:, :, at] = product.reshape(8, 96, 256)
        return carry

    lax.fori_loop(0, units // 256, hidden_step, 0)
    load_gate_up.wait()

    def own_term(dz, dy, at):
        return second[(spread.z + dz) % 4, (spread.y + dy) % 2, at, :].astype(f32)

    fold = Fold(
        second,
        own_term,
        (over_z, from_partner, ready, second_in, own_first, last_first),
        back_sends,
        back_recvs,
        0,
    )

    def block(dz):
        first = ((spread.z + dz) % 4) * 2
        both = pl.ds(first, 2)

        def units_step(tile, carry):
            at = columns(tile, 256)
            up_at = pl.ds(pl.multiple_of(units + tile * 256, 256), 256)
            rows = normed[both].reshape(192, width)
            gate_columns = gate_up[:, :, :, at].reshape(width, 256)
            up_columns = gate_up[:, :, :, up_at].reshape(width, 256)
            gate_in = jnp.dot(rows, gate_columns, preferred_element_type=f32)
            up_in = jnp.dot(rows, up_columns, preferred_element_type=f32)
            grad = grad_hidden[both, :, at].reshape(192, 256)
            sigmoid = jax.nn.sigmoid(gate_in)
            silu = gate_in * sigmoid
            hidden[both, :, at] = (silu * up_in).astype(bf16).reshape(2, 96, 256)
            grad_gate = grad * up_in * sigmoid * (1.0 + gate_in * (1.0 - sigmoid))
            grad_units[both, :, at] = grad_gate.astype(bf16).reshape(2, 96, 256)
            grad_units[both, :, up_at] = (grad * silu).astype(bf16).reshape(2, 96, 256)
            return carry

        lax.fori_loop(0, units // 256, units_step, 0)

        def second_step(tile, carry):
            at = columns(tile, 512)
            rows = grad_units[both].reshape(192, 2 * units)
            weight_rows = gate_up[tile // 2, pl.ds((tile % 2) * 4, 4)].reshape(512, 2 * units)
            product = nt(rows, weight_rows).astype(bf16)
            second[first // 2, :, :, at] = product.reshape(2, 96, 512)
            return carry

        lax.fori_loop(0, width // 512, second_step, 0)
        fold.begin(dz)

    block(0)
    spread.pass_on(1)
    block(1)
    fold.pass_z(0)
    block(3)
    fold.pass_z(1)
    spread.finish()
    block(2)
    fold.pass_z(3)

    def mlp_step(tile, carry):
        at = columns(tile, 256)
        rows = hidden[...].reshape(8 * 96, units)
        weight_rows = down[tile // 4, pl.ds((tile % 4) * 2, 2)].reshape(256, units)
        mlp[:, :, at] = nt(rows, weight_rows).astype(bf16).reshape(8, 96, 256)
        return carry

    lax.fori_loop(0, width // 512, mlp_step, 0)
    fold.pass_z(2)
    lax.fori_loop(width // 512, width // 256, mlp_step, 0)
    store_mlp = pltpu.make_async_copy(mlp, mlp_out, mlp_sem)
    store_mlp.start()

    def store(tile, slot):
        place = grads_out.at[pl.ds((tile % 4) * 2, 2), (tile // 4 + dp) % 2]
        return pltpu.make_async_copy(grads.at[slot], place, out_sems.at[slot])

    def grads_pair(pair, carry):
        for slot in range(2):
            tile = 2 * pair + slot
            at = columns(tile, 256)

            @pl.when(pair > 0)
            def _():
                store(tile - 2, slot).wait()

            wide = tn(
                normed[:, :, at].reshape(8 * 96, 256), grad_units[...].reshape(8 * 96, 2 * units)
            )
            grads[slot, :, :, : 2 * units] = wide.astype(bf16).reshape(2, 128, 2 * units)
            narrow = tn(cot[:, :, :, at].reshape(8 * 96, 256), hidden[...].reshape(8 * 96, units))
            grads[slot, :, :, 2 * units :] = narrow.astype(bf16).reshape(2, 128, units)
            store(tile, slot).start()
        return carry

    tiles = width // 256
    lax.fori_loop(0, tiles // 2 - 1, grads_pair, 0)
    fold.pass_partner()
    lax.fori_loop(tiles // 2 - 1, tiles // 2, grads_pair, 0)
    for slot in range(2):
        store(tiles - 2 + slot, slot).wait()
    store_mlp.wait()
    spread.drain()
    fold.finish()
    grad_gain[...] = jnp.zeros_like(grad_gain)

    def chunk(k, carry):
        at = pl.ds(pl.multiple_of(k * 16, 16), 16)
        grad = fold.total(at)
        rows = mid[at, :]
        inverse = inverse_rms(rows)
        normed_rows = rows * inverse
        product = grad * normed_rows
        grad_gain[...] += product[:8] + product[8:]
        inner = jnp.mean(product * gain[1:2, :], axis=-1, keepdims=True)
        own_cot = cot[tensor, k // 2, pl.ds(pl.multiple_of((k % 2) * 16, 16), 16), :].astype(f32)
        result = own_cot + inverse * (grad * gain[1:2, :] - normed_rows * inner)
        grad_mid[at, :] = result
        branch[at, :] = result.astype(bf16)
        return carry

    lax.fori_loop(0, 6, chunk, 0)


def feed_forward(own, cotangent, weights, mid, gain):
    rows, width = mid.shape
    units = weights.shape[3] // 3
    dma = pltpu.SemaphoreType.DMA
    return pl.pallas_call(
        feed_forward_kernel,
        out_shape=(
            jax.ShapeDtypeStruct((rows, width), bf16),
            jax.ShapeDtypeStruct((rows, width), f32),
            jax.ShapeDtypeStruct((8, width), f32),
            jax.ShapeDtypeStruct((8, rows, width), bf16),
            jax.ShapeDtypeStruct((8, 2) + weights.shape[2:], bf16),
        ),
        in_specs=[VMEM, ANY, ANY, VMEM, VMEM],
        out_specs=(VMEM, VMEM, VMEM, ANY, ANY),
        scratch_shapes=[
            pltpu.VMEM((2, 8, 128, 2 * units), bf16),
            pltpu.VMEM((2, 8, 128, units), bf16),
            pltpu.VMEM((8, 3, 32, width), bf16),
            pltpu.VMEM((8, rows, width), bf16),
            pltpu.VMEM((8, rows, units), f32),
            pltpu.VMEM((8, rows, 2 * units), bf16),
            pltpu.VMEM((8, rows, units), bf16),
            pltpu.VMEM((4, 2, rows, width), bf16),
            *fold_scratch((), rows, width),
            pltpu.VMEM((8, rows, width), bf16),
            pltpu.VMEM((2, 2, 128, 3 * units), bf16),
            dma((9,)), dma((9,)), dma((11,)), dma((11,)), dma((2,)), dma((8,)), dma((2,)), dma,
        ],
        compiler_params=params(5, 60),
        cost_estimate=pl.CostEstimate(
            flops=18 * 8 * rows * width * units, bytes_accessed=120 * MIB, transcendentals=0
        ),
        name="feed_forward",
    )(own, cotangent, weights, mid, gain)


def backward_kernel(
    branch, query_hbm, pairs_hbm, kept_hbm, mixed_hbm, packed_hbm, first_hbm, mlp_part, mid_hbm,
    cos_table, sin_table,
    part, ready, block_out,
    query, pairs, kept, mixed, packed, h_first, mid,
    whole, attended, raw, grad_pairs, near_pairs, ready_pairs, landed_pairs, bias, total, weights,
    near, mlp_own, mlp_pair, over_z, from_partner, ready_rows, second, own_first, last_first,
    out_sends, out_recvs, pair_near_sends, pair_near_recvs, pair_sends, pair_recvs, near_sends,
    near_recvs, mlp_sends, mlp_recvs, local,
):
    dp, seq, tensor = lax.axis_index("dp"), lax.axis_index("seq"), lax.axis_index("tensor")
    x, core = seq // 2, seq % 2
    peers = tensor_peers()
    rows_beside = row_peers()
    beside = {"seq": sibling()}
    z, y = tensor // 2, tensor % 2
    count, width = whole.shape[0], whole.shape[2]
    rows, keys = bias.shape
    loads = [
        pltpu.make_async_copy(source, place, local.at[k])
        for k, (source, place) in enumerate(
            (
                (packed_hbm, packed),
                (pairs_hbm, pairs),
                (query_hbm, query),
                (kept_hbm, kept),
                (mixed_hbm, mixed),
                (first_hbm, h_first),
                (mid_hbm, mid),
                (mlp_part.at[:, y], mlp_own),
                (mlp_part.at[z, 1 - y], mlp_pair),
            )
        )
    ]
    for copy in loads:
        copy.start()
    greet(
        [{"tensor": peer} for peer in peers]
        + [{"seq": 2 * px + c} for px, c in rows_beside]
        + [beside]
    )
    mine = pl.ds(pl.multiple_of(tensor * 32, 32), 32)
    spread = [
        remote(
            branch.at[pl.ds(32 * i, 32)], whole.at[i, mine], out_sends, out_recvs, 7 * i + k,
            {"tensor": peer},
        )
        for i in range(count)
        for k, peer in enumerate(peers)
    ]
    for copy in spread:
        copy.start()

    def mlp_term(dz, dy, at):
        rows_here = mlp_pair[at, :] if dy else mlp_own[(z + dz) % 4, at, :]
        return rows_here.astype(f32)

    fold = Fold(
        mlp_part,
        mlp_term,
        (over_z, from_partner, ready_rows, second, own_first, last_first),
        mlp_sends,
        mlp_recvs,
        0,
    )
    for dz in (2, 1, 3, 0):
        fold.begin(dz)
    for i in range(count):
        whole[i, mine, :] = branch[32 * i : 32 * i + 32, :]
    causal_bias(bias)
    for copy in loads:
        copy.wait()
    lane = lax.broadcasted_iota(jnp.int32, (rows, 2 * HEAD_SIZE), 1)
    scale = HEAD_SIZE ** (-0.5)

    def sequence(i):
        for copy in spread[7 * i : 7 * i + 7]:
            copy.wait_recv()
        attended[...] = (
            jnp.dot(
                whole[i], packed[:, :, 384:640].reshape(width, 256), preferred_element_type=f32
            )
            .astype(bf16)
            .astype(f32)
        )
        total[...] = jnp.zeros_like(total)

        def head_pair(at, carry):
            columns_at = columns(at, 2 * HEAD_SIZE)
            grads_here = attended[:, columns_at]
            grad_query = []
            for odd in range(2):
                pair = pairs[:, i].reshape(keys, 2 * HEAD_SIZE)
                placed = grads_here if odd else pltpu.roll(grads_here, HEAD_SIZE, 1)
                placed = jnp.where(lane >= HEAD_SIZE, placed, 0.0)
                grad_rows = placed.astype(bf16)
                query_rows = query[i, 2 * at + odd]
                kept_rows = kept[i, 2 * at + odd]
                probs = jnp.exp(nt(query_rows, pair) + bias[...] - kept_rows[:, :1])
                inner = jnp.sum(kept_rows * placed, axis=-1, keepdims=True)
                grad_scores = (probs * (nt(grad_rows, pair) - inner)).astype(bf16)
                grad_query.append(jnp.dot(grad_scores, pair, preferred_element_type=f32))
                total[...] += jnp.dot(
                    query_rows.T, grad_scores, preferred_element_type=f32
                ) + jnp.dot(grad_rows.T, probs.astype(bf16), preferred_element_type=f32)
            both = jnp.where(lane < HEAD_SIZE, grad_query[0], pltpu.roll(grad_query[1], HEAD_SIZE, 1))
            both = turn(both * scale, cos_table[...], sin_table[...])
            raw[i, :, columns_at] = both.astype(bf16)
            return carry

        lax.fori_loop(0, GROUP // 2, head_pair, 0)
        for block in range(8):
            grad_pairs[block // 2, block % 2, i] = (
                total[:, block * rows : (block + 1) * rows].T.astype(bf16)
            )

    def cross(i):
        copy = remote(
            grad_pairs.at[:, 1 - core, i], near_pairs.at[i], pair_near_sends, pair_near_recvs, i,
            beside,
        )
        copy.start()
        return copy

    def onward(i, crossing):
        crossing.wait()
        out = []
        for k, (px, c) in enumerate(rows_beside):
            both = grad_pairs[px, core, i].astype(f32) + near_pairs[i, px].astype(f32)
            ready_pairs[i, k] = both.astype(bf16)
            copy = remote(
                ready_pairs.at[i, k], landed_pairs.at[i, k], pair_sends, pair_recvs, 3 * i + k,
                {"seq": 2 * px + c},
            )
            copy.start()
            out.append(copy)
        return out

    def settle(i, moving):
        mine_pairs = grad_pairs[x, core, i].astype(f32) + near_pairs[i, x].astype(f32)
        for k, copy in enumerate(moving):
            copy.wait()
            mine_pairs = mine_pairs + landed_pairs[i, k].astype(f32)
        turned = turn(mine_pairs, cos_table[...], sin_table[...])
        raw[i, :, 256:] = jnp.where(lane < HEAD_SIZE, turned, mine_pairs).astype(bf16)

        def term(tile, carry):
            at = columns(tile, 512)
            weight_rows = packed[pl.ds(tile * 4, 4), :, :384].reshape(512, 384)
            product = nt(raw[i], weight_rows).astype(bf16)
            part[i, :, :, :, at] = product.reshape(4, 2, 32, 512)
            return carry

        lax.fori_loop(0, width // 512, term, 0)

    def outer(tile, carry):
        at = columns(tile, 256)
        product = tn(
            whole[:, :, at].reshape(count * rows, 256), mixed[...].reshape(count * rows, 256)
        )
        weights[tile, :, :, 256:512] = product.astype(bf16).reshape(2, 128, 256)
        return carry

    def query_weights(tile, carry):
        at = columns(tile, 256)
        product = tn(
            h_first[:, :, at].reshape(count * rows, 256), raw[:, :, :256].reshape(count * rows, 256)
        )
        weights[tile, :, :, :256] = product.astype(bf16).reshape(2, 128, 256)
        return carry

    def pair_weights(tile, carry):
        at = columns(tile, 512)
        product = tn(
            h_first[:, :, at].reshape(count * rows, 512), raw[:, :, 256:].reshape(count * rows, 128)
        )
        weights[pl.ds(2 * tile, 2), :, :, 512:] = product.astype(bf16).reshape(2, 2, 128, 128)
        return carry

    sequence(0)
    crossing = cross(0)
    sequence(1)
    moving = onward(0, crossing)
    crossing = cross(1)
    settle(0, moving)
    sequence(2)
    crossing_last = cross(2)
    moving = onward(1, crossing)
    for dz in (2, 1, 3, 0):
        fold.pass_z(dz)
    lax.fori_loop(0, width // 256, outer, 0)
    moving_last = onward(2, crossing_last)
    settle(1, moving)
    lax.fori_loop(0, width // 256, query_weights, 0)
    settle(2, moving_last)
    fold.pass_partner()
    lax.fori_loop(0, width // 512, pair_weights, 0)
    across = remote(weights.at[:, 1 - core], near, near_sends, near_recvs, 0, beside)
    across.start()
    for copy in spread:
        copy.wait_send()
    across.wait()
    for at in range(8):
        ready[at] = (weights[at, core].astype(f32) + near[at].astype(f32)).astype(bf16)
    fold.finish()

    def finish_rows(i, row):
        at = pl.ds(pl.multiple_of(i * 32 + row, 16), 16)
        result = mid[at, :] + fold.total(at)
        block_out[i, pl.ds(row, 16), :] = result.astype(bf16)

    own_chunks(finish_rows)


def backward(
    branch, query, pairs, kept, mixed, packed, h_first, mlp_part, mid, cos_table, sin_table
):
    count, rows, width = h_first.shape
    mlp_part = mlp_part.reshape((4, 2) + mlp_part.shape[1:])
    keys = pairs.shape[0] * rows
    pair_rows = (rows, 2 * HEAD_SIZE)
    own = mid.shape[0]
    dma = pltpu.SemaphoreType.DMA
    vmem = pltpu.VMEM
    return pl.pallas_call(
        backward_kernel,
        out_shape=(
            jax.ShapeDtypeStruct((count, 4, 2, 32, width), bf16),
            jax.ShapeDtypeStruct((8, 128, 640), bf16),
            jax.ShapeDtypeStruct((count, 32, width), bf16),
        ),
        in_specs=[VMEM] + [ANY] * 8 + [VMEM] * 2,
        out_specs=(VMEM,) * 3,
        scratch_shapes=[
            vmem(query.shape, bf16),
            vmem(pairs.shape, bf16),
            vmem(kept.shape, f32),
            vmem(mixed.shape, bf16),
            vmem(packed.shape, bf16),
            vmem(h_first.shape, bf16),
            vmem(mid.shape, f32),
            vmem((count, rows, width), bf16),
            vmem((rows, GROUP * HEAD_SIZE), f32),
            vmem((count, rows, 384), bf16),
            vmem((4, 2, count) + pair_rows, bf16),
            vmem((count, 4) + pair_rows, bf16),
            vmem((count, 3) + pair_rows, bf16),
            vmem((count, 3) + pair_rows, bf16),
            vmem((rows, keys), f32),
            vmem((2 * HEAD_SIZE, keys), f32),
            vmem((8, 2, 128, 640), bf16),
            vmem((8, 128, 640), bf16),
            vmem((4, own, width), bf16),
            vmem((own, width), bf16),
            *fold_scratch((), own, width),
            dma((21,)), dma((21,)), dma((3,)), dma((3,)), dma((9,)), dma((9,)), dma((1,)), dma((1,)),
            dma((11,)), dma((11,)), dma((9,)),
        ],
        compiler_params=params(7, 62),
        cost_estimate=pl.CostEstimate(flops=40000 * MIB, bytes_accessed=200 * MIB, transcendentals=0),
        name="backward",
    )(
        branch, query, pairs, kept, mixed, packed, h_first, mlp_part, mid, cos_table, sin_table
    )


def ending_kernel(
    part, weights, ff, tokens_hbm, grad_mid_hbm, gain, gain_two,
    input_grad, share_query, share_pair, share_output, gain_sum, share_gate_up, share_down,
    part_own, weights_own, ff_own, tokens, grad_mid, landed, ours, partner, landed_last, shares, ff_in, grads, gains, gains_in, gains_near,
    sends, recvs, last_sends, last_recvs, far_sends, far_recvs, ff_sends, ff_recvs,
    gain_sends, gain_recvs, gain_last_sends, gain_last_recvs, local,
):
    dp, seq, tensor = lax.axis_index("dp"), lax.axis_index("seq"), lax.axis_index("tensor")
    z, y = tensor // 2, tensor % 2
    peers = tensor_peers()
    chips = chip_peers()
    owners = [((dp + k // 8) % 2, (seq + k % 8) % 8) for k in range(1, 16)]
    count = part.shape[0]
    units = share_down.shape[0]
    here = dp * 4 + seq // 2
    loads = [
        pltpu.make_async_copy(source, place, local.at[k])
        for k, (source, place) in enumerate(
            (
                (part.at[:, z], part_own),
                (ff.at[0], ff_own),
                (weights.at[here], weights_own),
                (tokens_hbm.at[:, block_of(tensor)], tokens),
                (grad_mid_hbm, grad_mid),
            )
        )
    ]
    for copy in loads:
        copy.start()
    greet(
        [{"tensor": peer} for peer in peers] + [{"dp": d, "seq": s} for d, s in owners]
    )

    out = []
    for i in range(count):
        for k, dz in enumerate((2, 1, 3)):
            other = (z + dz) % 4
            copy = remote(
                part.at[i, other], landed.at[i, k], sends, recvs, 3 * i + k,
                {"tensor": 2 * other + y},
            )
            copy.start()
            out.append(copy)
    far = [
        remote(
            weights.at[d * 4 + px], shares.at[i], far_sends, far_recvs, i,
            {"dp": d, "seq": 2 * px + c},
        )
        for i, (d, px, c) in enumerate(chips)
    ]
    for copy in far:
        copy.start()
    swap = remote(ff.at[1], ff_in, ff_sends, ff_recvs, 0, {"dp": 1 - dp})
    swap.start()
    for copy in loads:
        copy.wait()
    grads[...] = jnp.zeros_like(grads)

    def collect(i):
        for copy in out[3 * i : 3 * i + 3]:
            copy.wait()

        def step(k, carry):
            row = pl.multiple_of(k * 16, 16)
            for own in (False, True):
                side = y if own else 1 - y
                at = pl.ds(row, 16)
                result = part_own[i, side, at, :].astype(f32)
                for j in range(3):
                    result = result + landed[i, j, side, at, :].astype(f32)
                if own:
                    ours[i, pl.ds(row, 16), :] = result
                else:
                    partner[i, pl.ds(row, 16), :] = result.astype(bf16)
            return carry

        lax.fori_loop(0, 2, step, 0)
        copy = remote(
            partner.at[i], landed_last.at[i], last_sends, last_recvs, i, {"tensor": 2 * z + 1 - y}
        )
        copy.start()
        return copy

    def conclude(i, copy):
        copy.wait()

        def step(k, carry):
            row = pl.ds(pl.multiple_of(k * 16, 16), 16)
            grad = ours[i, row, :] + landed_last[i, row, :].astype(f32)
            token_rows = tokens[i, row, :].astype(f32)
            inverse = inverse_rms(token_rows)
            normed = token_rows * inverse
            product = grad * normed
            grads[...] += product[:8] + product[8:]
            inner = jnp.mean(product * gain[0:1, :], axis=-1, keepdims=True)
            at = pl.ds(pl.multiple_of(i * 32 + k * 16, 16), 16)
            result = grad_mid[at, :] + inverse * (grad * gain[0:1, :] - normed * inner)
            input_grad[i, row, :] = result.astype(bf16)
            return carry

        lax.fori_loop(0, 2, step, 0)

    first = collect(0)
    second = collect(1)
    conclude(0, first)
    third = collect(2)
    conclude(1, second)
    conclude(2, third)
    gains[...] = jnp.zeros_like(gains)
    gains[0:1, :] = jnp.sum(grads[...], axis=0, keepdims=True)
    gains[1:2, :] = jnp.sum(gain_two[...], axis=0, keepdims=True)
    spread_gains = []
    for k, (d, s) in enumerate(owners):
        at = pl.ds(pl.multiple_of((d * 8 + s) * 128, 128), 128)
        copy = remote(gains.at[:, at], gains_in.at[k], gain_sends, gain_recvs, k, {"dp": d, "seq": s})
        copy.start()
        spread_gains.append(copy)
    own = gains[:, pl.ds(pl.multiple_of((dp * 8 + seq) * 128, 128), 128)]
    swap.wait()
    for tile in range(8):
        at = slice(128 * tile, 128 * tile + 128)
        share_gate_up[0, :, at] = ff_own[:, at].astype(f32) + ff_in[:, at].astype(f32)
        up_at = slice(units + 128 * tile, units + 128 * tile + 128)
        share_gate_up[1, :, at] = ff_own[:, up_at].astype(f32) + ff_in[:, up_at].astype(f32)
    for k, copy in enumerate(spread_gains):
        copy.wait()
        own = own + gains_in[k]
    gains_near[7] = own
    last = [
        remote(gains_near.at[7], gains_near.at[i], gain_last_sends, gain_last_recvs, i, {"tensor": peer})
        for i, peer in enumerate(peers)
    ]
    for copy in last:
        copy.start()
    for tile in range(8):
        at = slice(128 * tile, 128 * tile + 128)
        down_at = slice(2 * units + 128 * tile, 2 * units + 128 * tile + 128)
        both = ff_own[:, down_at].astype(f32) + ff_in[:, down_at].astype(f32)
        share_down[at, :] = both.T
    for copy in far:
        copy.wait()
    sums = weights_own[...].astype(f32)
    for i in range(7):
        sums = sums + shares[i].astype(f32)
    share_query[...] = sums[:, :256]
    share_pair[...] = sums[:, 512:]
    share_output[...] = sums[:, 256:512].T
    for copy in last:
        copy.wait()
    shifts = ((2, 1), (1, 1), (3, 1), (2, 0), (1, 0), (3, 0), (0, 1))
    sums = jnp.zeros_like(own)
    for t in range(8):
        slot = jnp.int32(7)
        for i, (dz, dy) in enumerate(shifts):
            source = ((z + 4 - dz) % 4) * 2 + (y + dy) % 2
            slot = jnp.where(source == t, i, slot)
        sums = sums + gains_near[slot]
    gain_sum[...] = sums[0:2, :]


def ending(part, weights, ff, tokens, grad_mid, gain, gain_two):
    count, width = part.shape[0], part.shape[4]
    units = ff.shape[2] // 3
    dma = pltpu.SemaphoreType.DMA
    vmem = pltpu.VMEM
    return pl.pallas_call(
        ending_kernel,
        out_shape=(
            jax.ShapeDtypeStruct((count, 32, width), bf16),
            jax.ShapeDtypeStruct((128, 256), f32),
            jax.ShapeDtypeStruct((128, 128), f32),
            jax.ShapeDtypeStruct((256, 128), f32),
            jax.ShapeDtypeStruct((2, 128), f32),
            jax.ShapeDtypeStruct((2, 128, units), f32),
            jax.ShapeDtypeStruct((units, 128), f32),
        ),
        in_specs=[ANY] * 5 + [VMEM] * 2,
        out_specs=(VMEM,) * 7,
        scratch_shapes=[
            vmem((count, 2, 32, width), bf16),
            vmem((128, 640), bf16),
            vmem((128, 3 * units), bf16),
            vmem((count, 32, width), bf16),
            vmem((count * 32, width), f32),
            vmem((count, 3, 2, 32, width), bf16),
            vmem((count, 32, width), f32),
            vmem((count, 32, width), bf16),
            vmem((count, 32, width), bf16),
            vmem((7, 128, 640), bf16),
            vmem((128, 3 * units), bf16),
            vmem((8, width), f32),
            vmem((8, width), f32),
            vmem((15, 8, 128), f32),
            vmem((8, 8, 128), f32),
            dma((9,)), dma((9,)), dma((3,)), dma((3,)), dma((7,)), dma((7,)), dma((1,)), dma((1,)),
            dma((15,)), dma((15,)), dma((7,)), dma((7,)), dma((5,)),
        ],
        compiler_params=params(2, 55),
        cost_estimate=pl.CostEstimate(flops=MIB, bytes_accessed=150 * MIB, transcendentals=0),
        name="ending",
    )(part, weights, ff, tokens, grad_mid, gain, gain_two)


def shards(
    tokens,
    cotangent,
    query_weight,
    query_first,
    query_second,
    key_value_weight,
    key_value_first_moment,
    key_value_second_moment,
    output_weight,
    output_first,
    output_second,
    gate_up_weight,
    gate_up_first,
    gate_up_second,
    down_weight,
    down_first,
    down_second,
    norm_gains,
    gains_first,
    gains_second,
):
    count, local_len, width = tokens.shape
    packed = jnp.concatenate(
        [
            query_weight,
            key_value_weight.reshape(128, 2 * HEAD_SIZE),
            output_weight.T,
        ],
        axis=1,
    ).astype(bf16)
    ff_low = jnp.concatenate(
        [gate_up_weight[0], gate_up_weight[1], down_weight.T], axis=1
    ).astype(bf16)
    gains_low = jnp.pad(norm_gains.astype(bf16).astype(f32), ((0, 6), (0, 0)))
    positions = lax.axis_index("seq") * local_len + jnp.arange(local_len, dtype=jnp.int32)
    cos_table, sin_table = rotary(positions)
    cos_wide = jnp.tile(cos_table, (1, 4))
    sin_wide = jnp.tile(jnp.concatenate([sin_table, -sin_table], axis=1), (1, 2))
    query, pairs, kept, mixed, packed_all, h_first, mid, h_second, ff_all, gains_used = forward(
        tokens, packed, gains_low, ff_low, cos_wide, sin_wide
    )
    branch_own, grad_mid, gain_two, mlp_term, grads = feed_forward(
        h_second,
        cotangent.reshape(count, 8, 32, width),
        ff_all,
        mid,
        gains_used,
    )
    shares_ff = lax.psum_scatter(grads, "seq", scatter_dimension=0, tiled=False)
    part, grads_projection, block_out = backward(
        branch_own,
        query,
        pairs,
        kept,
        mixed,
        packed_all,
        h_first,
        mlp_term,
        mid,
        cos_wide,
        sin_wide,
    )
    (
        input_grad,
        share_query,
        share_pair,
        share_output,
        share_gains,
        share_gate_up,
        share_down,
    ) = ending(
        part,
        grads_projection,
        shares_ff,
        tokens,
        grad_mid,
        gains_used,
        gain_two,
    )

    query_new, query_first_new, query_second_new = adam(
        query_weight, share_query, query_first, query_second, rate_wide, weight_decay
    )
    pair_new, pair_first_new, pair_second_new = adam(
        key_value_weight,
        share_pair[:, None, :],
        key_value_first_moment,
        key_value_second_moment,
        rate_wide,
        weight_decay,
    )
    output_new, output_first_new, output_second_new = adam(
        output_weight,
        share_output,
        output_first,
        output_second,
        rate_output,
        weight_decay,
    )
    gate_up_new, gate_up_first_new, gate_up_second_new = adam(
        gate_up_weight,
        share_gate_up,
        gate_up_first,
        gate_up_second,
        rate_wide,
        weight_decay,
    )
    down_new, down_first_new, down_second_new = adam(
        down_weight, share_down, down_first, down_second, rate_down, weight_decay
    )
    gains_new, gains_first_new, gains_second_new = adam(
        norm_gains, share_gains, gains_first, gains_second, rate_gains, 0.0
    )
    return (
        block_out,
        input_grad,
        query_new,
        query_first_new,
        query_second_new,
        pair_new,
        pair_first_new,
        pair_second_new,
        output_new,
        output_first_new,
        output_second_new,
        gate_up_new,
        gate_up_first_new,
        gate_up_second_new,
        down_new,
        down_first_new,
        down_second_new,
        gains_new,
        gains_first_new,
        gains_second_new,
    )


def solution(mesh):
    return jax.shard_map(
        shards,
        mesh=mesh,
        in_specs=(
            P("dp", "seq", None),
            P("dp", "seq", None),
            P(("dp", "seq"), "tensor"),
            P(("dp", "seq"), "tensor"),
            P(("dp", "seq"), "tensor"),
            P(("dp", "seq"), "tensor", None),
            P(("dp", "seq"), "tensor", None),
            P(("dp", "seq"), "tensor", None),
            P("tensor", ("dp", "seq")),
            P("tensor", ("dp", "seq")),
            P("tensor", ("dp", "seq")),
            P(None, ("dp", "seq"), "tensor"),
            P(None, ("dp", "seq"), "tensor"),
            P(None, ("dp", "seq"), "tensor"),
            P("tensor", ("dp", "seq")),
            P("tensor", ("dp", "seq")),
            P("tensor", ("dp", "seq")),
            P(None, ("dp", "seq")),
            P(None, ("dp", "seq")),
            P(None, ("dp", "seq")),
        ),
        out_specs=(
            P("dp", ("seq", "tensor"), None),
            P("dp", ("seq", "tensor"), None),
            P(("dp", "seq"), "tensor"),
            P(("dp", "seq"), "tensor"),
            P(("dp", "seq"), "tensor"),
            P(("dp", "seq"), "tensor", None),
            P(("dp", "seq"), "tensor", None),
            P(("dp", "seq"), "tensor", None),
            P("tensor", ("dp", "seq")),
            P("tensor", ("dp", "seq")),
            P("tensor", ("dp", "seq")),
            P(None, ("dp", "seq"), "tensor"),
            P(None, ("dp", "seq"), "tensor"),
            P(None, ("dp", "seq"), "tensor"),
            P("tensor", ("dp", "seq")),
            P("tensor", ("dp", "seq")),
            P("tensor", ("dp", "seq")),
            P(None, ("dp", "seq")),
            P(None, ("dp", "seq")),
            P(None, ("dp", "seq")),
        ),
        check_vma=False,
    )
```
